128 devices in a mesh: tm: 32 (over z, y, core), head: 4 (over x).
Axes of the slice: x: 4, y: 4, z: 4, core: 2. Of those that a mesh axis runs over, the one named last changes fastest.
Arguments:
- queries: bfloat16 [16384, 1280], P('tm', 'head'), may hold values from -6 to 6
- key_rows: bfloat16 [16384, 1280], P('tm', 'head'), may hold values from -6 to 6
- value_rows: bfloat16 [16384, 1280], P('tm', 'head'), may hold values from -6 to 6
- cotangent: bfloat16 [16384, 1280], P('tm', 'head'), may hold values from -6 to 6
- out_weight: bfloat16 [1280, 1280], P('head'), may hold values from -0.15625 to 0.15625
- segment_units: int32 [64], replicated, may hold values from 1 to 32, as said below
- left_segments: int32 [64], replicated, may hold values from 0 to 4, as said below
Outputs:
- query_grad: bfloat16 [16384, 1280], P('tm', 'head')
- key_grad: bfloat16 [16384, 1280], P('tm', 'head')
- value_grad: bfloat16 [16384, 1280], P('tm', 'head')
- out_weight_grad: float32 [1280, 1280], P('head', 'tm')
The draws below stay inside these ranges and needn't reach their ends.
Inputs may be any that keep to these rules, and one draw needn't show every extreme that they name: `segment_units`: the segments cover all 16384 frames in order; some segment has exactly 32 units. `left_segments`: some segment has exactly 4.
All inputs are finite; a program needn't handle non-finite values.
Results may differ from the reference program's by a relative error of at most 0.0085.
Values may be sent and summed in bfloat16 or wider, within the bound.
A program may use at most 64 MiB of HBM per device.

```python
import jax
import jax.numpy as jnp
from jax import lax

D = 1280
H = 20
HS = 64
FR_DEV = 512
UNIT = 16
MOSTU = 32
LEFT_MAX = 4
SEG_DEV = 2
FRAMES = 16384
NSEG = 64
N_TM = 32


def lead_units():
    return min(MOSTU // 2, ((LEFT_MAX + 1) * MOSTU * UNIT - UNIT - 1) % FR_DEV // UNIT + 1)


def run_block(key):
    unit_count = FR_DEV // UNIT
    reach_depth = min(N_TM - 1, ((LEFT_MAX + 1) * MOSTU * UNIT - UNIT - 1) // FR_DEV + 1)
    highest = min(N_TM - reach_depth, N_TM + (lead_units() - (LEFT_MAX + 1) * (MOSTU - 1)) // (unit_count - SEG_DEV))
    return jax.random.randint(jax.random.fold_in(key, 91), (), 1, highest + 1, dtype=jnp.int32)


def draw_queries(key, part):
    key = jax.random.fold_in(key, 11)
    drawn = jax.random.truncated_normal(key, -4.0, 4.0, (FRAMES, H * HS))
    return drawn.astype(jnp.bfloat16)


def draw_key_rows(key, part):
    key = jax.random.fold_in(key, 13)
    drawn = jax.random.truncated_normal(key, -4.0, 4.0, (FRAMES, H * HS))
    return drawn.astype(jnp.bfloat16)


def draw_segment_units(key, part):
    start_block = run_block(key)
    key = jax.random.fold_in(key, 17)
    unit_count = FR_DEV // UNIT
    spare = MOSTU - 1
    run_parts = LEFT_MAX + 1
    before_parts = start_block * SEG_DEV
    before_units = start_block * unit_count - lead_units()
    after_parts = NSEG - before_parts - run_parts
    after_units = N_TM * unit_count - before_units - run_parts * MOSTU
    segment_index = jnp.arange(NSEG, dtype=jnp.int32)
    region = (segment_index >= before_parts).astype(jnp.int32) + (segment_index >= before_parts + run_parts).astype(jnp.int32)
    heat = jax.random.randint(jax.random.fold_in(key, 1), (NSEG, 1), 1, 9, dtype=jnp.int32)
    scores = jax.random.randint(jax.random.fold_in(key, 2), (NSEG, spare), 0, 4096, dtype=jnp.int32) * heat
    slot_count = NSEG * spare
    slot_region = jnp.broadcast_to(region[:, None], (NSEG, spare))
    slot_index = jnp.arange(slot_count, dtype=jnp.int32).reshape(NSEG, spare)
    order_key = ((slot_region * 32768 + (32767 - scores)) * slot_count + slot_index).reshape(-1)
    order = jnp.argsort(order_key).astype(jnp.int32)
    ranks = jnp.argsort(order).astype(jnp.int32).reshape(NSEG, spare)
    region_first = jnp.where(slot_region == 0, 0, jnp.where(slot_region == 1, before_parts * spare, (before_parts + run_parts) * spare))
    extra_wanted = jnp.where(slot_region == 0, before_units - before_parts, jnp.where(slot_region == 1, run_parts * spare, after_units - after_parts))
    chosen = ranks - region_first < extra_wanted
    return (1 + jnp.sum(chosen.astype(jnp.int32), axis=1)).astype(jnp.int32)


def draw_left_segments(key, part):
    start_block = run_block(key)
    key = jax.random.fold_in(key, 5)
    values_drawn = jax.random.randint(key, (NSEG,), 0, LEFT_MAX + 1, dtype=jnp.int32)
    last_run = start_block * SEG_DEV + LEFT_MAX
    return jnp.where(jnp.arange(NSEG, dtype=jnp.int32) == last_run, LEFT_MAX, values_drawn).astype(jnp.int32)


def strengthened(array, stream_key, source, target, shards_of, factor):
    owner, partner = [(jnp.arange(array.shape[dim]) // (array.shape[dim] // shards_of)).reshape([-1 if axis == dim else 1 for axis in range(array.ndim)]) for dim in (source, target)]
    chosen = jax.random.permutation(stream_key, shards_of)[partner]
    strong = (owner == chosen) | (owner == (partner + shards_of // 2) % shards_of)
    return jnp.where(strong, factor * array, array)


def level_of(own_key, dims, split, smallest, high):
    def one(position, parts):
        heights = jax.random.uniform(jax.random.fold_in(jax.random.fold_in(own_key, 6), position), (parts,), jnp.float32, smallest / len(split), high / len(split))
        return jnp.repeat(jnp.exp(heights), dims[position] // parts).reshape((-1,) + (1,) * (len(dims) - position - 1))

    factor_of = one(*split[0])
    for cut in split[1:]:
        factor_of = factor_of * one(*cut)
    return factor_of


def normal_values(rng, shape, width, most, cuts=(), kind=jnp.bfloat16):
    values = width * jax.random.normal(rng, shape, jnp.float32)
    if cuts:
        values = values * level_of(rng, shape, cuts, -0.22, 0.18)
    return jnp.clip(values, -most, most).astype(kind)


def noise_with(stream_key, shape, spread, limit, shards, heavy, kind=jnp.bfloat16):
    values = spread * jax.random.normal(stream_key, shape, jnp.float32)
    if shards:
        values = values * level_of(stream_key, shape, shards, -0.22, 0.18)
    return jnp.clip(strengthened(values, jax.random.fold_in(stream_key, 3), *heavy), -limit, limit).astype(kind)


def setup_inputs(seed: int = 0) -> dict:
    splits = jax.random.split(jax.random.key(seed), 8)
    return {
        "queries": draw_queries(jax.random.fold_in(splits[7], 71), 0),
        "key_rows": draw_key_rows(jax.random.fold_in(splits[7], 71), 0),
        "value_rows": normal_values(splits[2], (FRAMES, H * HS), 1.0, 6.0, ((0, 32), (1, 4))),
        "cotangent": noise_with(splits[3], (FRAMES, D), 1.0, 6.0, ((0, 32), (1, 4)), (0, 1, 32, 2.75)),
        "out_weight": normal_values(splits[4], (H * HS, D), (H * HS) ** -0.5, 0.15625, ((0, 4),)),
        "segment_units": draw_segment_units(jax.random.fold_in(splits[7], 71), 0),
        "left_segments": draw_left_segments(jax.random.fold_in(splits[7], 71), 0),
    }


masked_score = -1.0e30


def segment_bounds(frames, segment_units, left_segments):
    segment_ends = jnp.cumsum(segment_units).astype(jnp.int32) * UNIT
    segment_starts = segment_ends - segment_units * UNIT
    number = jnp.arange(segment_units.shape[0], dtype=jnp.int32)
    owner_segment = jnp.sum((segment_ends[None, :] <= frames[:, None]).astype(jnp.int32), axis=1, dtype=jnp.int32)
    match_own = number[None, :] == owner_segment[:, None]
    reach_back = jnp.sum(jnp.where(match_own, left_segments[None, :], 0), axis=1, dtype=jnp.int32)
    upper_end = jnp.sum(jnp.where(match_own, segment_ends[None, :], 0), axis=1, dtype=jnp.int32)
    lowest = jnp.maximum(owner_segment - reach_back, 0)
    lower_end = jnp.sum(jnp.where(number[None, :] == lowest[:, None], segment_starts[None, :], 0), axis=1, dtype=jnp.int32)
    return lower_end.astype(jnp.int32), upper_end.astype(jnp.int32)


def touches(lower_end, upper_end, key_first, key_count):
    return jnp.any(jnp.maximum(lower_end, key_first) < jnp.minimum(upper_end, key_first + key_count))


def visible_mask(lower_end, upper_end, key_first, key_count):
    key_frames = key_first + jnp.arange(key_count, dtype=jnp.int32)
    return (key_frames[None, :] >= lower_end[:, None]) & (key_frames[None, :] < upper_end[:, None])


def tile_product(left_part, right_part):
    return jnp.einsum("qhd,khd->hqk", left_part.astype(jnp.float32), right_part.astype(jnp.float32))


def tile_backward(query_part, grad_part, keys_here, values_here, visible, log_total, delta_rows):
    scores = tile_product(query_part, keys_here) * (HS ** -0.5)
    probs_full = jnp.where(visible, jnp.exp(scores - log_total[:, :, None]), 0.0)
    grad_probs = tile_product(grad_part, values_here)
    probs_low = lax.optimization_barrier(probs_full.astype(jnp.bfloat16))
    dscore = lax.optimization_barrier((probs_full * (grad_probs - delta_rows[:, :, None])).astype(jnp.bfloat16))
    return probs_low.astype(jnp.float32), dscore.astype(jnp.float32)


def reference(queries, key_rows, value_rows, cotangent, out_weight, segment_units, left_segments):
    reach_depth = min(N_TM - 1, ((LEFT_MAX + 1) * MOSTU * UNIT - UNIT - 1) // FR_DEV + 1)
    grad_out = jnp.dot(cotangent, out_weight.T, preferred_element_type=jnp.float32).astype(jnp.bfloat16)
    query_heads = queries.reshape(N_TM, FR_DEV, H, HS)
    key_heads = key_rows.reshape(N_TM, FR_DEV, H, HS)
    value_heads = value_rows.reshape(N_TM, FR_DEV, H, HS)
    grad_heads = grad_out.reshape(N_TM, FR_DEV, H, HS)
    lower_all, upper_all = segment_bounds(jnp.arange(FRAMES, dtype=jnp.int32), segment_units, left_segments)
    lower_all = lower_all.reshape(N_TM, FR_DEV)
    upper_all = upper_all.reshape(N_TM, FR_DEV)
    offsets = jnp.arange(reach_depth + 1, dtype=jnp.int32)

    def query_block(block_index):
        query_part = query_heads[block_index]
        grad_part = grad_heads[block_index]
        lower_here = lower_all[block_index]
        upper_here = upper_all[block_index]

        def visit_stats(loop_state, offset):
            source = block_index - offset
            key_first = source * FR_DEV
            clamped = jnp.maximum(source, 0)
            keys_here = key_heads[clamped]
            values_here = value_heads[clamped]

            def update(current):
                maxima, totals, weighted = current
                visible = visible_mask(lower_here, upper_here, key_first, FR_DEV)[None]
                scores = jnp.where(visible, tile_product(query_part, keys_here) * (HS ** -0.5), masked_score)
                grad_probs = tile_product(grad_part, values_here)
                new_max = jnp.maximum(maxima, jnp.max(scores, axis=2))
                weights = jnp.where(visible, jnp.exp(scores - new_max[:, :, None]), 0.0)
                factor = jnp.exp(maxima - new_max)
                return (new_max, totals * factor + jnp.sum(weights, axis=2), weighted * factor + jnp.sum(weights * grad_probs, axis=2))

            flag = touches(lower_here, upper_here, key_first, FR_DEV)
            return lax.cond(flag, update, lambda current: current, loop_state), None

        start_state = (jnp.full((H, FR_DEV), masked_score, jnp.float32), jnp.zeros((H, FR_DEV), jnp.float32), jnp.zeros((H, FR_DEV), jnp.float32))
        (maxima, totals, weighted), _ = lax.scan(visit_stats, start_state, offsets)
        log_total = maxima + jnp.log(totals)
        delta_rows = weighted / totals

        def visit_grads(loop_state, offset):
            source = block_index - offset
            key_first = source * FR_DEV
            clamped = jnp.maximum(source, 0)
            keys_here = key_heads[clamped]
            values_here = value_heads[clamped]

            def update(current):
                visible = visible_mask(lower_here, upper_here, key_first, FR_DEV)[None]
                probs_low, dscore = tile_backward(query_part, grad_part, keys_here, values_here, visible, log_total, delta_rows)
                return (current[0] + jnp.einsum("hqk,khd->qhd", probs_low, values_here.astype(jnp.float32)), current[1] + jnp.einsum("hqk,khd->qhd", dscore, keys_here.astype(jnp.float32)))

            flag = touches(lower_here, upper_here, key_first, FR_DEV)
            return lax.cond(flag, update, lambda current: current, loop_state), None

        zero_rows = jnp.zeros((FR_DEV, H, HS), jnp.float32)
        (out_block, query_sum), _ = lax.scan(visit_grads, (zero_rows, zero_rows), offsets)
        return log_total, delta_rows, out_block, query_sum

    log_all, delta_all, out_all, query_all = lax.map(query_block, jnp.arange(N_TM, dtype=jnp.int32))

    def key_block(block_index):
        keys_here = key_heads[block_index]
        values_here = value_heads[block_index]
        key_first = block_index * FR_DEV

        def visit_keys(loop_state, offset):
            source = block_index + offset
            in_range = source < N_TM
            clamped = jnp.minimum(source, N_TM - 1)
            query_part = query_heads[clamped]
            grad_part = grad_heads[clamped]
            lower_here = lower_all[clamped]
            upper_here = upper_all[clamped]

            def update(current):
                visible = visible_mask(lower_here, upper_here, key_first, FR_DEV)[None]
                probs_low, dscore = tile_backward(query_part, grad_part, keys_here, values_here, visible, log_all[clamped], delta_all[clamped])
                return (current[0] + jnp.einsum("hqk,qhd->khd", dscore, query_part.astype(jnp.float32)), current[1] + jnp.einsum("hqk,qhd->khd", probs_low, grad_part.astype(jnp.float32)))

            flag = in_range & touches(lower_here, upper_here, key_first, FR_DEV)
            return lax.cond(flag, update, lambda current: current, loop_state), None

        zero_rows = jnp.zeros((FR_DEV, H, HS), jnp.float32)
        sums, _ = lax.scan(visit_keys, (zero_rows, zero_rows), offsets)
        return sums

    key_all, value_all = lax.map(key_block, jnp.arange(N_TM, dtype=jnp.int32))
    scale_factor = HS ** -0.5
    attn_out = out_all.reshape(FRAMES, H * HS).astype(jnp.bfloat16)
    out_weight_grad = jnp.dot(attn_out.T, cotangent, preferred_element_type=jnp.float32)
    query_grad = (query_all * scale_factor).reshape(FRAMES, H * HS).astype(jnp.bfloat16)
    key_grad = (key_all * scale_factor).reshape(FRAMES, H * HS).astype(jnp.bfloat16)
    value_grad = value_all.reshape(FRAMES, H * HS).astype(jnp.bfloat16)
    return (query_grad, key_grad, value_grad, out_weight_grad)
```

```python
import functools

import jax
import jax.numpy as jnp
from jax import lax
from jax.experimental import pallas as pl
from jax.experimental.pallas import tpu as pltpu
from jax.sharding import PartitionSpec as P

HS = 64
UNIT = 16
MOSTU = 32
LEFT_MAX = 4
BLK = 512
HEADS = 5
WIDTH = HEADS * HS
BACK = 5
CK = 256
PARTS = (BACK + 1) * BLK // CK
HIDDEN = -2e30
LOWEST = -1e30
F32 = jnp.float32
BF16 = jnp.bfloat16


def greet(signal_list):
    barrier = pltpu.get_barrier_semaphore()
    for target in signal_list:
        pl.semaphore_signal(
            barrier, inc=1, device_id=target, device_id_type=pl.DeviceIdType.MESH
        )


def send(src, dst, send_sem, recv_sem, target):
    return pltpu.make_async_remote_copy(
        src_ref=src,
        dst_ref=dst,
        send_sem=send_sem,
        recv_sem=recv_sem,
        device_id=target,
        device_id_type=pl.DeviceIdType.MESH,
    )


def gather_kernel(tm_count, head_count, kv, cot, kv_out, cot_out, own_sem, ssem, rsem, xs, xr):
    t = lax.axis_index("tm")
    x = lax.axis_index("head")
    core = t % 2
    mate = t + 1 - 2 * core

    def later(by):
        return {"tm": (t + by) % tm_count}

    def earlier(by):
        return {"tm": (t + tm_count - by) % tm_count}

    def side(by):
        return {"head": (x + by) % head_count}

    sides = range(1, head_count)
    greet([{"tm": mate}, earlier(2), earlier(4)] + [side(head_count - i) for i in sides])
    barrier = pltpu.get_barrier_semaphore()

    @pl.when(core == 0)
    def _():
        pl.semaphore_signal(
            barrier, inc=1, device_id=earlier(5), device_id_type=pl.DeviceIdType.MESH
        )
        pl.semaphore_wait(barrier, 3 + len(sides))

    @pl.when(core == 1)
    def _():
        pl.semaphore_wait(barrier, 4 + len(sides))

    own = pltpu.make_async_copy(kv, kv_out.at[0], own_sem.at[0])
    own.start()
    own_cot = pltpu.make_async_copy(cot, cot_out.at[x], own_sem.at[1])
    own_cot.start()

    def slot(src, k, target, sent):
        return send(src, kv_out.at[k], ssem.at[sent], rsem.at[k], target)

    across = [
        send(cot, cot_out.at[x], xs.at[i - 1], xr.at[i - 1], side(i)) for i in sides
    ]
    near = slot(kv, 2, later(2), 0)
    far = slot(kv, 4, later(4), 1)
    near.start()
    for copy in across:
        copy.start()
    far.start()

    @pl.when(core == 0)
    def _():
        first = slot(kv, 1, {"tm": mate}, 2)
        first.start()
        near.wait_recv()
        second = slot(kv_out.at[2], 3, {"tm": mate}, 3)
        second.start()
        far.wait_recv()
        third = slot(kv_out.at[4], 5, {"tm": mate}, 4)
        third.start()
        slot(kv, 1, {"tm": mate}, 2).wait_recv()
        slot(kv, 3, {"tm": mate}, 3).wait_recv()
        slot(kv, 5, {"tm": mate}, 4).wait_recv()
        first.wait_send()
        second.wait_send()
        third.wait_send()

    @pl.when(core == 1)
    def _():
        last = slot(kv, 5, later(5), 4)
        last.start()
        near.wait_recv()
        first = slot(kv_out.at[2], 1, {"tm": mate}, 2)
        first.start()
        far.wait_recv()
        second = slot(kv_out.at[4], 3, {"tm": mate}, 3)
        second.start()
        slot(kv, 1, {"tm": mate}, 2).wait_recv()
        slot(kv, 3, {"tm": mate}, 3).wait_recv()
        slot(kv, 5, {"tm": mate}, 4).wait_recv()
        first.wait_send()
        second.wait_send()
        last.wait_send()

    near.wait_send()
    far.wait_send()
    for copy in across:
        copy.wait()
    own.wait()
    own_cot.wait()


def attend_kernel(
    count_ref,
    spans,
    query_info,
    q_ref,
    kv_ref,
    cot_ref,
    w_ref,
    dq_ref,
    dkv_ref,
    wt_ref,
    kvt,
    probs,
    rhs,
    gt,
    rows,
    out_t,
    dq_t,
    m_all,
    m_run,
    l_run,
    delta,
    acc,
):
    used = count_ref[0]
    own_first = count_ref[1]
    grad = jnp.zeros((BLK, WIDTH), F32)
    for x in range(cot_ref.shape[0]):
        grad += lax.dot_general(
            cot_ref[x], w_ref[x], (((1,), (1,)), ((), ())), preferred_element_type=F32
        )
    queries = (q_ref[...].astype(F32) * HS**-0.5).astype(BF16)
    pair = jnp.concatenate([queries, grad.astype(BF16)], axis=1)
    pair_t = pair.T
    seg_row = lax.broadcasted_iota(jnp.int32, (128, BLK), 0)
    bias = jnp.where(
        (seg_row >= query_info[0:1, :]) & (seg_row <= query_info[1:2, :]), 0.0, HIDDEN
    ).astype(BF16)
    blank_t = jnp.zeros((HS, BLK), BF16)
    lane = lax.broadcasted_iota(jnp.int32, (BLK, 128), 1)
    for j in range(2 * HEADS):
        g, half = divmod(j, 2)
        mine = pair_t[HS * j : HS * (j + 1), :]
        both = [mine, blank_t] if half == 0 else [blank_t, mine]
        if j < HEADS:
            rhs[j] = jnp.concatenate(both + [bias], axis=0)
        else:
            gt[j - HEADS] = jnp.concatenate(both, axis=0)
        group = pair[:, 128 * g : 128 * (g + 1)]
        keep = (lane < HS) if half == 0 else (lane >= HS)
        rows[j] = jnp.where(keep, group, jnp.zeros_like(group))
    m_run[...] = jnp.full(m_run.shape, LOWEST, F32)
    l_run[...] = jnp.zeros(l_run.shape, F32)
    out_t[...] = jnp.zeros(out_t.shape, F32)
    dq_t[...] = jnp.zeros(dq_t.shape, F32)

    def place(i):
        return 2 * (i // 2) + 1 - i % 2

    def forward(i, carry):
        c = place(i)
        frames = own_first + BLK - (i + 1) * CK + lax.broadcasted_iota(jnp.int32, (CK, 128), 0)
        hot = ((frames >= spans[0:1, :]) & (frames < spans[1:2, :])).astype(F32).astype(BF16)
        kvt[c] = kv_ref[c].T
        for h in range(HEADS):
            g = h // 2
            left = jnp.concatenate([kv_ref[c, :, 128 * g : 128 * (g + 1)], hot], axis=1)
            s = jnp.dot(left, rhs[h], preferred_element_type=F32)
            m_old = m_run[h : h + 1, :]
            m_new = jnp.maximum(m_old, jnp.max(s, axis=0, keepdims=True))
            p = jnp.exp(s - m_new)
            factor = jnp.exp(m_old - m_new)
            l_run[h : h + 1, :] = l_run[h : h + 1, :] * factor + jnp.sum(p, axis=0, keepdims=True)
            m_run[h : h + 1, :] = m_new
            m_all[c, h : h + 1, :] = m_new
            low = p.astype(BF16)
            probs[c, h] = low
            here = slice(HS * h, HS * (h + 1))
            out_t[here, :] = out_t[here, :] * factor + jnp.dot(
                kvt[c, WIDTH + HS * h : WIDTH + HS * (h + 1), :], low, preferred_element_type=F32
            )
        return carry

    lax.fori_loop(0, used, forward, 0)

    for h in range(HEADS):
        here = slice(HS * h, HS * (h + 1))
        out = out_t[here, :] / l_run[h : h + 1, :]
        out_t[here, :] = out
        own_grad = gt[h, HS * ((h + 1) % 2) : HS * ((h + 1) % 2) + HS, :].astype(F32)
        delta[h : h + 1, :] = jnp.sum(out * own_grad, axis=0, keepdims=True)
        l_run[h : h + 1, :] = m_run[h : h + 1, :] + jnp.log(l_run[h : h + 1, :])

    attn_t = out_t[...].astype(BF16)
    for x in range(cot_ref.shape[0]):
        term = jnp.dot(attn_t, cot_ref[x], preferred_element_type=F32)
        wt_ref[x] = term.T.astype(BF16)

    def backward(i, carry):
        c = place(i)
        for h in range(HEADS):
            g = (h + HEADS) // 2
            grad_p = jnp.dot(
                kv_ref[c, :, 128 * g : 128 * (g + 1)], gt[h], preferred_element_type=F32
            )
            scale = jnp.exp(m_all[c, h : h + 1, :] - l_run[h : h + 1, :])
            p = probs[c, h].astype(F32) * scale
            ds = (p * (grad_p - delta[h : h + 1, :])).astype(BF16)
            here = slice(HS * h, HS * (h + 1))
            dq_t[here, :] += jnp.dot(kvt[c, here, :], ds, preferred_element_type=F32)
            for j, lhs in ((h, ds), (h + HEADS, p.astype(BF16))):
                cols = slice(128 * (j // 2), 128 * (j // 2 + 1))
                part = jnp.dot(lhs, rows[j], preferred_element_type=F32)
                if j in (0, 5, 6, 2, 8):
                    acc[:, cols] = part
                else:
                    acc[:, cols] += part
        dkv_ref[c] = acc[...].astype(BF16)
        return carry

    lax.fori_loop(0, used, backward, 0)

    def clear(i, carry):
        dkv_ref[place(i)] = jnp.zeros(dkv_ref.shape[1:], BF16)
        return carry

    lax.fori_loop(used, PARTS, clear, 0)
    dq_ref[...] = (dq_t[...] * HS**-0.5).T.astype(BF16)


def return_kernel(
    tm_count,
    dkv,
    wt,
    dk_ref,
    dv_ref,
    dw_ref,
    from_mate,
    sums,
    homes,
    edge,
    z_in,
    z_sum,
    y_in,
    ms,
    mr,
    hs,
    hr,
    es,
    er,
    zs,
    zr,
    ys,
    yr,
):
    t = lax.axis_index("tm")
    core = t % 2
    mate = {"tm": t + 1 - 2 * core}
    z = t // 8
    low = t % 8

    def later(by):
        return {"tm": (t + by) % tm_count}

    def earlier(by):
        return {"tm": (t + tm_count - by) % tm_count}

    def z_peer(i):
        return {"tm": (t + 8 * i) % tm_count}

    def y_peer(i):
        return {"tm": 8 * z + (low + i) % 8}

    barrier = pltpu.get_barrier_semaphore()
    greetings = [mate, later(2), later(4)]
    greetings += [z_peer(4 - i) for i in range(1, 4)] + [y_peer(8 - i) for i in range(1, 8)]
    greet(greetings)

    @pl.when(core == 1)
    def _():
        pl.semaphore_signal(
            barrier, inc=1, device_id=later(5), device_id_type=pl.DeviceIdType.MESH
        )
        pl.semaphore_wait(barrier, len(greetings))

    @pl.when(core == 0)
    def _():
        pl.semaphore_wait(barrier, len(greetings) + 1)

    z_copies = [
        send(wt.at[(z + i) % 4], z_in.at[i - 1], zs.at[i - 1], zr.at[i - 1], z_peer(i))
        for i in range(1, 4)
    ]

    to_far = send(dkv.at[3 + 2 * core], from_mate.at[0], ms.at[0], mr.at[0], mate)
    to_near = send(dkv.at[1 + 2 * core], from_mate.at[1], ms.at[1], mr.at[1], mate)
    to_far.start()
    to_near.start()
    on_edge = send(dkv.at[5], edge, es.at[0], er.at[0], earlier(5))
    in_chip = send(dkv.at[1], edge, es.at[0], er.at[0], mate)

    @pl.when(core == 0)
    def _():
        on_edge.start()

    @pl.when(core == 1)
    def _():
        in_chip.start()

    for copy in z_copies:
        copy.start()
    home_copies = []
    for step, copy, kept in ((0, to_far, 4), (1, to_near, 2)):
        copy.wait_recv()
        sums[step] = (dkv[kept].astype(F32) + from_mate[step].astype(F32)).astype(BF16)
        home = send(sums.at[step], homes.at[step], hs.at[step], hr.at[step], earlier(kept))
        home.start()
        home_copies.append(home)

    for copy in z_copies:
        copy.wait_recv()
    z_sum[...] = wt[z].astype(F32)
    for i in range(3):
        z_sum[...] += z_in[i].astype(F32)
    y_copies = [
        send(
            z_sum.at[pl.ds(pl.multiple_of(40 * ((low + i) % 8), 8), 40)],
            y_in.at[i - 1],
            ys.at[i - 1],
            yr.at[i - 1],
            y_peer(i),
        )
        for i in range(1, 8)
    ]
    for copy in y_copies:
        copy.start()
    total = z_sum[pl.ds(pl.multiple_of(40 * low, 8), 40), :]
    for i, copy in enumerate(y_copies):
        copy.wait_recv()
        total = total + y_in[i]
    dw_ref[...] = total

    total = dkv[0].astype(F32)
    for step, copy in enumerate(home_copies):
        copy.wait_recv()
        total = total + homes[step].astype(F32)
    in_chip.wait_recv()
    total = total + edge[...].astype(F32)
    dk_ref[...] = total[:, :WIDTH].astype(BF16)
    dv_ref[...] = total[:, WIDTH:].astype(BF16)

    for copy in z_copies + y_copies + home_copies + [to_far, to_near, in_chip]:
        copy.wait_send()


def shards(queries, key_rows, value_rows, cotangent, out_weight, segment_units, left_segments):
    tm_count = lax.axis_size("tm")
    head_count = lax.axis_size("head")
    t = lax.axis_index("tm")
    any_space = pl.BlockSpec(memory_space=pl.ANY)
    vmem = pl.BlockSpec(memory_space=pltpu.VMEM)
    smem = pl.BlockSpec(memory_space=pltpu.SMEM)

    ends = jnp.cumsum(segment_units) * UNIT
    starts = ends - segment_units * UNIT
    segments = segment_units.shape[0]
    number = jnp.arange(segments, dtype=jnp.int32)
    own_first = t * BLK
    frames = own_first + jnp.arange(BLK, dtype=jnp.int32)
    own_seg = jnp.sum((ends[:, None] <= frames[None, :]).astype(jnp.int32), axis=0)
    reach = jnp.sum(
        jnp.where(number[:, None] == own_seg[None, :], left_segments[:, None], 0), axis=0
    )
    lowest = jnp.maximum(own_seg - reach, 0)
    first_key = jnp.min(
        jnp.where(number[:, None] == lowest[None, :], starts[:, None], tm_count * BLK)
    )
    used = (own_first + BLK - first_key + CK - 1) // CK
    counts = jnp.stack([jnp.minimum(used, PARTS), own_first]).astype(jnp.int32)
    pad = 128 - segments
    spans = jnp.zeros((8, 128), jnp.int32).at[0, :segments].set(starts).at[1, :segments].set(ends)
    query_info = jnp.stack([lowest, own_seg] + [own_seg] * 6).astype(jnp.int32)

    kv = jnp.concatenate([key_rows, value_rows], axis=1)
    dma = pltpu.SemaphoreType.DMA
    kv_all, cot_all = pl.pallas_call(
        functools.partial(gather_kernel, tm_count, head_count),
        out_shape=(
            jax.ShapeDtypeStruct((BACK + 1, BLK, 2 * WIDTH), BF16),
            jax.ShapeDtypeStruct((head_count, BLK, WIDTH), BF16),
        ),
        in_specs=[any_space] * 2,
        out_specs=(any_space, any_space),
        scratch_shapes=[dma((2,)), dma((5,)), dma((6,)), dma((3,)), dma((3,))],
        compiler_params=pltpu.CompilerParams(collective_id=0, has_side_effects=True),
    )(kv, cotangent)

    w_parts = out_weight.reshape(WIDTH, head_count, WIDTH).transpose(1, 0, 2)
    query_grad, dkv, w_term = pl.pallas_call(
        attend_kernel,
        out_shape=(
            jax.ShapeDtypeStruct((BLK, WIDTH), BF16),
            jax.ShapeDtypeStruct((PARTS, CK, 2 * WIDTH), BF16),
            jax.ShapeDtypeStruct((head_count, WIDTH, WIDTH), BF16),
        ),
        in_specs=[smem] + [vmem] * 6,
        out_specs=(vmem, vmem, vmem),
        scratch_shapes=[
            pltpu.VMEM((PARTS, 2 * WIDTH, CK), BF16),
            pltpu.VMEM((PARTS, HEADS, CK, BLK), BF16),
            pltpu.VMEM((HEADS, 256, BLK), BF16),
            pltpu.VMEM((HEADS, 128, BLK), BF16),
            pltpu.VMEM((2 * HEADS, BLK, 128), BF16),
            pltpu.VMEM((WIDTH, BLK), F32),
            pltpu.VMEM((WIDTH, BLK), F32),
            pltpu.VMEM((PARTS, 8, BLK), F32),
            pltpu.VMEM((8, BLK), F32),
            pltpu.VMEM((8, BLK), F32),
            pltpu.VMEM((8, BLK), F32),
            pltpu.VMEM((CK, 2 * WIDTH), F32),
        ],
        compiler_params=pltpu.CompilerParams(vmem_limit_bytes=52 << 20),
    )(
        counts,
        spans,
        query_info,
        queries,
        kv_all.reshape(PARTS, CK, 2 * WIDTH),
        cot_all,
        w_parts,
    )

    key_grad, value_grad, dw_t = pl.pallas_call(
        functools.partial(return_kernel, tm_count),
        out_shape=(
            jax.ShapeDtypeStruct((BLK, WIDTH), BF16),
            jax.ShapeDtypeStruct((BLK, WIDTH), BF16),
            jax.ShapeDtypeStruct((40, WIDTH), F32),
        ),
        in_specs=[vmem] * 2,
        out_specs=(vmem, vmem, vmem),
        scratch_shapes=[
            pltpu.VMEM((2, BLK, 2 * WIDTH), BF16),
            pltpu.VMEM((2, BLK, 2 * WIDTH), BF16),
            pltpu.VMEM((2, BLK, 2 * WIDTH), BF16),
            pltpu.VMEM((BLK, 2 * WIDTH), BF16),
            pltpu.VMEM((3, WIDTH, WIDTH), BF16),
            pltpu.VMEM((WIDTH, WIDTH), F32),
            pltpu.VMEM((7, 40, WIDTH), F32),
        ]
        + [dma((2,))] * 4
        + [dma((1,))] * 2
        + [dma((3,))] * 2
        + [dma((7,))] * 2,
        compiler_params=pltpu.CompilerParams(
            collective_id=1, has_side_effects=True, vmem_limit_bytes=40 << 20
        ),
    )(dkv.reshape(BACK + 1, BLK, 2 * WIDTH), w_term)
    return (query_grad, key_grad, value_grad, dw_t.T)


def solution(mesh):
    placed = (
        P("tm", "head"),
        P("tm", "head"),
        P("tm", "head"),
        P("tm", "head"),
        P("head", None),
        P(),
        P(),
    )
    return jax.shard_map(
        shards,
        mesh=mesh,
        in_specs=placed,
        out_specs=(P("tm", "head"), P("tm", "head"), P("tm", "head"), P("head", "tm")),
        check_vma=False,
    )
```

```python
import functools

import jax
import jax.numpy as jnp
from jax import lax
from jax.experimental import pallas as pl
from jax.experimental.pallas import tpu as pltpu
from jax.sharding import PartitionSpec as P

HS = 64
UNIT = 16
BLK = 512
HEADS = 5
WIDTH = HEADS * HS
BACK = 5
HALF = BLK // 2
STRIP = 128
HIDDEN = -2e30
LOWEST = -1e30
F32 = jnp.float32
BF16 = jnp.bfloat16
MESH = pl.DeviceIdType.MESH


def kernel(
    tm_count,
    head_count,
    units_ref,
    left_ref,
    q_hbm,
    k_hbm,
    v_hbm,
    cot_hbm,
    w_hbm,
    dq_ref,
    dk_ref,
    dv_ref,
    dw_ref,
    slots,
    relay,
    kv_all,
    probs,
    cot_all,
    w_ref,
    q_ref,
    rhs,
    gt,
    rows,
    square,
    work,
    out_t,
    dq_t,
    m_all,
    m_run,
    l_run,
    delta,
    dkv,
    from_mate,
    sums,
    home_near,
    home_far,
    chain_in,
    relay_back,
    edge,
    wt,
    z_in,
    z_sum,
    y_in,
    local,
    sent,
    got_k,
    got_v,
    got_relay,
    side_sent,
    side_got,
    back_sent,
    back_got,
    z_sent,
    z_got,
    y_sent,
    y_got,
):
    t = lax.axis_index("tm")
    x = lax.axis_index("head")
    core = t % 2
    z = t // 8
    y = (t // 2) % 4
    low = t % 8
    sides = range(1, head_count)

    def at(place):
        return {"tm": (place + tm_count) % tm_count}

    def chip(z_place, y_place):
        return (z_place * 4 + y_place % 4) * 2 + core

    mate = at(t + 1 - 2 * core)
    before, after = chip(z, y + 3), chip(z, y + 1)
    src_four = (t + tm_count - 4) % tm_count
    src_relay = chip(src_four // 8, (src_four // 2) % 4 + 3)
    own_four = (t + 4) % tm_count
    own_relay = chip(own_four // 8, (own_four // 2) % 4 + 1)

    greeted = [mate, at(t - 2), at(after), at(src_relay)]
    greeted += [at(t + 2), at(before), at(own_relay)]
    greeted += [{"head": (x + head_count - i) % head_count} for i in sides]
    greeted += [at(t - 8 * i) for i in range(1, 4)]
    greeted += [at(8 * z + (low + 8 - i) % 8) for i in range(1, 8)]
    barrier = pltpu.get_barrier_semaphore()
    for target in greeted:
        pl.semaphore_signal(barrier, inc=1, device_id=target, device_id_type=MESH)
    edge_source = at(t + 5 * (2 * core - 1))
    pl.semaphore_signal(barrier, inc=1, device_id=edge_source, device_id_type=MESH)

    loads = [
        pltpu.make_async_copy(k_hbm, slots.at[0, 0:WIDTH], local.at[0]),
        pltpu.make_async_copy(v_hbm, slots.at[0, WIDTH : 2 * WIDTH], local.at[1]),
        pltpu.make_async_copy(q_hbm, q_ref, local.at[2]),
        pltpu.make_async_copy(
            cot_hbm, cot_all.at[pl.ds(pl.multiple_of(WIDTH * x, 64), WIDTH)], local.at[3]
        ),
        pltpu.make_async_copy(w_hbm, w_ref, local.at[4]),
    ]
    for load in loads:
        load.start()
    pl.semaphore_wait(barrier, len(greeted) + 1)

    def push(src, dst, send_sem, recv_sem, target):
        return pltpu.make_async_remote_copy(
            src_ref=src,
            dst_ref=dst,
            send_sem=send_sem,
            recv_sem=recv_sem,
            device_id=target,
            device_id_type=MESH,
        )

    def keys(src, slot, number, target):
        return push(src, slots.at[slot, 0:WIDTH], sent.at[number], got_k.at[slot], target)

    def values(src, slot, number, target):
        return push(
            src, slots.at[slot, WIDTH : 2 * WIDTH], sent.at[number], got_v.at[slot], target
        )

    def key_part(slot):
        return slots.at[slot, 0:WIDTH]

    def value_part(slot):
        return slots.at[slot, WIDTH : 2 * WIDTH]

    near_k = keys(k_hbm, 2, 0, at(t + 2))
    near_v = values(v_hbm, 2, 1, at(t + 2))
    relay_first = push(v_hbm, relay, sent.at[2], got_relay.at[0], at(before))
    near_k.start()
    relay_first.start()
    across = [
        push(
            cot_hbm,
            cot_all.at[pl.ds(pl.multiple_of(WIDTH * x, 64), WIDTH)],
            side_sent.at[i - 1],
            side_got.at[i - 1],
            {"head": (x + i) % head_count},
        )
        for i in sides
    ]
    for copy in across:
        copy.start()
    near_v.start()
    direct_slot = 1 + 4 * core
    direct_to = at(t + 1 + 4 * core)
    direct_k = keys(k_hbm, direct_slot, 3, direct_to)
    direct_v = values(v_hbm, direct_slot, 4, direct_to)
    direct_k.start()
    direct_v.start()
    chain_k = keys(key_part(2), 4, 5, at(t + 2))
    relay_second = values(relay, 4, 6, at(after + 4))
    pass_near = 3 - 2 * core
    pass_far = 5 - 2 * core
    pass_near_k = keys(key_part(2), pass_near, 7, mate)
    pass_near_v = values(value_part(2), pass_near, 8, mate)
    pass_far_k = keys(key_part(4), pass_far, 9, mate)
    pass_far_v = values(value_part(4), pass_far, 10, mate)

    segments = units_ref.shape[1]
    units = jnp.broadcast_to(units_ref[...].astype(F32), (8, segments)).astype(BF16)
    lefts = jnp.broadcast_to(left_ref[...].astype(F32), (8, segments)).astype(BF16)
    down = lax.broadcasted_iota(jnp.int32, (segments, 128), 0)
    over = lax.broadcasted_iota(jnp.int32, (segments, 128), 1)
    until = jnp.where(down <= over, 1.0, 0.0).astype(BF16)
    ahead = jnp.where(down < over, 1.0, 0.0).astype(BF16)
    same = jnp.where(down == over, 1.0, 0.0).astype(BF16)
    end_row = jnp.dot(units, until, preferred_element_type=F32)[0:1, :] * UNIT
    start_row = jnp.dot(units, ahead, preferred_element_type=F32)[0:1, :] * UNIT
    columns = (((0,), (1,)), ((), ()))
    end_col = lax.dot_general(until, units, columns, preferred_element_type=F32)[:, 0:1] * UNIT
    left_col = lax.dot_general(same, lefts, columns, preferred_element_type=F32)[:, 0:1]
    frame_row = (t * BLK + lax.broadcasted_iota(jnp.int32, (1, BLK), 1)).astype(F32)
    own_seg = jnp.sum(jnp.where(end_col <= frame_row, 1.0, 0.0), axis=0, keepdims=True)
    seg_down = lax.broadcasted_iota(jnp.int32, (128, BLK), 0).astype(F32)
    reach = jnp.sum(jnp.where(seg_down == own_seg, left_col, 0.0), axis=0, keepdims=True)
    lowest = jnp.maximum(own_seg - reach, 0.0)
    bias = jnp.where((seg_down >= lowest) & (seg_down <= own_seg), 0.0, HIDDEN).astype(BF16)

    blank = jnp.zeros((HS, BLK), BF16)
    lane = lax.broadcasted_iota(jnp.int32, (BLK, 128), 1)

    def spread(j, upright, transposed):
        g, half = divmod(j, 2)
        both = [transposed, blank] if half == 0 else [blank, transposed]
        if j < HEADS:
            rhs[j] = jnp.concatenate(both + [bias], axis=0)
        else:
            gt[j - HEADS] = jnp.concatenate(both, axis=0)
        zeros = jnp.zeros((BLK, HS), BF16)
        pair = [upright, zeros] if half == 0 else [zeros, upright]
        rows[g, BLK * half : BLK * (half + 1), :] = jnp.concatenate(pair, axis=1)

    loads[2].wait()
    queries_t = (q_ref[...].astype(F32) * HS**-0.5).astype(BF16)
    for j in range(HEADS):
        mine = queries_t[HS * j : HS * (j + 1), :]
        spread(j, mine.T, mine)
    m_run[...] = jnp.full(m_run.shape, LOWEST, F32)
    l_run[...] = jnp.zeros(l_run.shape, F32)
    out_t[...] = jnp.zeros(out_t.shape, F32)
    dq_t[...] = jnp.zeros(dq_t.shape, F32)
    loads[0].wait()
    loads[1].wait()

    def wait_slot(slot):
        keys(k_hbm, slot, 0, mate).wait_recv()
        values(v_hbm, slot, 1, mate).wait_recv()

    def near_event():
        relay_first.wait_recv()
        relay_second.start()
        near_k.wait_recv()
        chain_k.start()
        pass_near_k.start()
        near_v.wait_recv()
        pass_near_v.start()

    def forward(step, carry):
        @pl.when(step == 1)
        def _():
            loads[3].wait()
            loads[4].wait()
            for copy in across:
                copy.wait_recv()
            grad_t = jnp.dot(w_ref[...], cot_all[...], preferred_element_type=F32).astype(BF16)
            for j in range(HEADS):
                mine = grad_t[HS * j : HS * (j + 1), :]
                spread(j + HEADS, mine.T, mine)

        swapped = jnp.where(step == 0, 0, jnp.where(step < 3, 3 - step, 8 - step))
        slot = jnp.where(core == 0, swapped, step)

        @pl.when(step == 1 + core)
        def _():
            near_event()

        @pl.when((step == 2 - core) | (step == 3) | (step == 5))
        def _():
            wait_slot(slot)

        @pl.when(step == 4)
        def _():
            keys(k_hbm, 4, 0, mate).wait_recv()
            pass_far_k.start()
            values(v_hbm, 4, 1, mate).wait_recv()
            pass_far_v.start()

        kv_all[slot] = slots[slot].T
        first = ((t + tm_count - slot) % tm_count) * BLK
        frames = (first + lax.broadcasted_iota(jnp.int32, (BLK, 128), 0)).astype(F32)
        hot = jnp.where((frames >= start_row) & (frames < end_row), 1.0, 0.0).astype(BF16)
        tops = []
        for turn in range(HEADS + 1):
            if turn < HEADS:
                g = turn // 2
                lhs = jnp.concatenate([kv_all[slot, :, 128 * g : 128 * (g + 1)], hot], axis=1)
                scores = jnp.dot(lhs, rhs[turn], preferred_element_type=F32)
                square[turn % 2] = scores
                tops.append(jnp.max(scores.reshape(BLK // 8, 8, BLK), axis=0))
            if turn == 0:
                continue
            h = turn - 1
            m_old = m_run[h, 0:1, :]
            m_new = jnp.maximum(m_old, jnp.max(tops[h], axis=0, keepdims=True))
            factor = jnp.exp(m_old - m_new)
            total = l_run[h] * factor
            for r in range(0, BLK, STRIP):
                p = jnp.exp(square[h % 2, r : r + STRIP, :] - m_new)
                total = total + jnp.sum(p.reshape(STRIP // 8, 8, BLK), axis=0)
                probs[slot, h, r : r + STRIP, :] = p.astype(BF16)
            m_run[h, 0:1, :] = m_new
            l_run[h] = total
            m_all[slot, h, 0:1, :] = m_new
            here = slice(HS * h, HS * (h + 1))
            out_t[here, :] = out_t[here, :] * factor + jnp.dot(
                slots[slot, WIDTH + HS * h : WIDTH + HS * (h + 1), :],
                probs[slot, h],
                preferred_element_type=F32,
            )
        return carry

    lax.fori_loop(0, BACK + 1, forward, 0)

    for h in range(HEADS):
        here = slice(HS * h, HS * (h + 1))
        total = jnp.sum(l_run[h], axis=0, keepdims=True)
        out = out_t[here, :] / total
        out_t[here, :] = out
        side = HS * ((h + HEADS) % 2)
        own_grad = gt[h, side : side + HS, :].astype(F32)
        delta[h, 0:1, :] = jnp.sum(out * own_grad, axis=0, keepdims=True)
        l_run[h, 0:1, :] = m_run[h, 0:1, :] + jnp.log(total)

    z_copies = [
        push(
            wt.at[(z + i) % 4], z_in.at[i - 1], z_sent.at[i - 1], z_got.at[i - 1], at(t + 8 * i)
        )
        for i in range(1, 4)
    ]
    y_copies = [
        push(
            z_sum.at[pl.ds(pl.multiple_of(40 * ((low + i) % 8), 8), 40)],
            y_in.at[i - 1],
            y_sent.at[i - 1],
            y_got.at[i - 1],
            at(8 * z + (low + i) % 8),
        )
        for i in range(1, 8)
    ]

    far_slot, near_slot, edge_slot = 3 + 2 * core, 1 + 2 * core, 5 - 4 * core
    to_far = push(dkv.at[far_slot], from_mate.at[0], back_sent.at[0], back_got.at[0], mate)
    to_near = push(dkv.at[near_slot], from_mate.at[1], back_sent.at[1], back_got.at[1], mate)
    chain = push(sums.at[0, 0:HALF], chain_in, back_sent.at[2], back_got.at[2], at(t - 2))
    back_first = push(
        sums.at[0, HALF:BLK], relay_back, back_sent.at[3], back_got.at[3], at(after)
    )
    back_second = push(relay_back, home_far, back_sent.at[4], back_got.at[4], at(before - 4))
    homeward = push(sums.at[1], home_near, back_sent.at[5], back_got.at[5], at(t - 2))
    edge_to = at(t - 5 + 4 * core)
    edge_copy = push(dkv.at[edge_slot], edge, back_sent.at[6], back_got.at[6], edge_to)

    def backward(step, carry):
        crossed = jnp.where(
            step < 2, 3 + step, jnp.where(step < 4, step - 1, jnp.where(step == 4, 5, 0))
        )
        slot = jnp.where(core == 0, crossed, 5 - step)
        for turn in range(HEADS + 1):
            if turn < HEADS:
                g = (turn + HEADS) // 2
                grad_p = jnp.dot(
                    kv_all[slot, :, 128 * g : 128 * (g + 1)], gt[turn], preferred_element_type=F32
                )
                scale = jnp.exp(m_all[slot, turn, 0:1, :] - l_run[turn, 0:1, :])
                shift = delta[turn, 0:1, :]
                ds_at, p_at = BLK * (turn % 2), BLK * ((turn + HEADS) % 2)
                for r in range(0, BLK, STRIP):
                    p = probs[slot, turn, r : r + STRIP, :].astype(F32) * scale
                    ds = p * (grad_p[r : r + STRIP] - shift)
                    work[turn // 2, r : r + STRIP, ds_at : ds_at + BLK] = ds.astype(BF16)
                    work[(turn + HEADS) // 2, r : r + STRIP, p_at : p_at + BLK] = p.astype(BF16)
            if turn == 0:
                continue
            h = turn - 1
            here = slice(HS * h, HS * (h + 1))
            ds_at = BLK * (h % 2)
            dq_t[here, :] += jnp.dot(
                slots[slot, here, :],
                work[h // 2, :, ds_at : ds_at + BLK],
                preferred_element_type=F32,
            )
            for g in ((), (0,), (3,), (1,), (2, 4))[h]:
                dkv[slot, :, 128 * g : 128 * (g + 1)] = jnp.dot(
                    work[g], rows[g], preferred_element_type=F32
                ).astype(BF16)

        @pl.when(step == 0)
        def _():
            to_far.start()

        @pl.when(step == 1)
        def _():
            to_far.wait_recv()
            sums[0] = (dkv[4].astype(F32) + from_mate[0].astype(F32)).astype(BF16)
            chain.start()
            back_first.start()
            attn = out_t[...].T.astype(BF16)
            for part in range(4):
                piece = slice(WIDTH * part, WIDTH * (part + 1))
                term = jnp.dot(cot_all[piece, :], attn, preferred_element_type=F32)
                wt[part] = term.astype(BF16)
            for copy in z_copies:
                copy.start()

        @pl.when(step == 2)
        def _():
            to_near.start()

        @pl.when(step == 3)
        def _():
            to_near.wait_recv()
            both = dkv[2].astype(F32) + from_mate[1].astype(F32)
            chain.wait_recv()
            sums[1, 0:HALF] = (both[0:HALF] + chain_in[...].astype(F32)).astype(BF16)
            sums[1, HALF:BLK] = both[HALF:BLK].astype(BF16)
            homeward.start()
            back_first.wait_recv()
            back_second.start()

        @pl.when(step == 4)
        def _():
            edge_copy.start()
            for copy in z_copies:
                copy.wait_recv()
            z_sum[...] = wt[z].astype(F32)
            for i in range(3):
                z_sum[...] += z_in[i].astype(F32)
            for copy in y_copies:
                copy.start()

        return carry

    lax.fori_loop(0, BACK + 1, backward, 0)

    dq_ref[...] = (dq_t[...] * HS**-0.5).astype(BF16)
    total = z_sum[pl.ds(pl.multiple_of(40 * low, 8), 40), :]
    for i, copy in enumerate(y_copies):
        copy.wait_recv()
        total = total + y_in[i]
    dw_ref[...] = total

    edge_copy.wait_recv()
    homeward.wait_recv()
    back_second.wait_recv()
    for half in range(2):
        part = slice(HALF * half, HALF * (half + 1))
        total = dkv[0, part].astype(F32) + edge[part].astype(F32) + home_near[part].astype(F32)
        if half == 1:
            total = total + home_far[...].astype(F32)
        total_t = total.T.astype(BF16)
        dk_ref[:, part] = total_t[:WIDTH]
        dv_ref[:, part] = total_t[WIDTH:]

    copies = [near_k, near_v, relay_first, direct_k, direct_v, chain_k, relay_second]
    copies += [pass_near_k, pass_near_v, pass_far_k, pass_far_v]
    copies += [to_far, to_near, chain, back_first, back_second, homeward, edge_copy]
    for copy in across + copies + z_copies + y_copies:
        copy.wait_send()


def shards(queries, key_rows, value_rows, cotangent, out_weight, segment_units, left_segments):
    tm_count = lax.axis_size("tm")
    head_count = lax.axis_size("head")
    anywhere = pl.BlockSpec(memory_space=pl.ANY)
    vmem = pl.BlockSpec(memory_space=pltpu.VMEM)
    dma = pltpu.SemaphoreType.DMA
    out_t = jax.ShapeDtypeStruct((WIDTH, BLK), BF16)
    both = 2 * WIDTH
    blocks = BACK + 1
    query_t, key_t, value_t, weight_t = pl.pallas_call(
        functools.partial(kernel, tm_count, head_count),
        out_shape=(out_t, out_t, out_t, jax.ShapeDtypeStruct((40, WIDTH), F32)),
        in_specs=[vmem] * 2 + [anywhere] * 5,
        out_specs=(vmem, vmem, vmem, vmem),
        scratch_shapes=[
            pltpu.VMEM((blocks, both, BLK), BF16),
            pltpu.VMEM((WIDTH, BLK), BF16),
            pltpu.VMEM((blocks, BLK, both), BF16),
            pltpu.VMEM((blocks, HEADS, BLK, BLK), BF16),
            pltpu.VMEM((head_count * WIDTH, BLK), BF16),
            pltpu.VMEM((WIDTH, head_count * WIDTH), BF16),
            pltpu.VMEM((WIDTH, BLK), BF16),
            pltpu.VMEM((HEADS, 256, BLK), BF16),
            pltpu.VMEM((HEADS, 128, BLK), BF16),
            pltpu.VMEM((HEADS, 2 * BLK, 128), BF16),
            pltpu.VMEM((2, BLK, BLK), F32),
            pltpu.VMEM((HEADS, BLK, 2 * BLK), BF16),
            pltpu.VMEM((WIDTH, BLK), F32),
            pltpu.VMEM((WIDTH, BLK), F32),
            pltpu.VMEM((blocks, HEADS, 8, BLK), F32),
            pltpu.VMEM((HEADS, 8, BLK), F32),
            pltpu.VMEM((HEADS, 8, BLK), F32),
            pltpu.VMEM((HEADS, 8, BLK), F32),
            pltpu.VMEM((blocks, BLK, both), BF16),
            pltpu.VMEM((2, BLK, both), BF16),
            pltpu.VMEM((2, BLK, both), BF16),
            pltpu.VMEM((BLK, both), BF16),
            pltpu.VMEM((HALF, both), BF16),
            pltpu.VMEM((HALF, both), BF16),
            pltpu.VMEM((HALF, both), BF16),
            pltpu.VMEM((BLK, both), BF16),
            pltpu.VMEM((4, WIDTH, WIDTH), BF16),
            pltpu.VMEM((3, WIDTH, WIDTH), BF16),
            pltpu.VMEM((WIDTH, WIDTH), F32),
            pltpu.VMEM((7, 40, WIDTH), F32),
            dma((5,)),
            dma((11,)),
            dma((blocks,)),
            dma((blocks,)),
            dma((1,)),
            dma((3,)),
            dma((3,)),
            dma((7,)),
            dma((7,)),
            dma((3,)),
            dma((3,)),
            dma((7,)),
            dma((7,)),
        ],
        compiler_params=pltpu.CompilerParams(
            collective_id=0, has_side_effects=True, vmem_limit_bytes=60 << 20
        ),
    )(
        segment_units.reshape(1, -1),
        left_segments.reshape(1, -1),
        queries.T,
        key_rows.T,
        value_rows.T,
        cotangent.T,
        out_weight,
    )
    return (query_t.T, key_t.T, value_t.T, weight_t.T)


def solution(mesh):
    placed = (
        P("tm", "head"),
        P("tm", "head"),
        P("tm", "head"),
        P("tm", "head"),
        P("head", None),
        P(),
        P(),
    )
    return jax.shard_map(
        shards,
        mesh=mesh,
        in_specs=placed,
        out_specs=(P("tm", "head"), P("tm", "head"), P("tm", "head"), P("head", "tm")),
        check_vma=False,
    )
```

```python
import functools

import jax
import jax.numpy as jnp
from jax import lax
from jax.experimental import pallas as pl
from jax.experimental.pallas import tpu as pltpu
from jax.sharding import PartitionSpec as P

HS = 64
UNIT = 16
BLK = 512
HEADS = 5
WIDTH = HEADS * HS
BACK = 5
HALF = BLK // 2
STRIP = 128
WIDE = 256
HIDDEN = -2e30
LOWEST = -1e30
F32 = jnp.float32
BF16 = jnp.bfloat16
MESH = pl.DeviceIdType.MESH


def kernel(
    tm_count,
    head_count,
    units_ref,
    left_ref,
    q_hbm,
    k_hbm,
    v_hbm,
    cot_hbm,
    w_hbm,
    dq_ref,
    dk_ref,
    dv_ref,
    dw_ref,
    slots,
    relay,
    cross,
    kv_all,
    probs,
    cot_all,
    w_ref,
    q_ref,
    rhs,
    gt,
    rows,
    square,
    work,
    out_t,
    dq_t,
    m_all,
    m_run,
    l_run,
    delta,
    dkv,
    from_mate,
    sums,
    home_near,
    home_far,
    chain_in,
    relay_back,
    cross_back,
    edge,
    wt,
    z_in,
    z_sum,
    y_in,
    local,
    sent,
    got_k,
    got_v,
    got_relay,
    side_sent,
    side_got,
    back_sent,
    back_got,
    z_sent,
    z_got,
    y_sent,
    y_got,
):
    t = lax.axis_index("tm")
    x = lax.axis_index("head")
    core = t % 2
    z = t // 8
    y = (t // 2) % 4
    low = t % 8
    sides = range(1, head_count)

    def at(place):
        return {"tm": (place + tm_count) % tm_count}

    def chip(z_place, y_place):
        return (((z_place + 4) % 4) * 4 + y_place % 4) * 2 + core

    mate = at(t + 1 - 2 * core)
    before, after = chip(z, y + 3), chip(z, y + 1)
    inner = jnp.where((y == 1) | (y == 2), 1, 0)
    relay_to = chip(z + jnp.where(y >= 2, 1, 0), y + 3)
    relay_from = chip(z - inner, y + 1)
    back_to = chip(z - jnp.where(y < 2, 1, 0), y + 1)
    back_from = chip(z + inner, y + 3)

    greeted = [at(t - 2), at(t + 2), at(relay_from), at(back_from)]
    greeted += [{"head": (x + head_count - i) % head_count} for i in sides]
    greeted += [at(t - 8 * i) for i in range(1, 4)]
    greeted += [at(8 * z + (low + 8 - i) % 8) for i in range(1, 8)]
    barrier = pltpu.get_barrier_semaphore()
    for target in greeted:
        pl.semaphore_signal(barrier, inc=1, device_id=target, device_id_type=MESH)
    edge_source = at(t + 5 * (2 * core - 1))
    pl.semaphore_signal(barrier, inc=1, device_id=edge_source, device_id_type=MESH)

    loads = [
        pltpu.make_async_copy(k_hbm, slots.at[0, 0:WIDTH], local.at[0]),
        pltpu.make_async_copy(v_hbm, slots.at[0, WIDTH : 2 * WIDTH], local.at[1]),
        pltpu.make_async_copy(q_hbm, q_ref, local.at[2]),
        pltpu.make_async_copy(
            cot_hbm, cot_all.at[pl.ds(pl.multiple_of(WIDTH * x, 64), WIDTH)], local.at[3]
        ),
        pltpu.make_async_copy(w_hbm, w_ref, local.at[4]),
    ]
    for load in loads:
        load.start()
    pl.semaphore_wait(barrier, len(greeted) + 1)

    def push(src, dst, send_sem, recv_sem, target):
        return pltpu.make_async_remote_copy(
            src_ref=src,
            dst_ref=dst,
            send_sem=send_sem,
            recv_sem=recv_sem,
            device_id=target,
            device_id_type=MESH,
        )

    def keys(src, slot, number, target):
        return push(src, slots.at[slot, 0:WIDTH], sent.at[number], got_k.at[slot], target)

    def values(src, slot, number, target):
        return push(
            src, slots.at[slot, WIDTH : 2 * WIDTH], sent.at[number], got_v.at[slot], target
        )

    def key_part(slot):
        return slots.at[slot, 0:WIDTH]

    def value_part(slot):
        return slots.at[slot, WIDTH : 2 * WIDTH]

    near_k = keys(k_hbm, 2, 0, at(t + 2))
    near_v = values(v_hbm, 2, 1, at(t + 2))
    over_first = push(v_hbm, cross, sent.at[1], got_relay.at[1], at(t + 8))
    over_second = values(cross, 2, 11, at(t - 6))
    relay_first = push(v_hbm, relay, sent.at[2], got_relay.at[0], at(relay_to))
    near_k.start()
    relay_first.start()
    across = [
        push(
            cot_hbm,
            cot_all.at[pl.ds(pl.multiple_of(WIDTH * x, 64), WIDTH)],
            side_sent.at[i - 1],
            side_got.at[i - 1],
            {"head": (x + i) % head_count},
        )
        for i in sides
    ]
    for copy in across:
        copy.start()

    @pl.when(y < 3)
    def _():
        near_v.start()

    @pl.when(y == 3)
    def _():
        over_first.start()

    direct_slot = 1 + 4 * core
    direct_to = at(t + 1 + 4 * core)
    direct_k = keys(k_hbm, direct_slot, 3, direct_to)
    direct_v = values(v_hbm, direct_slot, 4, direct_to)
    direct_k.start()
    direct_v.start()
    chain_k = keys(key_part(2), 4, 5, at(t + 2))
    relay_second = values(relay, 4, 6, at(before))
    pass_near = 3 - 2 * core
    pass_far = 5 - 2 * core
    pass_near_k = keys(key_part(2), pass_near, 7, mate)
    pass_near_v = values(value_part(2), pass_near, 8, mate)
    pass_far_k = keys(key_part(4), pass_far, 9, mate)
    pass_far_v = values(value_part(4), pass_far, 10, mate)

    segments = units_ref.shape[1]
    units = jnp.broadcast_to(units_ref[...].astype(F32), (8, segments)).astype(BF16)
    lefts = jnp.broadcast_to(left_ref[...].astype(F32), (8, segments)).astype(BF16)
    down = lax.broadcasted_iota(jnp.int32, (segments, 128), 0)
    over = lax.broadcasted_iota(jnp.int32, (segments, 128), 1)
    until = jnp.where(down <= over, 1.0, 0.0).astype(BF16)
    ahead = jnp.where(down < over, 1.0, 0.0).astype(BF16)
    same = jnp.where(down == over, 1.0, 0.0).astype(BF16)
    end_row = jnp.dot(units, until, preferred_element_type=F32)[0:1, :] * UNIT
    start_row = jnp.dot(units, ahead, preferred_element_type=F32)[0:1, :] * UNIT
    columns = (((0,), (1,)), ((), ()))
    end_col = lax.dot_general(until, units, columns, preferred_element_type=F32)[:, 0:1] * UNIT
    left_col = lax.dot_general(same, lefts, columns, preferred_element_type=F32)[:, 0:1]
    frame_row = (t * BLK + lax.broadcasted_iota(jnp.int32, (1, BLK), 1)).astype(F32)
    own_seg = jnp.sum(jnp.where(end_col <= frame_row, 1.0, 0.0), axis=0, keepdims=True)
    seg_down = lax.broadcasted_iota(jnp.int32, (128, BLK), 0).astype(F32)
    reach = jnp.sum(jnp.where(seg_down == own_seg, left_col, 0.0), axis=0, keepdims=True)
    lowest = jnp.maximum(own_seg - reach, 0.0)
    bias = jnp.where((seg_down >= lowest) & (seg_down <= own_seg), 0.0, HIDDEN).astype(BF16)

    blank = jnp.zeros((HS, BLK), BF16)
    lane = lax.broadcasted_iota(jnp.int32, (BLK, 128), 1)

    def spread(j, upright, transposed):
        g, half = divmod(j, 2)
        both = [transposed, blank] if half == 0 else [blank, transposed]
        if j < HEADS:
            rhs[j] = jnp.concatenate(both + [bias], axis=0)
        else:
            gt[j - HEADS] = jnp.concatenate(both, axis=0)
        zeros = jnp.zeros((BLK, HS), BF16)
        pair = [upright, zeros] if half == 0 else [zeros, upright]
        rows[g, BLK * half : BLK * (half + 1), :] = jnp.concatenate(pair, axis=1)

    loads[2].wait()
    queries_t = (q_ref[...].astype(F32) * HS**-0.5).astype(BF16)
    for j in range(HEADS):
        mine = queries_t[HS * j : HS * (j + 1), :]
        spread(j, mine.T, mine)
    m_run[...] = jnp.full(m_run.shape, LOWEST, F32)
    l_run[...] = jnp.zeros(l_run.shape, F32)
    out_t[...] = jnp.zeros(out_t.shape, F32)
    dq_t[...] = jnp.zeros(dq_t.shape, F32)
    loads[0].wait()
    loads[1].wait()

    def wait_slot(slot):
        keys(k_hbm, slot, 0, mate).wait_recv()
        values(v_hbm, slot, 1, mate).wait_recv()

    def near_event():
        relay_first.wait_recv()
        relay_second.start()

        @pl.when(y == 3)
        def _():
            over_first.wait_recv()
            over_second.start()

        near_k.wait_recv()
        chain_k.start()
        pass_near_k.start()
        near_v.wait_recv()
        pass_near_v.start()

    def forward(step, carry):
        @pl.when(step == 1)
        def _():
            loads[3].wait()
            loads[4].wait()
            for copy in across:
                copy.wait_recv()
            grad_t = jnp.dot(w_ref[...], cot_all[...], preferred_element_type=F32).astype(BF16)
            for j in range(HEADS):
                mine = grad_t[HS * j : HS * (j + 1), :]
                spread(j + HEADS, mine.T, mine)

        swapped = jnp.where(step == 0, 0, jnp.where(step < 3, 3 - step, 8 - step))
        slot = jnp.where(core == 0, swapped, step)

        @pl.when(step == 1 + core)
        def _():
            near_event()

        @pl.when((step == 2 - core) | (step == 3) | (step == 5))
        def _():
            wait_slot(slot)

        @pl.when(step == 4)
        def _():
            keys(k_hbm, 4, 0, mate).wait_recv()
            pass_far_k.start()
            values(v_hbm, 4, 1, mate).wait_recv()
            pass_far_v.start()

        kv_all[slot] = slots[slot].T
        first = ((t + tm_count - slot) % tm_count) * BLK
        frames = (first + lax.broadcasted_iota(jnp.int32, (BLK, 128), 0)).astype(F32)
        hot = jnp.where((frames >= start_row) & (frames < end_row), 1.0, 0.0).astype(BF16)
        tops = []
        for turn in range(HEADS + 1):
            if turn < HEADS:
                g = turn // 2
                tops.append([None] * (BLK // WIDE))
            if turn > 0:
                h = turn - 1
                m_old = m_run[h, 0:1, :]
                top = [jnp.max(part, axis=0, keepdims=True) for part in tops[h]]
                m_new = jnp.maximum(m_old, jnp.concatenate(top, axis=1))
                factor = jnp.exp(m_old - m_new)
                m_run[h, 0:1, :] = m_new
                m_all[slot, h, 0:1, :] = m_new
            for c in range(BLK // WIDE):
                cols = slice(WIDE * c, WIDE * (c + 1))
                if turn > 0:
                    total = l_run[h, :, cols] * factor[:, cols]
                for r in range(0, BLK, STRIP):
                    if turn < HEADS:
                        lhs = jnp.concatenate(
                            [kv_all[slot, r : r + STRIP, 128 * g : 128 * (g + 1)], hot[r : r + STRIP]],
                            axis=1,
                        )
                        scores = jnp.dot(lhs, rhs[turn, :, cols], preferred_element_type=F32)
                        square[turn % 2, r : r + STRIP, cols] = scores
                        fold = jnp.max(scores.reshape(STRIP // 8, 8, WIDE), axis=0)
                        seen = tops[turn][c]
                        tops[turn][c] = fold if seen is None else jnp.maximum(seen, fold)
                    if turn > 0:
                        p = jnp.exp(square[h % 2, r : r + STRIP, cols] - m_new[:, cols])
                        total = total + jnp.sum(p.reshape(STRIP // 8, 8, WIDE), axis=0)
                        probs[slot, h, r : r + STRIP, cols] = p.astype(BF16)
                if turn > 0:
                    l_run[h, :, cols] = total
                    here = slice(HS * h, HS * (h + 1))
                    out_t[here, cols] = out_t[here, cols] * factor[:, cols] + jnp.dot(
                        slots[slot, WIDTH + HS * h : WIDTH + HS * (h + 1), :],
                        probs[slot, h, :, cols],
                        preferred_element_type=F32,
                    )
        return carry

    lax.fori_loop(0, BACK + 1, forward, 0)

    for h in range(HEADS):
        here = slice(HS * h, HS * (h + 1))
        total = jnp.sum(l_run[h], axis=0, keepdims=True)
        out = out_t[here, :] / total
        out_t[here, :] = out
        side = HS * ((h + HEADS) % 2)
        own_grad = gt[h, side : side + HS, :].astype(F32)
        delta[h, 0:1, :] = jnp.sum(out * own_grad, axis=0, keepdims=True)
        l_run[h, 0:1, :] = m_run[h, 0:1, :] + jnp.log(total)

    z_copies = [
        push(
            wt.at[(z + i) % 4], z_in.at[i - 1], z_sent.at[i - 1], z_got.at[i - 1], at(t + 8 * i)
        )
        for i in range(1, 4)
    ]
    attn = out_t[...].T.astype(BF16)
    for part in range(4):
        piece = slice(WIDTH * part, WIDTH * (part + 1))
        wt[part] = jnp.dot(cot_all[piece, :], attn, preferred_element_type=F32).astype(BF16)
    for copy in z_copies:
        copy.start()
    y_copies = [
        push(
            z_sum.at[pl.ds(pl.multiple_of(40 * ((low + i) % 8), 8), 40)],
            y_in.at[i - 1],
            y_sent.at[i - 1],
            y_got.at[i - 1],
            at(8 * z + (low + i) % 8),
        )
        for i in range(1, 8)
    ]

    far_slot, near_slot, edge_slot = 3 + 2 * core, 1 + 2 * core, 5 - 4 * core
    to_far = push(dkv.at[far_slot], from_mate.at[0], back_sent.at[0], back_got.at[0], mate)
    to_near = push(dkv.at[near_slot], from_mate.at[1], back_sent.at[1], back_got.at[1], mate)
    chain = push(sums.at[0, 0:HALF], chain_in, back_sent.at[2], back_got.at[2], at(t - 2))
    back_first = push(
        sums.at[0, HALF:BLK], relay_back, back_sent.at[3], back_got.at[3], at(back_to)
    )
    back_second = push(relay_back, home_far, back_sent.at[4], back_got.at[4], at(after))
    home_a = push(
        sums.at[1, 0:HALF], home_near.at[0:HALF], back_sent.at[5], back_got.at[5], at(t - 2)
    )
    home_b = push(
        sums.at[1, HALF:BLK], home_near.at[HALF:BLK], back_sent.at[7], back_got.at[7], at(t - 2)
    )
    over_back = push(sums.at[1, HALF:BLK], cross_back, back_sent.at[7], back_got.at[8], at(t - 8))
    over_home = push(
        cross_back, home_near.at[HALF:BLK], back_sent.at[8], back_got.at[7], at(t + 6)
    )
    edge_to = at(t - 5 + 4 * core)
    edge_copy = push(dkv.at[edge_slot], edge, back_sent.at[6], back_got.at[6], edge_to)

    def backward(step, carry):
        crossed = jnp.where(
            step < 2, 3 + step, jnp.where(step < 4, step - 1, jnp.where(step == 4, 5, 0))
        )
        slot = jnp.where(core == 0, crossed, 5 - step)
        for turn in range(HEADS + 1):
            if turn < HEADS:
                g = (turn + HEADS) // 2
                scale = jnp.exp(m_all[slot, turn, 0:1, :] - l_run[turn, 0:1, :])
                shift = delta[turn, 0:1, :]
                ds_at, p_at = BLK * (turn % 2), BLK * ((turn + HEADS) % 2)
                for c in range(0, BLK, WIDE):
                    cols = slice(c, c + WIDE)
                    for r in range(0, BLK, STRIP):
                        down = slice(r, r + STRIP)
                        grad_p = jnp.dot(
                            kv_all[slot, down, 128 * g : 128 * (g + 1)],
                            gt[turn, :, cols],
                            preferred_element_type=F32,
                        )
                        p = probs[slot, turn, down, cols].astype(F32) * scale[:, cols]
                        ds = p * (grad_p - shift[:, cols])
                        work[turn // 2, down, ds_at + c : ds_at + c + WIDE] = ds.astype(BF16)
                        work[(turn + HEADS) // 2, down, p_at + c : p_at + c + WIDE] = p.astype(
                            BF16
                        )
            if turn == 0:
                continue
            h = turn - 1
            here = slice(HS * h, HS * (h + 1))
            ds_at = BLK * (h % 2)
            dq_t[here, :] += jnp.dot(
                slots[slot, here, :],
                work[h // 2, :, ds_at : ds_at + BLK],
                preferred_element_type=F32,
            )
            for g in ((), (0,), (3,), (1,), (2, 4))[h]:
                for r in range(0, BLK, HALF):
                    dkv[slot, r : r + HALF, 128 * g : 128 * (g + 1)] = jnp.dot(
                        work[g, r : r + HALF, :], rows[g], preferred_element_type=F32
                    ).astype(BF16)

        @pl.when(step == 0)
        def _():
            to_far.start()

        @pl.when(step == 1)
        def _():
            to_far.wait_recv()
            sums[0] = (dkv[4].astype(F32) + from_mate[0].astype(F32)).astype(BF16)
            chain.start()
            back_first.start()

        @pl.when(step == 2)
        def _():
            to_near.start()
            for copy in z_copies:
                copy.wait_recv()
            z_sum[...] = wt[z].astype(F32)
            for i in range(3):
                z_sum[...] += z_in[i].astype(F32)
            for copy in y_copies:
                copy.start()

        @pl.when(step == 3)
        def _():
            to_near.wait_recv()
            both = dkv[2].astype(F32) + from_mate[1].astype(F32)
            chain.wait_recv()
            sums[1, 0:HALF] = (both[0:HALF] + chain_in[...].astype(F32)).astype(BF16)
            sums[1, HALF:BLK] = both[HALF:BLK].astype(BF16)
            home_a.start()

            @pl.when(y > 0)
            def _():
                home_b.start()

            @pl.when(y == 0)
            def _():
                over_back.start()

            back_first.wait_recv()
            back_second.start()

        @pl.when(step == 4)
        def _():
            edge_copy.start()

            @pl.when(y == 0)
            def _():
                over_back.wait_recv()
                over_home.start()

        return carry

    lax.fori_loop(0, BACK + 1, backward, 0)

    dq_ref[...] = (dq_t[...] * HS**-0.5).astype(BF16)
    total = z_sum[pl.ds(pl.multiple_of(40 * low, 8), 40), :]
    for i, copy in enumerate(y_copies):
        copy.wait_recv()
        total = total + y_in[i]
    dw_ref[...] = total

    edge_copy.wait_recv()
    home_a.wait_recv()
    home_b.wait_recv()
    back_second.wait_recv()
    for half in range(2):
        part = slice(HALF * half, HALF * (half + 1))
        total = dkv[0, part].astype(F32) + edge[part].astype(F32) + home_near[part].astype(F32)
        if half == 1:
            total = total + home_far[...].astype(F32)
        total_t = total.T.astype(BF16)
        dk_ref[:, part] = total_t[:WIDTH]
        dv_ref[:, part] = total_t[WIDTH:]

    copies = [near_k, near_v, relay_first, direct_k, direct_v, chain_k, relay_second]
    copies += [pass_near_k, pass_near_v, pass_far_k, pass_far_v]
    copies += [to_far, to_near, chain, back_first, back_second, home_a, home_b, edge_copy]
    for copy in across + copies + z_copies + y_copies:
        copy.wait_send()

    @pl.when(y == 3)
    def _():
        over_second.wait_send()

    @pl.when(y == 0)
    def _():
        over_home.wait_send()


def shards(queries, key_rows, value_rows, cotangent, out_weight, segment_units, left_segments):
    tm_count = lax.axis_size("tm")
    head_count = lax.axis_size("head")
    anywhere = pl.BlockSpec(memory_space=pl.ANY)
    vmem = pl.BlockSpec(memory_space=pltpu.VMEM)
    dma = pltpu.SemaphoreType.DMA
    out_t = jax.ShapeDtypeStruct((WIDTH, BLK), BF16)
    both = 2 * WIDTH
    blocks = BACK + 1
    query_t, key_t, value_t, weight_t = pl.pallas_call(
        functools.partial(kernel, tm_count, head_count),
        out_shape=(out_t, out_t, out_t, jax.ShapeDtypeStruct((40, WIDTH), F32)),
        in_specs=[vmem] * 2 + [anywhere] * 5,
        out_specs=(vmem, vmem, vmem, vmem),
        scratch_shapes=[
            pltpu.VMEM((blocks, both, BLK), BF16),
            pltpu.VMEM((WIDTH, BLK), BF16),
            pltpu.VMEM((WIDTH, BLK), BF16),
            pltpu.VMEM((blocks, BLK, both), BF16),
            pltpu.VMEM((blocks, HEADS, BLK, BLK), BF16),
            pltpu.VMEM((head_count * WIDTH, BLK), BF16),
            pltpu.VMEM((WIDTH, head_count * WIDTH), BF16),
            pltpu.VMEM((WIDTH, BLK), BF16),
            pltpu.VMEM((HEADS, 256, BLK), BF16),
            pltpu.VMEM((HEADS, 128, BLK), BF16),
            pltpu.VMEM((HEADS, 2 * BLK, 128), BF16),
            pltpu.VMEM((2, BLK, BLK), F32),
            pltpu.VMEM((HEADS, BLK, 2 * BLK), BF16),
            pltpu.VMEM((WIDTH, BLK), F32),
            pltpu.VMEM((WIDTH, BLK), F32),
            pltpu.VMEM((blocks, HEADS, 8, BLK), F32),
            pltpu.VMEM((HEADS, 8, BLK), F32),
            pltpu.VMEM((HEADS, 8, BLK), F32),
            pltpu.VMEM((HEADS, 8, BLK), F32),
            pltpu.VMEM((blocks, BLK, both), BF16),
            pltpu.VMEM((2, BLK, both), BF16),
            pltpu.VMEM((2, BLK, both), BF16),
            pltpu.VMEM((BLK, both), BF16),
            pltpu.VMEM((HALF, both), BF16),
            pltpu.VMEM((HALF, both), BF16),
            pltpu.VMEM((HALF, both), BF16),
            pltpu.VMEM((HALF, both), BF16),
            pltpu.VMEM((BLK, both), BF16),
            pltpu.VMEM((4, WIDTH, WIDTH), BF16),
            pltpu.VMEM((3, WIDTH, WIDTH), BF16),
            pltpu.VMEM((WIDTH, WIDTH), F32),
            pltpu.VMEM((7, 40, WIDTH), F32),
            dma((5,)),
            dma((12,)),
            dma((blocks,)),
            dma((blocks,)),
            dma((2,)),
            dma((3,)),
            dma((3,)),
            dma((9,)),
            dma((9,)),
            dma((3,)),
            dma((3,)),
            dma((7,)),
            dma((7,)),
        ],
        compiler_params=pltpu.CompilerParams(
            collective_id=0, has_side_effects=True, vmem_limit_bytes=60 << 20
        ),
    )(
        segment_units.reshape(1, -1),
        left_segments.reshape(1, -1),
        queries.T,
        key_rows.T,
        value_rows.T,
        cotangent.T,
        out_weight,
    )
    return (query_t.T, key_t.T, value_t.T, weight_t.T)


def solution(mesh):
    placed = (
        P("tm", "head"),
        P("tm", "head"),
        P("tm", "head"),
        P("tm", "head"),
        P("head", None),
        P(),
        P(),
    )
    return jax.shard_map(
        shards,
        mesh=mesh,
        in_specs=placed,
        out_specs=(P("tm", "head"), P("tm", "head"), P("tm", "head"), P("head", "tm")),
        check_vma=False,
    )
```

```python
import functools

import jax
import jax.numpy as jnp
from jax import lax
from jax.experimental import pallas as pl
from jax.experimental.pallas import tpu as pltpu
from jax.sharding import PartitionSpec as P

HS = 64
UNIT = 16
BLK = 512
HEADS = 5
WIDTH = HEADS * HS
BACK = 5
HALF = BLK // 2
STRIP = 128
WIDE = 256
HIDDEN = -2e30
LOWEST = -1e30
F32 = jnp.float32
BF16 = jnp.bfloat16
MESH = pl.DeviceIdType.MESH


def kernel(
    tm_count,
    head_count,
    units_ref,
    left_ref,
    q_hbm,
    k_hbm,
    v_hbm,
    cot_hbm,
    w_hbm,
    dq_ref,
    dk_ref,
    dv_ref,
    dw_ref,
    slots,
    relay,
    cross,
    kv_all,
    probs,
    cot_all,
    w_ref,
    q_ref,
    rhs,
    gt,
    rows,
    square,
    work,
    out_t,
    dq_t,
    m_all,
    m_run,
    l_run,
    delta,
    dkv,
    from_mate,
    sums,
    home_near,
    home_far,
    chain_in,
    relay_back,
    cross_back,
    edge,
    wt,
    z_in,
    z_sum,
    y_in,
    local,
    sent,
    got_k,
    got_v,
    got_relay,
    side_sent,
    side_got,
    back_sent,
    back_got,
    z_sent,
    z_got,
    y_sent,
    y_got,
):
    t = lax.axis_index("tm")
    x = lax.axis_index("head")
    core = t % 2
    z = t // 8
    y = (t // 2) % 4
    low = t % 8
    sides = range(1, head_count)

    def at(place):
        return {"tm": (place + tm_count) % tm_count}

    def chip(z_place, y_place):
        return (((z_place + 4) % 4) * 4 + y_place % 4) * 2 + core

    mate = at(t + 1 - 2 * core)
    before, after = chip(z, y + 3), chip(z, y + 1)
    inner = jnp.where((y == 1) | (y == 2), 1, 0)
    relay_to = chip(z + jnp.where(y >= 2, 1, 0), y + 3)
    relay_from = chip(z - inner, y + 1)
    back_to = chip(z - jnp.where(y < 2, 1, 0), y + 1)
    back_from = chip(z + inner, y + 3)

    greeted = [at(t - 2), at(t + 2), at(relay_from), at(back_from)]
    greeted += [{"head": (x + head_count - i) % head_count} for i in sides]
    greeted += [at(t - 8 * i) for i in range(1, 4)]
    greeted += [at(8 * z + (low + 8 - i) % 8) for i in range(1, 8)]
    barrier = pltpu.get_barrier_semaphore()
    for target in greeted:
        pl.semaphore_signal(barrier, inc=1, device_id=target, device_id_type=MESH)
    edge_source = at(t + 5 * (2 * core - 1))
    pl.semaphore_signal(barrier, inc=1, device_id=edge_source, device_id_type=MESH)

    loads = [
        pltpu.make_async_copy(k_hbm, slots.at[0, 0:WIDTH], local.at[0]),
        pltpu.make_async_copy(v_hbm, slots.at[0, WIDTH : 2 * WIDTH], local.at[1]),
        pltpu.make_async_copy(q_hbm, q_ref, local.at[2]),
        pltpu.make_async_copy(
            cot_hbm, cot_all.at[pl.ds(pl.multiple_of(WIDTH * x, 64), WIDTH)], local.at[3]
        ),
        pltpu.make_async_copy(w_hbm, w_ref, local.at[4]),
    ]
    for load in loads:
        load.start()
    pl.semaphore_wait(barrier, len(greeted) + 1)

    def push(src, dst, send_sem, recv_sem, target):
        return pltpu.make_async_remote_copy(
            src_ref=src,
            dst_ref=dst,
            send_sem=send_sem,
            recv_sem=recv_sem,
            device_id=target,
            device_id_type=MESH,
        )

    def keys(src, slot, number, target):
        return push(src, slots.at[slot, 0:WIDTH], sent.at[number], got_k.at[slot], target)

    def values(src, slot, number, target):
        return push(
            src, slots.at[slot, WIDTH : 2 * WIDTH], sent.at[number], got_v.at[slot], target
        )

    def key_part(slot):
        return slots.at[slot, 0:WIDTH]

    def value_part(slot):
        return slots.at[slot, WIDTH : 2 * WIDTH]

    near_k = keys(k_hbm, 2, 0, at(t + 2))
    near_v = values(v_hbm, 2, 1, at(t + 2))
    over_first = push(v_hbm, cross, sent.at[1], got_relay.at[1], at(t + 8))
    over_second = values(cross, 2, 11, at(t - 6))
    relay_first = push(v_hbm, relay, sent.at[2], got_relay.at[0], at(relay_to))
    near_k.start()
    relay_first.start()
    across = [
        push(
            cot_hbm,
            cot_all.at[pl.ds(pl.multiple_of(WIDTH * x, 64), WIDTH)],
            side_sent.at[i - 1],
            side_got.at[i - 1],
            {"head": (x + i) % head_count},
        )
        for i in sides
    ]
    for copy in across:
        copy.start()

    @pl.when(y < 3)
    def _():
        near_v.start()

    @pl.when(y == 3)
    def _():
        over_first.start()

    direct_slot = 1 + 4 * core
    direct_to = at(t + 1 + 4 * core)
    direct_k = keys(k_hbm, direct_slot, 3, direct_to)
    direct_v = values(v_hbm, direct_slot, 4, direct_to)
    direct_k.start()
    direct_v.start()
    chain_k = keys(key_part(2), 4, 5, at(t + 2))
    relay_second = values(relay, 4, 6, at(before))
    pass_near = 3 - 2 * core
    pass_far = 5 - 2 * core
    pass_near_k = keys(key_part(2), pass_near, 7, mate)
    pass_near_v = values(value_part(2), pass_near, 8, mate)
    pass_far_k = keys(key_part(4), pass_far, 9, mate)
    pass_far_v = values(value_part(4), pass_far, 10, mate)

    segments = units_ref.shape[1]
    units = jnp.broadcast_to(units_ref[...].astype(F32), (8, segments)).astype(BF16)
    lefts = jnp.broadcast_to(left_ref[...].astype(F32), (8, segments)).astype(BF16)
    down = lax.broadcasted_iota(jnp.int32, (segments, 128), 0)
    over = lax.broadcasted_iota(jnp.int32, (segments, 128), 1)
    until = jnp.where(down <= over, 1.0, 0.0).astype(BF16)
    ahead = jnp.where(down < over, 1.0, 0.0).astype(BF16)
    same = jnp.where(down == over, 1.0, 0.0).astype(BF16)
    end_row = jnp.dot(units, until, preferred_element_type=F32)[0:1, :] * UNIT
    start_row = jnp.dot(units, ahead, preferred_element_type=F32)[0:1, :] * UNIT
    columns = (((0,), (1,)), ((), ()))
    end_col = lax.dot_general(until, units, columns, preferred_element_type=F32)[:, 0:1] * UNIT
    left_col = lax.dot_general(same, lefts, columns, preferred_element_type=F32)[:, 0:1]
    frame_row = (t * BLK + lax.broadcasted_iota(jnp.int32, (1, BLK), 1)).astype(F32)
    own_seg = jnp.sum(jnp.where(end_col <= frame_row, 1.0, 0.0), axis=0, keepdims=True)
    seg_down = lax.broadcasted_iota(jnp.int32, (128, BLK), 0).astype(F32)
    reach = jnp.sum(jnp.where(seg_down == own_seg, left_col, 0.0), axis=0, keepdims=True)
    lowest = jnp.maximum(own_seg - reach, 0.0)
    bias = jnp.where((seg_down >= lowest) & (seg_down <= own_seg), 0.0, HIDDEN).astype(BF16)

    blank = jnp.zeros((HS, BLK), BF16)
    lane = lax.broadcasted_iota(jnp.int32, (BLK, 128), 1)

    def spread(j, upright, transposed):
        g, half = divmod(j, 2)
        both = [transposed, blank] if half == 0 else [blank, transposed]
        if j < HEADS:
            rhs[j] = jnp.concatenate(both + [bias], axis=0)
        else:
            gt[j - HEADS] = jnp.concatenate(both, axis=0)
        zeros = jnp.zeros((BLK, HS), BF16)
        pair = [upright, zeros] if half == 0 else [zeros, upright]
        rows[g, BLK * half : BLK * (half + 1), :] = jnp.concatenate(pair, axis=1)

    loads[2].wait()
    queries_t = (q_ref[...].astype(F32) * HS**-0.5).astype(BF16)
    for j in range(HEADS):
        mine = queries_t[HS * j : HS * (j + 1), :]
        spread(j, mine.T, mine)
    m_run[...] = jnp.full(m_run.shape, LOWEST, F32)
    l_run[...] = jnp.zeros(l_run.shape, F32)
    out_t[...] = jnp.zeros(out_t.shape, F32)
    dq_t[...] = jnp.zeros(dq_t.shape, F32)
    loads[0].wait()
    loads[1].wait()

    def wait_slot(slot):
        keys(k_hbm, slot, 0, mate).wait_recv()
        values(v_hbm, slot, 1, mate).wait_recv()

    def near_event():
        relay_first.wait_recv()
        relay_second.start()

        @pl.when(y == 3)
        def _():
            over_first.wait_recv()
            over_second.start()

        near_k.wait_recv()
        chain_k.start()
        pass_near_k.start()
        near_v.wait_recv()
        pass_near_v.start()

    def forward(step, carry):
        @pl.when(step == 1)
        def _():
            loads[3].wait()
            loads[4].wait()
            for copy in across:
                copy.wait_recv()
            grad_t = jnp.dot(w_ref[...], cot_all[...], preferred_element_type=F32).astype(BF16)
            for j in range(HEADS):
                mine = grad_t[HS * j : HS * (j + 1), :]
                spread(j + HEADS, mine.T, mine)

        swapped = jnp.where(step == 0, 0, jnp.where(step < 3, 3 - step, 8 - step))
        slot = jnp.where(core == 0, swapped, step)

        @pl.when(step == 1 + core)
        def _():
            near_event()

        @pl.when((step == 2 - core) | (step == 3) | (step == 5))
        def _():
            wait_slot(slot)

        @pl.when(step == 4)
        def _():
            keys(k_hbm, 4, 0, mate).wait_recv()
            pass_far_k.start()
            values(v_hbm, 4, 1, mate).wait_recv()
            pass_far_v.start()

        def upright(g):
            group = slice(128 * g, 128 * (g + 1))
            kv_all[slot, :, group] = slots[slot, group, :].T

        first = ((t + tm_count - slot) % tm_count) * BLK
        frames = (first + lax.broadcasted_iota(jnp.int32, (BLK, 128), 0)).astype(F32)
        hot = jnp.where((frames >= start_row) & (frames < end_row), 1.0, 0.0).astype(BF16)
        upright(0)
        pieces = BLK // WIDE
        units_of = HEADS * pieces
        top = None
        for turn in range(units_of + 1):
            last = top
            if turn < units_of:
                h, c = divmod(turn, pieces)
                cols = slice(WIDE * c, WIDE * (c + 1))
                g = h // 2
                lhs = jnp.concatenate([kv_all[slot, :, 128 * g : 128 * (g + 1)], hot], axis=1)
                scores = jnp.dot(lhs, rhs[h, :, cols], preferred_element_type=F32)
                square[turn % 2] = scores
                top = jnp.max(scores.reshape(BLK // 8, 8, WIDE), axis=0)
                if turn < HEADS - 1:
                    upright(turn + 1)
            if turn == 0:
                continue
            h, c = divmod(turn - 1, pieces)
            cols = slice(WIDE * c, WIDE * (c + 1))
            m_old = m_run[h, 0:1, cols]
            m_new = jnp.maximum(m_old, jnp.max(last, axis=0, keepdims=True))
            factor = jnp.exp(m_old - m_new)
            m_run[h, 0:1, cols] = m_new
            m_all[slot, h, 0:1, cols] = m_new
            total = l_run[h, :, cols] * factor
            for r in range(0, BLK, STRIP):
                p = jnp.exp(square[(turn - 1) % 2, r : r + STRIP, :] - m_new)
                total = total + jnp.sum(p.reshape(STRIP // 8, 8, WIDE), axis=0)
                probs[slot, h, r : r + STRIP, cols] = p.astype(BF16)
            l_run[h, :, cols] = total
            here = slice(HS * h, HS * (h + 1))
            out_t[here, cols] = out_t[here, cols] * factor + jnp.dot(
                slots[slot, WIDTH + HS * h : WIDTH + HS * (h + 1), :],
                probs[slot, h, :, cols],
                preferred_element_type=F32,
            )
        return carry

    lax.fori_loop(0, BACK + 1, forward, 0)

    for h in range(HEADS):
        here = slice(HS * h, HS * (h + 1))
        total = jnp.sum(l_run[h], axis=0, keepdims=True)
        out = out_t[here, :] / total
        out_t[here, :] = out
        side = HS * ((h + HEADS) % 2)
        own_grad = gt[h, side : side + HS, :].astype(F32)
        delta[h, 0:1, :] = jnp.sum(out * own_grad, axis=0, keepdims=True)
        l_run[h, 0:1, :] = m_run[h, 0:1, :] + jnp.log(total)

    z_copies = [
        push(
            wt.at[(z + i) % 4], z_in.at[i - 1], z_sent.at[i - 1], z_got.at[i - 1], at(t + 8 * i)
        )
        for i in range(1, 4)
    ]
    attn = out_t[...].T.astype(BF16)
    for part in range(4):
        piece = slice(WIDTH * part, WIDTH * (part + 1))
        wt[part] = jnp.dot(cot_all[piece, :], attn, preferred_element_type=F32).astype(BF16)
    for copy in z_copies:
        copy.start()
    y_copies = [
        push(
            z_sum.at[pl.ds(pl.multiple_of(40 * ((low + i) % 8), 8), 40)],
            y_in.at[i - 1],
            y_sent.at[i - 1],
            y_got.at[i - 1],
            at(8 * z + (low + i) % 8),
        )
        for i in range(1, 8)
    ]

    far_slot, near_slot, edge_slot = 3 + 2 * core, 1 + 2 * core, 5 - 4 * core
    to_far = push(dkv.at[far_slot], from_mate.at[0], back_sent.at[0], back_got.at[0], mate)
    to_near = push(dkv.at[near_slot], from_mate.at[1], back_sent.at[1], back_got.at[1], mate)
    chain = push(sums.at[0, 0:HALF], chain_in, back_sent.at[2], back_got.at[2], at(t - 2))
    back_first = push(
        sums.at[0, HALF:BLK], relay_back, back_sent.at[3], back_got.at[3], at(back_to)
    )
    back_second = push(relay_back, home_far, back_sent.at[4], back_got.at[4], at(after))
    home_a = push(
        sums.at[1, 0:HALF], home_near.at[0:HALF], back_sent.at[5], back_got.at[5], at(t - 2)
    )
    home_b = push(
        sums.at[1, HALF:BLK], home_near.at[HALF:BLK], back_sent.at[7], back_got.at[7], at(t - 2)
    )
    over_back = push(sums.at[1, HALF:BLK], cross_back, back_sent.at[7], back_got.at[8], at(t - 8))
    over_home = push(
        cross_back, home_near.at[HALF:BLK], back_sent.at[8], back_got.at[7], at(t + 6)
    )
    edge_to = at(t - 5 + 4 * core)
    edge_copy = push(dkv.at[edge_slot], edge, back_sent.at[6], back_got.at[6], edge_to)

    def backward(step, carry):
        crossed = jnp.where(
            step < 2, 3 + step, jnp.where(step < 4, step - 1, jnp.where(step == 4, 5, 0))
        )
        slot = jnp.where(core == 0, crossed, 5 - step)
        pieces = BLK // WIDE
        units_of = HEADS * pieces
        for turn in range(units_of + 1):
            if turn < units_of:
                h, c = divmod(turn, pieces)
                g = (h + HEADS) // 2
                square[turn % 2] = jnp.dot(
                    kv_all[slot, :, 128 * g : 128 * (g + 1)],
                    gt[h, :, WIDE * c : WIDE * (c + 1)],
                    preferred_element_type=F32,
                )
            if turn == 0:
                continue
            h, c = divmod(turn - 1, pieces)
            cols = slice(WIDE * c, WIDE * (c + 1))
            scale = jnp.exp(m_all[slot, h, 0:1, cols] - l_run[h, 0:1, cols])
            shift = delta[h, 0:1, cols]
            ds_at = BLK * (h % 2) + WIDE * c
            p_at = BLK * ((h + HEADS) % 2) + WIDE * c
            for r in range(0, BLK, STRIP):
                down = slice(r, r + STRIP)
                p = probs[slot, h, down, cols].astype(F32) * scale
                ds = p * (square[(turn - 1) % 2, down, :] - shift)
                work[h // 2, down, ds_at : ds_at + WIDE] = ds.astype(BF16)
                work[(h + HEADS) // 2, down, p_at : p_at + WIDE] = p.astype(BF16)
            here = slice(HS * h, HS * (h + 1))
            dq_t[here, cols] += jnp.dot(
                slots[slot, here, :],
                work[h // 2, :, ds_at : ds_at + WIDE],
                preferred_element_type=F32,
            )
            if c < pieces - 1:
                continue
            for g in ((), (0,), (3,), (1,), (2, 4))[h]:
                dkv[slot, :, 128 * g : 128 * (g + 1)] = jnp.dot(
                    work[g], rows[g], preferred_element_type=F32
                ).astype(BF16)

        @pl.when(step == 0)
        def _():
            to_far.start()

        @pl.when(step == 1)
        def _():
            to_far.wait_recv()
            sums[0] = (dkv[4].astype(F32) + from_mate[0].astype(F32)).astype(BF16)
            chain.start()
            back_first.start()

        @pl.when(step == 2)
        def _():
            to_near.start()
            for copy in z_copies:
                copy.wait_recv()
            z_sum[...] = wt[z].astype(F32)
            for i in range(3):
                z_sum[...] += z_in[i].astype(F32)
            for copy in y_copies:
                copy.start()

        @pl.when(step == 3)
        def _():
            to_near.wait_recv()
            both = dkv[2].astype(F32) + from_mate[1].astype(F32)
            chain.wait_recv()
            sums[1, 0:HALF] = (both[0:HALF] + chain_in[...].astype(F32)).astype(BF16)
            sums[1, HALF:BLK] = both[HALF:BLK].astype(BF16)
            home_a.start()

            @pl.when(y > 0)
            def _():
                home_b.start()

            @pl.when(y == 0)
            def _():
                over_back.start()

            back_first.wait_recv()
            back_second.start()

        @pl.when(step == 4)
        def _():
            edge_copy.start()

            @pl.when(y == 0)
            def _():
                over_back.wait_recv()
                over_home.start()

        return carry

    lax.fori_loop(0, BACK + 1, backward, 0)

    dq_ref[...] = (dq_t[...] * HS**-0.5).astype(BF16)
    total = z_sum[pl.ds(pl.multiple_of(40 * low, 8), 40), :]
    for i, copy in enumerate(y_copies):
        copy.wait_recv()
        total = total + y_in[i]
    dw_ref[...] = total

    edge_copy.wait_recv()
    home_a.wait_recv()
    home_b.wait_recv()
    back_second.wait_recv()
    for half in range(2):
        part = slice(HALF * half, HALF * (half + 1))
        total = dkv[0, part].astype(F32) + edge[part].astype(F32) + home_near[part].astype(F32)
        if half == 1:
            total = total + home_far[...].astype(F32)
        total_t = total.T.astype(BF16)
        dk_ref[:, part] = total_t[:WIDTH]
        dv_ref[:, part] = total_t[WIDTH:]

    copies = [near_k, near_v, relay_first, direct_k, direct_v, chain_k, relay_second]
    copies += [pass_near_k, pass_near_v, pass_far_k, pass_far_v]
    copies += [to_far, to_near, chain, back_first, back_second, home_a, home_b, edge_copy]
    for copy in across + copies + z_copies + y_copies:
        copy.wait_send()

    @pl.when(y == 3)
    def _():
        over_second.wait_send()

    @pl.when(y == 0)
    def _():
        over_home.wait_send()


def shards(queries, key_rows, value_rows, cotangent, out_weight, segment_units, left_segments):
    tm_count = lax.axis_size("tm")
    head_count = lax.axis_size("head")
    anywhere = pl.BlockSpec(memory_space=pl.ANY)
    vmem = pl.BlockSpec(memory_space=pltpu.VMEM)
    dma = pltpu.SemaphoreType.DMA
    out_t = jax.ShapeDtypeStruct((WIDTH, BLK), BF16)
    both = 2 * WIDTH
    blocks = BACK + 1
    query_t, key_t, value_t, weight_t = pl.pallas_call(
        functools.partial(kernel, tm_count, head_count),
        out_shape=(out_t, out_t, out_t, jax.ShapeDtypeStruct((40, WIDTH), F32)),
        in_specs=[vmem] * 2 + [anywhere] * 5,
        out_specs=(vmem, vmem, vmem, vmem),
        scratch_shapes=[
            pltpu.VMEM((blocks, both, BLK), BF16),
            pltpu.VMEM((WIDTH, BLK), BF16),
            pltpu.VMEM((WIDTH, BLK), BF16),
            pltpu.VMEM((blocks, BLK, both), BF16),
            pltpu.VMEM((blocks, HEADS, BLK, BLK), BF16),
            pltpu.VMEM((head_count * WIDTH, BLK), BF16),
            pltpu.VMEM((WIDTH, head_count * WIDTH), BF16),
            pltpu.VMEM((WIDTH, BLK), BF16),
            pltpu.VMEM((HEADS, 256, BLK), BF16),
            pltpu.VMEM((HEADS, 128, BLK), BF16),
            pltpu.VMEM((HEADS, 2 * BLK, 128), BF16),
            pltpu.VMEM((2, BLK, WIDE), F32),
            pltpu.VMEM((HEADS, BLK, 2 * BLK), BF16),
            pltpu.VMEM((WIDTH, BLK), F32),
            pltpu.VMEM((WIDTH, BLK), F32),
            pltpu.VMEM((blocks, HEADS, 8, BLK), F32),
            pltpu.VMEM((HEADS, 8, BLK), F32),
            pltpu.VMEM((HEADS, 8, BLK), F32),
            pltpu.VMEM((HEADS, 8, BLK), F32),
            pltpu.VMEM((blocks, BLK, both), BF16),
            pltpu.VMEM((2, BLK, both), BF16),
            pltpu.VMEM((2, BLK, both), BF16),
            pltpu.VMEM((BLK, both), BF16),
            pltpu.VMEM((HALF, both), BF16),
            pltpu.VMEM((HALF, both), BF16),
            pltpu.VMEM((HALF, both), BF16),
            pltpu.VMEM((HALF, both), BF16),
            pltpu.VMEM((BLK, both), BF16),
            pltpu.VMEM((4, WIDTH, WIDTH), BF16),
            pltpu.VMEM((3, WIDTH, WIDTH), BF16),
            pltpu.VMEM((WIDTH, WIDTH), F32),
            pltpu.VMEM((7, 40, WIDTH), F32),
            dma((5,)),
            dma((12,)),
            dma((blocks,)),
            dma((blocks,)),
            dma((2,)),
            dma((3,)),
            dma((3,)),
            dma((9,)),
            dma((9,)),
            dma((3,)),
            dma((3,)),
            dma((7,)),
            dma((7,)),
        ],
        compiler_params=pltpu.CompilerParams(
            collective_id=0, has_side_effects=True, vmem_limit_bytes=60 << 20
        ),
    )(
        segment_units.reshape(1, -1),
        left_segments.reshape(1, -1),
        queries.T,
        key_rows.T,
        value_rows.T,
        cotangent.T,
        out_weight,
    )
    return (query_t.T, key_t.T, value_t.T, weight_t.T)


def solution(mesh):
    placed = (
        P("tm", "head"),
        P("tm", "head"),
        P("tm", "head"),
        P("tm", "head"),
        P("head", None),
        P(),
        P(),
    )
    return jax.shard_map(
        shards,
        mesh=mesh,
        in_specs=placed,
        out_specs=(P("tm", "head"), P("tm", "head"), P("tm", "head"), P("head", "tm")),
        check_vma=False,
    )
```

```python
import functools

import jax
import jax.numpy as jnp
from jax import lax
from jax.experimental import pallas as pl
from jax.experimental.pallas import tpu as pltpu
from jax.sharding import PartitionSpec as P

HS = 64
UNIT = 16
BLK = 512
HEADS = 5
WIDTH = HEADS * HS
BACK = 5
HALF = BLK // 2
STRIP = 128
WIDE = 256
HIDDEN = -2e30
LOWEST = -1e30
F32 = jnp.float32
BF16 = jnp.bfloat16
MESH = pl.DeviceIdType.MESH


def kernel(
    tm_count,
    head_count,
    units_ref,
    left_ref,
    q_hbm,
    k_hbm,
    v_hbm,
    cot_hbm,
    w_hbm,
    dq_ref,
    dk_ref,
    dv_ref,
    dw_ref,
    slots,
    relay,
    cross,
    kv_all,
    probs,
    cot_all,
    w_ref,
    q_ref,
    rhs,
    gt,
    rows,
    square,
    work,
    out_t,
    dq_t,
    m_all,
    m_run,
    l_run,
    delta,
    dkv,
    from_mate,
    sums,
    home_near,
    home_far,
    chain_in,
    relay_back,
    cross_back,
    edge,
    wt,
    z_in,
    z_sum,
    y_in,
    local,
    sent,
    got_k,
    got_v,
    got_relay,
    side_sent,
    side_got,
    back_sent,
    back_got,
    mate_sent,
    mate_got,
    z_sent,
    z_got,
    y_sent,
    y_got,
):
    t = lax.axis_index("tm")
    x = lax.axis_index("head")
    core = t % 2
    z = t // 8
    y = (t // 2) % 4
    low = t % 8
    sides = range(1, head_count)

    def at(place):
        return {"tm": (place + tm_count) % tm_count}

    def chip(z_place, y_place):
        return (((z_place + 4) % 4) * 4 + y_place % 4) * 2 + core

    mate = at(t + 1 - 2 * core)
    before, after = chip(z, y + 3), chip(z, y + 1)
    inner = jnp.where((y == 1) | (y == 2), 1, 0)
    relay_to = chip(z + jnp.where(y >= 2, 1, 0), y + 3)
    relay_from = chip(z - inner, y + 1)
    back_to = chip(z - jnp.where(y < 2, 1, 0), y + 1)
    back_from = chip(z + inner, y + 3)

    greeted = [at(t - 2), at(t + 2), at(relay_from), at(back_from)]
    greeted += [{"head": (x + head_count - i) % head_count} for i in sides]
    greeted += [at(t - 8 * i) for i in range(1, 4)]
    greeted += [at(8 * z + (low + 8 - i) % 8) for i in range(1, 8)]
    barrier = pltpu.get_barrier_semaphore()
    for target in greeted:
        pl.semaphore_signal(barrier, inc=1, device_id=target, device_id_type=MESH)
    edge_source = at(t + 5 * (2 * core - 1))
    pl.semaphore_signal(barrier, inc=1, device_id=edge_source, device_id_type=MESH)

    loads = [
        pltpu.make_async_copy(k_hbm, slots.at[0, 0:WIDTH], local.at[0]),
        pltpu.make_async_copy(v_hbm, slots.at[0, WIDTH : 2 * WIDTH], local.at[1]),
        pltpu.make_async_copy(q_hbm, q_ref, local.at[2]),
        pltpu.make_async_copy(
            cot_hbm, cot_all.at[pl.ds(pl.multiple_of(WIDTH * x, 64), WIDTH)], local.at[3]
        ),
        pltpu.make_async_copy(w_hbm, w_ref, local.at[4]),
    ]
    for load in loads:
        load.start()
    pl.semaphore_wait(barrier, len(greeted) + 1)

    def push(src, dst, send_sem, recv_sem, target):
        return pltpu.make_async_remote_copy(
            src_ref=src,
            dst_ref=dst,
            send_sem=send_sem,
            recv_sem=recv_sem,
            device_id=target,
            device_id_type=MESH,
        )

    def keys(src, slot, number, target):
        return push(src, slots.at[slot, 0:WIDTH], sent.at[number], got_k.at[slot], target)

    def values(src, slot, number, target):
        return push(
            src, slots.at[slot, WIDTH : 2 * WIDTH], sent.at[number], got_v.at[slot], target
        )

    def key_part(slot):
        return slots.at[slot, 0:WIDTH]

    def value_part(slot):
        return slots.at[slot, WIDTH : 2 * WIDTH]

    near_k = keys(k_hbm, 2, 0, at(t + 2))
    near_v = values(v_hbm, 2, 1, at(t + 2))
    over_first = push(v_hbm, cross, sent.at[1], got_relay.at[1], at(t + 8))
    over_second = values(cross, 2, 11, at(t - 6))
    relay_first = push(v_hbm, relay, sent.at[2], got_relay.at[0], at(relay_to))
    near_k.start()
    relay_first.start()
    across = [
        push(
            cot_hbm,
            cot_all.at[pl.ds(pl.multiple_of(WIDTH * x, 64), WIDTH)],
            side_sent.at[i - 1],
            side_got.at[i - 1],
            {"head": (x + i) % head_count},
        )
        for i in sides
    ]
    for copy in across:
        copy.start()

    @pl.when(y < 3)
    def _():
        near_v.start()

    @pl.when(y == 3)
    def _():
        over_first.start()

    direct_slot = 1 + 4 * core
    direct_to = at(t + 1 + 4 * core)
    direct_k = keys(k_hbm, direct_slot, 3, direct_to)
    direct_v = values(v_hbm, direct_slot, 4, direct_to)

    @pl.when(core == 0)
    def _():
        direct_k.start()
        direct_v.start()

    chain_k = keys(key_part(2), 4, 5, at(t + 2))
    relay_second = values(relay, 4, 6, at(before))
    pass_near = 3 - 2 * core
    pass_far = 5 - 2 * core
    pass_near_k = keys(key_part(2), pass_near, 7, mate)
    pass_near_v = values(value_part(2), pass_near, 8, mate)
    pass_far_k = keys(key_part(4), pass_far, 9, mate)
    pass_far_v = values(value_part(4), pass_far, 10, mate)

    segments = units_ref.shape[1]
    units = jnp.broadcast_to(units_ref[...].astype(F32), (8, segments)).astype(BF16)
    lefts = jnp.broadcast_to(left_ref[...].astype(F32), (8, segments)).astype(BF16)
    down = lax.broadcasted_iota(jnp.int32, (segments, 128), 0)
    over = lax.broadcasted_iota(jnp.int32, (segments, 128), 1)
    until = jnp.where(down <= over, 1.0, 0.0).astype(BF16)
    ahead = jnp.where(down < over, 1.0, 0.0).astype(BF16)
    same = jnp.where(down == over, 1.0, 0.0).astype(BF16)
    end_row = jnp.dot(units, until, preferred_element_type=F32)[0:1, :] * UNIT
    start_row = jnp.dot(units, ahead, preferred_element_type=F32)[0:1, :] * UNIT
    columns = (((0,), (1,)), ((), ()))
    end_col = lax.dot_general(until, units, columns, preferred_element_type=F32)[:, 0:1] * UNIT
    left_col = lax.dot_general(same, lefts, columns, preferred_element_type=F32)[:, 0:1]
    frame_row = (t * BLK + lax.broadcasted_iota(jnp.int32, (1, BLK), 1)).astype(F32)
    own_seg = jnp.sum(jnp.where(end_col <= frame_row, 1.0, 0.0), axis=0, keepdims=True)
    seg_down = lax.broadcasted_iota(jnp.int32, (128, BLK), 0).astype(F32)
    reach = jnp.sum(jnp.where(seg_down == own_seg, left_col, 0.0), axis=0, keepdims=True)
    lowest = jnp.maximum(own_seg - reach, 0.0)
    bias = jnp.where((seg_down >= lowest) & (seg_down <= own_seg), 0.0, HIDDEN).astype(BF16)

    blank = jnp.zeros((HS, BLK), BF16)
    lane = lax.broadcasted_iota(jnp.int32, (BLK, 128), 1)

    def spread(j, upright, transposed):
        g, half = divmod(j, 2)
        both = [transposed, blank] if half == 0 else [blank, transposed]
        if j < HEADS:
            rhs[j] = jnp.concatenate(both + [bias], axis=0)
        else:
            gt[j - HEADS] = jnp.concatenate(both, axis=0)
        zeros = jnp.zeros((BLK, HS), BF16)
        pair = [upright, zeros] if half == 0 else [zeros, upright]
        rows[g, BLK * half : BLK * (half + 1), :] = jnp.concatenate(pair, axis=1)

    loads[2].wait()
    queries_t = (q_ref[...].astype(F32) * HS**-0.5).astype(BF16)
    for j in range(HEADS):
        mine = queries_t[HS * j : HS * (j + 1), :]
        spread(j, mine.T, mine)
    m_run[...] = jnp.full(m_run.shape, LOWEST, F32)
    l_run[...] = jnp.zeros(l_run.shape, F32)
    out_t[...] = jnp.zeros(out_t.shape, F32)
    dq_t[...] = jnp.zeros(dq_t.shape, F32)
    loads[0].wait()
    loads[1].wait()

    def wait_slot(slot):
        keys(k_hbm, slot, 0, mate).wait_recv()
        values(v_hbm, slot, 1, mate).wait_recv()

    def near_event():
        relay_first.wait_recv()
        relay_second.start()

        near_k.wait_recv()
        chain_k.start()
        pass_near_k.start()
        near_v.wait_recv()
        pass_near_v.start()

    def forward(step, carry):
        @pl.when((step == 1) & (core == 1))
        def _():
            direct_k.start()
            direct_v.start()

        @pl.when((step == 1) & (y == 3))
        def _():
            over_first.wait_recv()
            over_second.start()

        @pl.when(step == 1)
        def _():
            loads[3].wait()
            loads[4].wait()
            for copy in across:
                copy.wait_recv()
            grad_t = jnp.dot(w_ref[...], cot_all[...], preferred_element_type=F32).astype(BF16)
            for j in range(HEADS):
                mine = grad_t[HS * j : HS * (j + 1), :]
                spread(j + HEADS, mine.T, mine)

        swapped = jnp.where(step == 0, 0, jnp.where(step < 3, 3 - step, 8 - step))
        slot = jnp.where(core == 0, swapped, step)

        @pl.when(step == 1 + core)
        def _():
            near_event()

        @pl.when((step == 2 - core) | (step == 3) | (step == 5))
        def _():
            wait_slot(slot)

        @pl.when(step == 4)
        def _():
            keys(k_hbm, 4, 0, mate).wait_recv()
            pass_far_k.start()
            values(v_hbm, 4, 1, mate).wait_recv()
            pass_far_v.start()

        def upright(g):
            group = slice(128 * g, 128 * (g + 1))
            turned = slots[slot, group, :].T
            kv_all[2 * slot, :, group] = turned[0:HALF]
            kv_all[2 * slot + 1, :, group] = turned[HALF:BLK]

        first = ((t + tm_count - slot) % tm_count) * BLK
        frames = (first + lax.broadcasted_iota(jnp.int32, (BLK, 128), 0)).astype(F32)
        hot = jnp.where((frames >= start_row) & (frames < end_row), 1.0, 0.0).astype(BF16)
        upright(0)
        pieces = BLK // WIDE
        units_of = HEADS * pieces
        top = None
        for turn in range(units_of + 1):
            last = top
            if turn < units_of:
                h, c = divmod(turn, pieces)
                cols = slice(WIDE * c, WIDE * (c + 1))
                g = h // 2
                group = slice(128 * g, 128 * (g + 1))
                keys_here = [kv_all[2 * slot, :, group], kv_all[2 * slot + 1, :, group]]
                lhs = jnp.concatenate([jnp.concatenate(keys_here, axis=0), hot], axis=1)
                scores = jnp.dot(lhs, rhs[h, :, cols], preferred_element_type=F32)
                square[turn % 2] = scores
                top = jnp.max(scores.reshape(BLK // 8, 8, WIDE), axis=0)
                if turn < HEADS - 1:
                    upright(turn + 1)
            if turn == 0:
                continue
            h, c = divmod(turn - 1, pieces)
            cols = slice(WIDE * c, WIDE * (c + 1))
            m_old = m_run[h, 0:1, cols]
            m_new = jnp.maximum(m_old, jnp.max(last, axis=0, keepdims=True))
            factor = jnp.exp(m_old - m_new)
            m_run[h, 0:1, cols] = m_new
            m_all[slot, h, 0:1, cols] = m_new
            total = l_run[h, :, cols] * factor
            for r in range(0, BLK, STRIP):
                p = jnp.exp(square[(turn - 1) % 2, r : r + STRIP, :] - m_new)
                total = total + jnp.sum(p.reshape(STRIP // 8, 8, WIDE), axis=0)
                half, row = divmod(r, HALF)
                probs[2 * slot + half, h, row : row + STRIP, cols] = p.astype(BF16)
            l_run[h, :, cols] = total
            here = slice(HS * h, HS * (h + 1))
            added = out_t[here, cols] * factor
            for half in range(2):
                added += jnp.dot(
                    slots[slot, WIDTH + HS * h : WIDTH + HS * (h + 1), half * HALF : (half + 1) * HALF],
                    probs[2 * slot + half, h, :, cols],
                    preferred_element_type=F32,
                )
            out_t[here, cols] = added
        return carry

    lax.fori_loop(0, BACK + 1, forward, 0)

    for h in range(HEADS):
        here = slice(HS * h, HS * (h + 1))
        total = jnp.sum(l_run[h], axis=0, keepdims=True)
        out = out_t[here, :] / total
        out_t[here, :] = out
        side = HS * ((h + HEADS) % 2)
        own_grad = gt[h, side : side + HS, :].astype(F32)
        delta[h, 0:1, :] = jnp.sum(out * own_grad, axis=0, keepdims=True)
        l_run[h, 0:1, :] = m_run[h, 0:1, :] + jnp.log(total)

    z_copies = [
        push(
            wt.at[(z + i) % 4], z_in.at[i - 1], z_sent.at[i - 1], z_got.at[i - 1], at(t + 8 * i)
        )
        for i in range(1, 4)
    ]
    y_copies = [
        push(
            z_sum.at[pl.ds(pl.multiple_of(40 * ((low + i) % 8), 8), 40)],
            y_in.at[i - 1],
            y_sent.at[i - 1],
            y_got.at[i - 1],
            at(8 * z + (low + i) % 8),
        )
        for i in range(1, 8)
    ]

    def piece(slot, half):
        return dkv.at[2 * slot + half]

    def to_mate(pair, half):
        number = 2 * pair + half
        return push(
            piece(3 + 2 * core - 2 * pair, half),
            from_mate.at[number],
            mate_sent.at[number],
            mate_got.at[number],
            mate,
        )

    mated = [[to_mate(pair, half) for half in range(2)] for pair in range(2)]
    chain = push(sums.at[0], chain_in, back_sent.at[0], back_got.at[0], at(t - 2))
    back_first = push(sums.at[1], relay_back, back_sent.at[1], back_got.at[1], at(back_to))
    back_second = push(relay_back, home_far, back_sent.at[2], back_got.at[2], at(after))
    home_a = push(sums.at[2], home_near.at[0], back_sent.at[3], back_got.at[3], at(t - 2))
    home_b = push(sums.at[3], home_near.at[1], back_sent.at[4], back_got.at[4], at(t - 2))
    over_back = push(sums.at[3], cross_back, back_sent.at[4], back_got.at[5], at(t - 8))
    over_home = push(cross_back, home_near.at[1], back_sent.at[5], back_got.at[4], at(t + 6))
    edge_copies = [
        push(
            piece(5 - 4 * core, half),
            edge.at[half],
            back_sent.at[6 + half],
            back_got.at[6 + half],
            at(t - 5 + 4 * core),
        )
        for half in range(2)
    ]

    def backward(step, carry):
        pair, within = step // 4, step % 4
        paired = jnp.where(within % 2 == 0, 3 + 2 * core, 4) - 2 * pair
        slot = jnp.where(step < 8, paired, jnp.where(step < 10, 5 - 4 * core, 0))
        half = jnp.where(step < 8, within // 2, step % 2)
        here = 2 * slot + half
        pieces = BLK // WIDE
        units_of = HEADS * pieces
        for turn in range(units_of + 1):
            if turn < units_of:
                h, c = divmod(turn, pieces)
                g = (h + HEADS) // 2
                square[turn % 2, 0:HALF] = jnp.dot(
                    kv_all[here, :, 128 * g : 128 * (g + 1)],
                    gt[h, :, WIDE * c : WIDE * (c + 1)],
                    preferred_element_type=F32,
                )
            if turn == 0:
                continue
            h, c = divmod(turn - 1, pieces)
            cols = slice(WIDE * c, WIDE * (c + 1))
            scale = jnp.exp(m_all[slot, h, 0:1, cols] - l_run[h, 0:1, cols])
            shift = delta[h, 0:1, cols]
            ds_at = BLK * (h % 2) + WIDE * c
            p_at = BLK * ((h + HEADS) % 2) + WIDE * c
            for r in range(0, HALF, STRIP):
                down = slice(r, r + STRIP)
                p = probs[here, h, down, cols].astype(F32) * scale
                ds = p * (square[(turn - 1) % 2, down, :] - shift)
                work[h // 2, down, ds_at : ds_at + WIDE] = ds.astype(BF16)
                work[(h + HEADS) // 2, down, p_at : p_at + WIDE] = p.astype(BF16)
            mine = slice(HS * h, HS * (h + 1))
            dq_t[mine, cols] += jnp.dot(
                slots[slot, mine, pl.ds(pl.multiple_of(HALF * half, HALF), HALF)],
                work[h // 2, :, ds_at : ds_at + WIDE],
                preferred_element_type=F32,
            )
            if c < pieces - 1:
                continue
            for g in ((), (0,), (3,), (1,), (2, 4))[h]:
                dkv[here, :, 128 * g : 128 * (g + 1)] = jnp.dot(
                    work[g], rows[g], preferred_element_type=F32
                ).astype(BF16)

        for j in range(2):
            for k in range(2):

                @pl.when(step == 4 * j + 2 * k)
                def _(j=j, k=k):
                    mated[j][k].start()

        def summed(pair, half):
            mated[pair][half].wait_recv()
            kept = dkv[2 * (4 - 2 * pair) + half].astype(F32)
            return kept + from_mate[2 * pair + half].astype(F32)

        @pl.when(step == 1)
        def _():
            sums[0] = summed(0, 0).astype(BF16)
            chain.start()

        @pl.when(step == 3)
        def _():
            sums[1] = summed(0, 1).astype(BF16)
            back_first.start()
            attn = out_t[...].T.astype(BF16)
            for part in range(4):
                some = slice(WIDTH * part, WIDTH * (part + 1))
                term = jnp.dot(cot_all[some, :], attn, preferred_element_type=F32)
                wt[part] = term.astype(BF16)
            for copy in z_copies:
                copy.start()

        @pl.when(step == 5)
        def _():
            both = summed(1, 0)
            chain.wait_recv()
            sums[2] = (both + chain_in[...].astype(F32)).astype(BF16)
            home_a.start()

        @pl.when(step == 7)
        def _():
            sums[3] = summed(1, 1).astype(BF16)

            @pl.when(y > 0)
            def _():
                home_b.start()

            @pl.when(y == 0)
            def _():
                over_back.start()

            back_first.wait_recv()
            back_second.start()

        @pl.when(step == 8)
        def _():
            edge_copies[0].start()

        @pl.when(step == 9)
        def _():
            edge_copies[1].start()
            for copy in z_copies:
                copy.wait_recv()
            z_sum[...] = wt[z].astype(F32)
            for i in range(3):
                z_sum[...] += z_in[i].astype(F32)
            for copy in y_copies:
                copy.start()

        @pl.when((step == 9) & (y == 0))
        def _():
            over_back.wait_recv()
            over_home.start()

        return carry

    lax.fori_loop(0, 2 * (BACK + 1), backward, 0)

    dq_ref[...] = (dq_t[...] * HS**-0.5).astype(BF16)
    total = z_sum[pl.ds(pl.multiple_of(40 * low, 8), 40), :]
    for i, copy in enumerate(y_copies):
        copy.wait_recv()
        total = total + y_in[i]
    dw_ref[...] = total

    for copy in edge_copies + [home_a, home_b, back_second]:
        copy.wait_recv()
    for half in range(2):
        part = slice(HALF * half, HALF * (half + 1))
        total = dkv[half].astype(F32) + edge[half].astype(F32) + home_near[half].astype(F32)
        if half == 1:
            total = total + home_far[...].astype(F32)
        total_t = total.T.astype(BF16)
        dk_ref[:, part] = total_t[:WIDTH]
        dv_ref[:, part] = total_t[WIDTH:]

    copies = [near_k, near_v, relay_first, direct_k, direct_v, chain_k, relay_second]
    copies += [pass_near_k, pass_near_v, pass_far_k, pass_far_v]
    copies += mated[0] + mated[1] + edge_copies
    copies += [chain, back_first, back_second, home_a, home_b]
    for copy in across + copies + z_copies + y_copies:
        copy.wait_send()

    @pl.when(y == 3)
    def _():
        over_second.wait_send()

    @pl.when(y == 0)
    def _():
        over_home.wait_send()


def shards(queries, key_rows, value_rows, cotangent, out_weight, segment_units, left_segments):
    tm_count = lax.axis_size("tm")
    head_count = lax.axis_size("head")
    anywhere = pl.BlockSpec(memory_space=pl.ANY)
    vmem = pl.BlockSpec(memory_space=pltpu.VMEM)
    dma = pltpu.SemaphoreType.DMA
    out_t = jax.ShapeDtypeStruct((WIDTH, BLK), BF16)
    both = 2 * WIDTH
    blocks = BACK + 1
    query_t, key_t, value_t, weight_t = pl.pallas_call(
        functools.partial(kernel, tm_count, head_count),
        out_shape=(out_t, out_t, out_t, jax.ShapeDtypeStruct((40, WIDTH), F32)),
        in_specs=[vmem] * 2 + [anywhere] * 5,
        out_specs=(vmem, vmem, vmem, vmem),
        scratch_shapes=[
            pltpu.VMEM((blocks, both, BLK), BF16),
            pltpu.VMEM((WIDTH, BLK), BF16),
            pltpu.VMEM((WIDTH, BLK), BF16),
            pltpu.VMEM((2 * blocks, HALF, both), BF16),
            pltpu.VMEM((2 * blocks, HEADS, HALF, BLK), BF16),
            pltpu.VMEM((head_count * WIDTH, BLK), BF16),
            pltpu.VMEM((WIDTH, head_count * WIDTH), BF16),
            pltpu.VMEM((WIDTH, BLK), BF16),
            pltpu.VMEM((HEADS, 256, BLK), BF16),
            pltpu.VMEM((HEADS, 128, BLK), BF16),
            pltpu.VMEM((HEADS, 2 * BLK, 128), BF16),
            pltpu.VMEM((2, BLK, WIDE), F32),
            pltpu.VMEM((HEADS, HALF, 2 * BLK), BF16),
            pltpu.VMEM((WIDTH, BLK), F32),
            pltpu.VMEM((WIDTH, BLK), F32),
            pltpu.VMEM((blocks, HEADS, 8, BLK), F32),
            pltpu.VMEM((HEADS, 8, BLK), F32),
            pltpu.VMEM((HEADS, 8, BLK), F32),
            pltpu.VMEM((HEADS, 8, BLK), F32),
            pltpu.VMEM((2 * blocks, HALF, both), BF16),
            pltpu.VMEM((4, HALF, both), BF16),
            pltpu.VMEM((4, HALF, both), BF16),
            pltpu.VMEM((2, HALF, both), BF16),
            pltpu.VMEM((HALF, both), BF16),
            pltpu.VMEM((HALF, both), BF16),
            pltpu.VMEM((HALF, both), BF16),
            pltpu.VMEM((HALF, both), BF16),
            pltpu.VMEM((2, HALF, both), BF16),
            pltpu.VMEM((4, WIDTH, WIDTH), BF16),
            pltpu.VMEM((3, WIDTH, WIDTH), BF16),
            pltpu.VMEM((WIDTH, WIDTH), F32),
            pltpu.VMEM((7, 40, WIDTH), F32),
            dma((5,)),
            dma((12,)),
            dma((blocks,)),
            dma((blocks,)),
            dma((2,)),
            dma((3,)),
            dma((3,)),
            dma((8,)),
            dma((8,)),
            dma((4,)),
            dma((4,)),
            dma((3,)),
            dma((3,)),
            dma((7,)),
            dma((7,)),
        ],
        compiler_params=pltpu.CompilerParams(
            collective_id=0, has_side_effects=True, vmem_limit_bytes=60 << 20
        ),
    )(
        segment_units.reshape(1, -1),
        left_segments.reshape(1, -1),
        queries.T,
        key_rows.T,
        value_rows.T,
        cotangent.T,
        out_weight,
    )
    return (query_t.T, key_t.T, value_t.T, weight_t.T)


def solution(mesh):
    placed = (
        P("tm", "head"),
        P("tm", "head"),
        P("tm", "head"),
        P("tm", "head"),
        P("head", None),
        P(),
        P(),
    )
    return jax.shard_map(
        shards,
        mesh=mesh,
        in_specs=placed,
        out_specs=(P("tm", "head"), P("tm", "head"), P("tm", "head"), P("head", "tm")),
        check_vma=False,
    )
```

```python
import functools

import jax
import jax.numpy as jnp
from jax import lax
from jax.experimental import pallas as pl
from jax.experimental.pallas import tpu as pltpu
from jax.sharding import PartitionSpec as P

HS = 64
UNIT = 16
BLK = 512
HEADS = 5
WIDTH = HEADS * HS
BACK = 5
HALF = BLK // 2
WEIGHT_WIDTH = 384
STRIP = 128
WIDE = 256
HIDDEN = -2e30
LOWEST = -1e30
F32 = jnp.float32
BF16 = jnp.bfloat16
MESH = pl.DeviceIdType.MESH


def kernel(
    tm_count,
    head_count,
    units_ref,
    left_ref,
    q_hbm,
    k_hbm,
    v_hbm,
    cot_hbm,
    w_hbm,
    dq_ref,
    dk_ref,
    dv_ref,
    dw_ref,
    slots,
    relay,
    cross,
    kv_all,
    probs,
    cot_all,
    w_ref,
    q_ref,
    rhs,
    gt,
    rows,
    square,
    work,
    out_t,
    dq_t,
    m_all,
    m_run,
    l_run,
    delta,
    dkv,
    from_mate,
    sums,
    home_near,
    home_far,
    chain_in,
    relay_back,
    cross_back,
    edge,
    wt,
    z_in,
    z_sum,
    y_in,
    local,
    sent,
    got_k,
    got_v,
    got_relay,
    side_sent,
    side_got,
    back_sent,
    back_got,
    mate_sent,
    mate_got,
    z_sent,
    z_got,
    y_sent,
    y_got,
):
    t = lax.axis_index("tm")
    x = lax.axis_index("head")
    core = t % 2
    z = t // 8
    y = (t // 2) % 4
    low = t % 8
    sides = range(1, head_count)

    def at(place):
        return {"tm": (place + tm_count) % tm_count}

    def chip(z_place, y_place):
        return (((z_place + 4) % 4) * 4 + y_place % 4) * 2 + core

    mate = at(t + 1 - 2 * core)
    before, after = chip(z, y + 3), chip(z, y + 1)
    inner = jnp.where((y == 1) | (y == 2), 1, 0)
    relay_to = chip(z + jnp.where(y >= 2, 1, 0), y + 3)
    relay_from = chip(z - inner, y + 1)
    back_to = chip(z - jnp.where(y < 2, 1, 0), y + 1)
    back_from = chip(z + inner, y + 3)

    greeted = [at(t - 2), at(t + 2), at(relay_from), at(back_from)]
    greeted += [{"head": (x + head_count - i) % head_count} for i in sides]
    greeted += [at(t - 8 * i) for i in range(1, 4)]
    greeted += [at(8 * z + (low + 8 - i) % 8) for i in range(1, 8)]
    barrier = pltpu.get_barrier_semaphore()
    for target in greeted:
        pl.semaphore_signal(barrier, inc=1, device_id=target, device_id_type=MESH)
    edge_source = at(t + 5 * (2 * core - 1))
    pl.semaphore_signal(barrier, inc=1, device_id=edge_source, device_id_type=MESH)

    loads = [
        pltpu.make_async_copy(k_hbm, slots.at[0, 0:WIDTH], local.at[0]),
        pltpu.make_async_copy(v_hbm, slots.at[0, WIDTH : 2 * WIDTH], local.at[1]),
        pltpu.make_async_copy(q_hbm, q_ref, local.at[2]),
        pltpu.make_async_copy(
            cot_hbm, cot_all.at[pl.ds(pl.multiple_of(WIDTH * x, 64), WIDTH)], local.at[3]
        ),
        pltpu.make_async_copy(w_hbm, w_ref, local.at[4]),
    ]
    for load in loads:
        load.start()
    pl.semaphore_wait(barrier, len(greeted) + 1)

    def push(src, dst, send_sem, recv_sem, target):
        return pltpu.make_async_remote_copy(
            src_ref=src,
            dst_ref=dst,
            send_sem=send_sem,
            recv_sem=recv_sem,
            device_id=target,
            device_id_type=MESH,
        )

    def keys(src, slot, number, target):
        return push(src, slots.at[slot, 0:WIDTH], sent.at[number], got_k.at[slot], target)

    def values(src, slot, number, target):
        return push(
            src, slots.at[slot, WIDTH : 2 * WIDTH], sent.at[number], got_v.at[slot], target
        )

    def key_part(slot):
        return slots.at[slot, 0:WIDTH]

    def value_part(slot):
        return slots.at[slot, WIDTH : 2 * WIDTH]

    near_k = keys(k_hbm, 2, 0, at(t + 2))
    near_v = values(v_hbm, 2, 1, at(t + 2))
    over_first = push(v_hbm, cross, sent.at[1], got_relay.at[1], at(t + 8))
    over_second = values(cross, 2, 11, at(t - 6))
    relay_first = push(v_hbm, relay, sent.at[2], got_relay.at[0], at(relay_to))
    near_k.start()
    relay_first.start()
    across = [
        push(
            cot_hbm,
            cot_all.at[pl.ds(pl.multiple_of(WIDTH * x, 64), WIDTH)],
            side_sent.at[i - 1],
            side_got.at[i - 1],
            {"head": (x + i) % head_count},
        )
        for i in sides
    ]
    for copy in across:
        copy.start()

    @pl.when(y < 3)
    def _():
        near_v.start()

    @pl.when(y == 3)
    def _():
        over_first.start()

    direct_slot = 1 + 4 * core
    direct_to = at(t + 1 + 4 * core)
    direct_k = keys(k_hbm, direct_slot, 3, direct_to)
    direct_v = values(v_hbm, direct_slot, 4, direct_to)

    @pl.when(core == 0)
    def _():
        direct_k.start()
        direct_v.start()

    chain_k = keys(key_part(2), 4, 5, at(t + 2))
    relay_second = values(relay, 4, 6, at(before))
    pass_near = 3 - 2 * core
    pass_far = 5 - 2 * core
    pass_near_k = keys(key_part(2), pass_near, 7, mate)
    pass_near_v = values(value_part(2), pass_near, 8, mate)
    pass_far_k = keys(key_part(4), pass_far, 9, mate)
    pass_far_v = values(value_part(4), pass_far, 10, mate)

    segments = units_ref.shape[1]
    units = jnp.broadcast_to(units_ref[...].astype(F32), (8, segments)).astype(BF16)
    lefts = jnp.broadcast_to(left_ref[...].astype(F32), (8, segments)).astype(BF16)
    down = lax.broadcasted_iota(jnp.int32, (segments, 128), 0)
    over = lax.broadcasted_iota(jnp.int32, (segments, 128), 1)
    until = jnp.where(down <= over, 1.0, 0.0).astype(BF16)
    ahead = jnp.where(down < over, 1.0, 0.0).astype(BF16)
    same = jnp.where(down == over, 1.0, 0.0).astype(BF16)
    end_row = jnp.dot(units, until, preferred_element_type=F32)[0:1, :] * UNIT
    start_row = jnp.dot(units, ahead, preferred_element_type=F32)[0:1, :] * UNIT
    columns = (((0,), (1,)), ((), ()))
    end_col = lax.dot_general(until, units, columns, preferred_element_type=F32)[:, 0:1] * UNIT
    left_col = lax.dot_general(same, lefts, columns, preferred_element_type=F32)[:, 0:1]
    frame_row = (t * BLK + lax.broadcasted_iota(jnp.int32, (1, BLK), 1)).astype(F32)
    own_seg = jnp.sum(jnp.where(end_col <= frame_row, 1.0, 0.0), axis=0, keepdims=True)
    seg_down = lax.broadcasted_iota(jnp.int32, (128, BLK), 0).astype(F32)
    reach = jnp.sum(jnp.where(seg_down == own_seg, left_col, 0.0), axis=0, keepdims=True)
    lowest = jnp.maximum(own_seg - reach, 0.0)
    bias = jnp.where((seg_down >= lowest) & (seg_down <= own_seg), 0.0, HIDDEN).astype(BF16)

    blank = jnp.zeros((HS, BLK), BF16)
    lane = lax.broadcasted_iota(jnp.int32, (BLK, 128), 1)

    def spread(j, upright, transposed):
        g, half = divmod(j, 2)
        both = [transposed, blank] if half == 0 else [blank, transposed]
        if j < HEADS:
            rhs[j] = jnp.concatenate(both + [bias], axis=0)
        else:
            gt[j - HEADS] = jnp.concatenate(both, axis=0)
        zeros = jnp.zeros((BLK, HS), BF16)
        pair = [upright, zeros] if half == 0 else [zeros, upright]
        rows[g, BLK * half : BLK * (half + 1), :] = jnp.concatenate(pair, axis=1)

    loads[2].wait()
    queries_t = (q_ref[...].astype(F32) * HS**-0.5).astype(BF16)
    for j in range(HEADS):
        mine = queries_t[HS * j : HS * (j + 1), :]
        spread(j, mine.T, mine)
    m_run[...] = jnp.full(m_run.shape, LOWEST, F32)
    l_run[...] = jnp.zeros(l_run.shape, F32)
    out_t[...] = jnp.zeros(out_t.shape, F32)
    dq_t[...] = jnp.zeros(dq_t.shape, F32)
    loads[0].wait()
    loads[1].wait()

    def wait_slot(slot):
        keys(k_hbm, slot, 0, mate).wait_recv()
        values(v_hbm, slot, 1, mate).wait_recv()

    def near_event():
        relay_first.wait_recv()
        relay_second.start()

        near_k.wait_recv()
        chain_k.start()
        pass_near_k.start()
        near_v.wait_recv()
        pass_near_v.start()

    def forward(step, carry):
        @pl.when((step == 1) & (core == 1))
        def _():
            direct_k.start()
            direct_v.start()

        @pl.when((step == 1) & (y == 3))
        def _():
            over_first.wait_recv()
            over_second.start()

        @pl.when(step == 1)
        def _():
            loads[3].wait()
            loads[4].wait()
            for copy in across:
                copy.wait_recv()
            grad_t = jnp.dot(w_ref[...], cot_all[...], preferred_element_type=F32).astype(BF16)
            for j in range(HEADS):
                mine = grad_t[HS * j : HS * (j + 1), :]
                spread(j + HEADS, mine.T, mine)

        swapped = jnp.where(step == 0, 0, jnp.where(step < 3, 3 - step, 8 - step))
        slot = jnp.where(core == 0, swapped, step)

        @pl.when(step == 1 + core)
        def _():
            near_event()

        @pl.when((step == 2 - core) | (step == 3) | (step == 5))
        def _():
            wait_slot(slot)

        @pl.when(step == 4)
        def _():
            keys(k_hbm, 4, 0, mate).wait_recv()
            pass_far_k.start()
            values(v_hbm, 4, 1, mate).wait_recv()
            pass_far_v.start()

        def upright(g):
            group = slice(128 * g, 128 * (g + 1))
            turned = slots[slot, group, :].T
            kv_all[2 * slot, :, group] = turned[0:HALF]
            kv_all[2 * slot + 1, :, group] = turned[HALF:BLK]

        first = ((t + tm_count - slot) % tm_count) * BLK
        frames = (first + lax.broadcasted_iota(jnp.int32, (BLK, 128), 0)).astype(F32)
        hot = jnp.where((frames >= start_row) & (frames < end_row), 1.0, 0.0).astype(BF16)
        upright(0)
        pieces = BLK // WIDE
        units_of = HEADS * pieces
        top = None
        for turn in range(units_of + 1):
            last = top
            if turn < units_of:
                h, c = divmod(turn, pieces)
                cols = slice(WIDE * c, WIDE * (c + 1))
                g = h // 2
                group = slice(128 * g, 128 * (g + 1))
                keys_here = [kv_all[2 * slot, :, group], kv_all[2 * slot + 1, :, group]]
                lhs = jnp.concatenate([jnp.concatenate(keys_here, axis=0), hot], axis=1)
                scores = jnp.dot(lhs, rhs[h, :, cols], preferred_element_type=F32)
                square[turn % 2] = scores
                top = jnp.max(scores.reshape(BLK // 8, 8, WIDE), axis=0)
                if turn < HEADS - 1:
                    upright(turn + 1)
            if turn == 0:
                continue
            h, c = divmod(turn - 1, pieces)
            cols = slice(WIDE * c, WIDE * (c + 1))
            m_old = m_run[h, 0:1, cols]
            m_new = jnp.maximum(m_old, jnp.max(last, axis=0, keepdims=True))
            factor = jnp.exp(m_old - m_new)
            m_run[h, 0:1, cols] = m_new
            m_all[slot, h, 0:1, cols] = m_new
            total = l_run[h, :, cols] * factor
            for r in range(0, BLK, STRIP):
                p = jnp.exp(square[(turn - 1) % 2, r : r + STRIP, :] - m_new)
                total = total + jnp.sum(p.reshape(STRIP // 8, 8, WIDE), axis=0)
                half, row = divmod(r, HALF)
                probs[2 * slot + half, h, row : row + STRIP, cols] = p.astype(BF16)
            l_run[h, :, cols] = total
            here = slice(HS * h, HS * (h + 1))
            added = out_t[here, cols] * factor
            for half in range(2):
                added += jnp.dot(
                    slots[slot, WIDTH + HS * h : WIDTH + HS * (h + 1), half * HALF : (half + 1) * HALF],
                    probs[2 * slot + half, h, :, cols],
                    preferred_element_type=F32,
                )
            out_t[here, cols] = added
        return carry

    lax.fori_loop(0, BACK + 1, forward, 0)

    for h in range(HEADS):
        here = slice(HS * h, HS * (h + 1))
        total = jnp.sum(l_run[h], axis=0, keepdims=True)
        out = out_t[here, :] / total
        out_t[here, :] = out
        side = HS * ((h + HEADS) % 2)
        own_grad = gt[h, side : side + HS, :].astype(F32)
        delta[h, 0:1, :] = jnp.sum(out * own_grad, axis=0, keepdims=True)
        l_run[h, 0:1, :] = m_run[h, 0:1, :] + jnp.log(total)

    z_copies = [
        push(
            wt.at[(z + i) % 4], z_in.at[i - 1], z_sent.at[i - 1], z_got.at[i - 1], at(t + 8 * i)
        )
        for i in range(1, 4)
    ]
    y_copies = [
        push(
            z_sum.at[pl.ds(pl.multiple_of(40 * ((low + i) % 8), 8), 40)],
            y_in.at[i - 1],
            y_sent.at[i - 1],
            y_got.at[i - 1],
            at(8 * z + (low + i) % 8),
        )
        for i in range(1, 8)
    ]

    def piece(slot, half):
        return dkv.at[2 * slot + half]

    def to_mate(pair, half):
        number = 2 * pair + half
        return push(
            piece(3 + 2 * core - 2 * pair, half),
            from_mate.at[number],
            mate_sent.at[number],
            mate_got.at[number],
            mate,
        )

    mated = [[to_mate(pair, half) for half in range(2)] for pair in range(2)]
    chain = push(sums.at[0], chain_in, back_sent.at[0], back_got.at[0], at(t - 2))
    back_first = push(sums.at[1], relay_back, back_sent.at[1], back_got.at[1], at(back_to))
    back_second = push(relay_back, home_far, back_sent.at[2], back_got.at[2], at(after))
    home_a = push(sums.at[2], home_near.at[0], back_sent.at[3], back_got.at[3], at(t - 2))
    home_b = push(sums.at[3], home_near.at[1], back_sent.at[4], back_got.at[4], at(t - 2))
    over_back = push(sums.at[3], cross_back, back_sent.at[4], back_got.at[5], at(t - 8))
    over_home = push(cross_back, home_near.at[1], back_sent.at[5], back_got.at[4], at(t + 6))
    edge_copies = [
        push(
            piece(5 - 4 * core, half),
            edge.at[half],
            back_sent.at[6 + half],
            back_got.at[6 + half],
            at(t - 5 + 4 * core),
        )
        for half in range(2)
    ]

    def backward(step, carry):
        pair, within = step // 4, step % 4
        paired = jnp.where(within % 2 == 0, 3 + 2 * core, 4) - 2 * pair
        slot = jnp.where(step < 8, paired, jnp.where(step < 10, 5 - 4 * core, 0))
        half = jnp.where(step < 8, within // 2, step % 2)
        here = 2 * slot + half
        pieces = BLK // WIDE
        units_of = HEADS * pieces
        for turn in range(units_of + 1):
            if turn < units_of:
                h, c = divmod(turn, pieces)
                g = (h + HEADS) // 2
                square[turn % 2, 0:HALF] = jnp.dot(
                    kv_all[here, :, 128 * g : 128 * (g + 1)],
                    gt[h, :, WIDE * c : WIDE * (c + 1)],
                    preferred_element_type=F32,
                )
            if turn == 0:
                continue
            h, c = divmod(turn - 1, pieces)
            cols = slice(WIDE * c, WIDE * (c + 1))
            scale = jnp.exp(m_all[slot, h, 0:1, cols] - l_run[h, 0:1, cols])
            shift = delta[h, 0:1, cols]
            ds_at = BLK * (h % 2) + WIDE * c
            p_at = BLK * ((h + HEADS) % 2) + WIDE * c
            for r in range(0, HALF, STRIP):
                down = slice(r, r + STRIP)
                p = probs[here, h, down, cols].astype(F32) * scale
                ds = p * (square[(turn - 1) % 2, down, :] - shift)
                work[h // 2, down, ds_at : ds_at + WIDE] = ds.astype(BF16)
                work[(h + HEADS) // 2, down, p_at : p_at + WIDE] = p.astype(BF16)
            mine = slice(HS * h, HS * (h + 1))
            dq_t[mine, cols] += jnp.dot(
                slots[slot, mine, pl.ds(pl.multiple_of(HALF * half, HALF), HALF)],
                work[h // 2, :, ds_at : ds_at + WIDE],
                preferred_element_type=F32,
            )
            if c < pieces - 1:
                continue
            for g in ((), (0,), (3,), (1,), (2, 4))[h]:
                dkv[here, :, 128 * g : 128 * (g + 1)] = jnp.dot(
                    work[g], rows[g], preferred_element_type=F32
                ).astype(BF16)

        for j in range(2):
            for k in range(2):

                @pl.when(step == 4 * j + 2 * k)
                def _(j=j, k=k):
                    mated[j][k].start()

        def summed(pair, half):
            mated[pair][half].wait_recv()
            kept = dkv[2 * (4 - 2 * pair) + half].astype(F32)
            return kept + from_mate[2 * pair + half].astype(F32)

        @pl.when(step == 1)
        def _():
            sums[0] = summed(0, 0).astype(BF16)
            chain.start()

        @pl.when(step == 3)
        def _():
            sums[1] = summed(0, 1).astype(BF16)
            back_first.start()
            attn = jnp.concatenate(
                [out_t[...].T.astype(BF16), jnp.zeros((BLK, WEIGHT_WIDTH - WIDTH), BF16)], axis=1
            )
            for part in range(4):
                some = slice(WIDTH * part, WIDTH * (part + 1))
                term = jnp.dot(cot_all[some, :], attn, preferred_element_type=F32)
                wt[part] = term.astype(BF16)
            for copy in z_copies:
                copy.start()

        @pl.when(step == 5)
        def _():
            both = summed(1, 0)
            chain.wait_recv()
            sums[2] = (both + chain_in[...].astype(F32)).astype(BF16)
            home_a.start()

        @pl.when(step == 7)
        def _():
            sums[3] = summed(1, 1).astype(BF16)

            @pl.when(y > 0)
            def _():
                home_b.start()

            @pl.when(y == 0)
            def _():
                over_back.start()

            back_first.wait_recv()
            back_second.start()

        @pl.when(step == 8)
        def _():
            edge_copies[0].start()

        @pl.when(step == 9)
        def _():
            edge_copies[1].start()
            for copy in z_copies:
                copy.wait_recv()
            z_sum[...] = wt[z].astype(F32)
            for i in range(3):
                z_sum[...] += z_in[i].astype(F32)
            for copy in y_copies:
                copy.start()

        @pl.when((step == 9) & (y == 0))
        def _():
            over_back.wait_recv()
            over_home.start()

        return carry

    lax.fori_loop(0, 2 * (BACK + 1), backward, 0)

    dq_ref[...] = (dq_t[...] * HS**-0.5).astype(BF16)
    total = z_sum[pl.ds(pl.multiple_of(40 * low, 8), 40), :]
    for i, copy in enumerate(y_copies):
        copy.wait_recv()
        total = total + y_in[i]
    dw_ref[...] = total[:, :WIDTH]

    for copy in edge_copies + [home_a, home_b, back_second]:
        copy.wait_recv()
    for half in range(2):
        part = slice(HALF * half, HALF * (half + 1))
        total = dkv[half].astype(F32) + edge[half].astype(F32) + home_near[half].astype(F32)
        if half == 1:
            total = total + home_far[...].astype(F32)
        total_t = total.T.astype(BF16)
        dk_ref[:, part] = total_t[:WIDTH]
        dv_ref[:, part] = total_t[WIDTH:]

    copies = [near_k, near_v, relay_first, direct_k, direct_v, chain_k, relay_second]
    copies += [pass_near_k, pass_near_v, pass_far_k, pass_far_v]
    copies += mated[0] + mated[1] + edge_copies
    copies += [chain, back_first, back_second, home_a, home_b]
    for copy in across + copies + z_copies + y_copies:
        copy.wait_send()

    @pl.when(y == 3)
    def _():
        over_second.wait_send()

    @pl.when(y == 0)
    def _():
        over_home.wait_send()


def shards(queries, key_rows, value_rows, cotangent, out_weight, segment_units, left_segments):
    tm_count = lax.axis_size("tm")
    head_count = lax.axis_size("head")
    anywhere = pl.BlockSpec(memory_space=pl.ANY)
    vmem = pl.BlockSpec(memory_space=pltpu.VMEM)
    dma = pltpu.SemaphoreType.DMA
    out_t = jax.ShapeDtypeStruct((WIDTH, BLK), BF16)
    both = 2 * WIDTH
    blocks = BACK + 1
    query_t, key_t, value_t, weight_t = pl.pallas_call(
        functools.partial(kernel, tm_count, head_count),
        out_shape=(out_t, out_t, out_t, jax.ShapeDtypeStruct((40, WIDTH), F32)),
        in_specs=[vmem] * 2 + [anywhere] * 5,
        out_specs=(vmem, vmem, vmem, vmem),
        scratch_shapes=[
            pltpu.VMEM((blocks, both, BLK), BF16),
            pltpu.VMEM((WIDTH, BLK), BF16),
            pltpu.VMEM((WIDTH, BLK), BF16),
            pltpu.VMEM((2 * blocks, HALF, both), BF16),
            pltpu.VMEM((2 * blocks, HEADS, HALF, BLK), BF16),
            pltpu.VMEM((head_count * WIDTH, BLK), BF16),
            pltpu.VMEM((WIDTH, head_count * WIDTH), BF16),
            pltpu.VMEM((WIDTH, BLK), BF16),
            pltpu.VMEM((HEADS, 256, BLK), BF16),
            pltpu.VMEM((HEADS, 128, BLK), BF16),
            pltpu.VMEM((HEADS, 2 * BLK, 128), BF16),
            pltpu.VMEM((2, BLK, WIDE), F32),
            pltpu.VMEM((HEADS, HALF, 2 * BLK), BF16),
            pltpu.VMEM((WIDTH, BLK), F32),
            pltpu.VMEM((WIDTH, BLK), F32),
            pltpu.VMEM((blocks, HEADS, 8, BLK), F32),
            pltpu.VMEM((HEADS, 8, BLK), F32),
            pltpu.VMEM((HEADS, 8, BLK), F32),
            pltpu.VMEM((HEADS, 8, BLK), F32),
            pltpu.VMEM((2 * blocks, HALF, both), BF16),
            pltpu.VMEM((4, HALF, both), BF16),
            pltpu.VMEM((4, HALF, both), BF16),
            pltpu.VMEM((2, HALF, both), BF16),
            pltpu.VMEM((HALF, both), BF16),
            pltpu.VMEM((HALF, both), BF16),
            pltpu.VMEM((HALF, both), BF16),
            pltpu.VMEM((HALF, both), BF16),
            pltpu.VMEM((2, HALF, both), BF16),
            pltpu.VMEM((4, WIDTH, WEIGHT_WIDTH), BF16),
            pltpu.VMEM((3, WIDTH, WEIGHT_WIDTH), BF16),
            pltpu.VMEM((WIDTH, WEIGHT_WIDTH), F32),
            pltpu.VMEM((7, 40, WEIGHT_WIDTH), F32),
            dma((5,)),
            dma((12,)),
            dma((blocks,)),
            dma((blocks,)),
            dma((2,)),
            dma((3,)),
            dma((3,)),
            dma((8,)),
            dma((8,)),
            dma((4,)),
            dma((4,)),
            dma((3,)),
            dma((3,)),
            dma((7,)),
            dma((7,)),
        ],
        compiler_params=pltpu.CompilerParams(
            collective_id=0, has_side_effects=True, vmem_limit_bytes=60 << 20
        ),
    )(
        segment_units.reshape(1, -1),
        left_segments.reshape(1, -1),
        queries.T,
        key_rows.T,
        value_rows.T,
        cotangent.T,
        out_weight,
    )
    return (query_t.T, key_t.T, value_t.T, weight_t.T)


def solution(mesh):
    placed = (
        P("tm", "head"),
        P("tm", "head"),
        P("tm", "head"),
        P("tm", "head"),
        P("head", None),
        P(),
        P(),
    )
    return jax.shard_map(
        shards,
        mesh=mesh,
        in_specs=placed,
        out_specs=(P("tm", "head"), P("tm", "head"), P("tm", "head"), P("head", "tm")),
        check_vma=False,
    )
```

```python
import functools

import jax
import jax.numpy as jnp
from jax import lax
from jax.experimental import pallas as pl
from jax.experimental.pallas import tpu as pltpu
from jax.sharding import PartitionSpec as P

HS = 64
UNIT = 16
BLK = 512
HEADS = 5
WIDTH = HEADS * HS
BACK = 5
HALF = BLK // 2
WEIGHT_WIDTH = 384
STRIP = 128
WIDE = 256
HIDDEN = -2e30
LOWEST = -1e30
F32 = jnp.float32
BF16 = jnp.bfloat16
MESH = pl.DeviceIdType.MESH


def kernel(
    tm_count,
    head_count,
    units_ref,
    left_ref,
    q_hbm,
    k_hbm,
    v_hbm,
    cot_hbm,
    w_hbm,
    dq_ref,
    dk_ref,
    dv_ref,
    dw_ref,
    slots,
    relay,
    cross,
    kv_all,
    probs,
    cot_all,
    w_ref,
    q_ref,
    rhs,
    gt,
    rows,
    square,
    work,
    out_t,
    dq_t,
    m_all,
    m_run,
    l_run,
    delta,
    dkv,
    from_mate,
    sums,
    home_near,
    home_far,
    chain_in,
    relay_back,
    cross_back,
    edge,
    wt,
    z_in,
    z_sum,
    z_out,
    y_in,
    local,
    sent,
    got_k,
    got_v,
    got_relay,
    side_sent,
    side_got,
    back_sent,
    back_got,
    mate_sent,
    mate_got,
    z_sent,
    z_got,
    y_sent,
    y_got,
):
    t = lax.axis_index("tm")
    x = lax.axis_index("head")
    core = t % 2
    z = t // 8
    y = (t // 2) % 4
    low = t % 8

    def at(place):
        return {"tm": (place + tm_count) % tm_count}

    def chip(z_place, y_place):
        return (((z_place + 4) % 4) * 4 + y_place % 4) * 2 + core

    mate = at(t + 1 - 2 * core)
    before, after = chip(z, y + 3), chip(z, y + 1)
    inner = jnp.where((y == 1) | (y == 2), 1, 0)
    relay_to = chip(z + jnp.where(y >= 2, 1, 0), y + 3)
    relay_from = chip(z - inner, y + 1)
    back_to = chip(z - jnp.where(y < 2, 1, 0), y + 1)
    back_from = chip(z + inner, y + 3)

    greeted = [at(t - 2), at(t + 2), at(relay_from), at(back_from)]
    greeted += [{"head": (x + head_count + by) % head_count} for by in (-1, 1)]
    greeted += [at(t - 8 * i) for i in range(1, 4)]
    greeted += [at(8 * z + (low + 8 - i) % 8) for i in range(1, 8)]
    barrier = pltpu.get_barrier_semaphore()
    for target in greeted:
        pl.semaphore_signal(barrier, inc=1, device_id=target, device_id_type=MESH)
    edge_source = at(t + 5 * (2 * core - 1))
    pl.semaphore_signal(barrier, inc=1, device_id=edge_source, device_id_type=MESH)

    loads = [
        pltpu.make_async_copy(k_hbm, slots.at[0, 0:WIDTH], local.at[0]),
        pltpu.make_async_copy(v_hbm, slots.at[0, WIDTH : 2 * WIDTH], local.at[1]),
        pltpu.make_async_copy(q_hbm, q_ref, local.at[2]),
        pltpu.make_async_copy(
            cot_hbm, cot_all.at[pl.ds(pl.multiple_of(WIDTH * x, 64), WIDTH)], local.at[3]
        ),
        pltpu.make_async_copy(w_hbm, w_ref, local.at[4]),
    ]
    for load in loads:
        load.start()
    pl.semaphore_wait(barrier, len(greeted) + 1)

    def push(src, dst, send_sem, recv_sem, target):
        return pltpu.make_async_remote_copy(
            src_ref=src,
            dst_ref=dst,
            send_sem=send_sem,
            recv_sem=recv_sem,
            device_id=target,
            device_id_type=MESH,
        )

    def keys(src, slot, number, target):
        return push(src, slots.at[slot, 0:WIDTH], sent.at[number], got_k.at[slot], target)

    def values(src, slot, number, target):
        return push(
            src, slots.at[slot, WIDTH : 2 * WIDTH], sent.at[number], got_v.at[slot], target
        )

    def key_part(slot):
        return slots.at[slot, 0:WIDTH]

    def value_part(slot):
        return slots.at[slot, WIDTH : 2 * WIDTH]

    near_k = keys(k_hbm, 2, 0, at(t + 2))
    near_v = values(v_hbm, 2, 1, at(t + 2))
    over_first = push(v_hbm, cross, sent.at[1], got_relay.at[1], at(t + 8))
    over_second = values(cross, 2, 11, at(t - 6))
    relay_first = push(v_hbm, relay, sent.at[2], got_relay.at[0], at(relay_to))
    near_k.start()
    relay_first.start()
    def cot_rows(place, first, count):
        start = WIDTH * (place % head_count) + first
        return cot_all.at[pl.ds(pl.multiple_of(start, 32), count)]

    def aside(src, rows_there, number, by):
        place = {"head": (x + head_count + by) % head_count}
        return push(src, rows_there, side_sent.at[number], side_got.at[number], place)

    own_cot = cot_rows(x, 0, WIDTH)
    upper = cot_rows(x + head_count - 1, 0, WIDTH // 2)
    lower = cot_rows(x + 1, WIDTH // 2, WIDTH // 2)
    beside = [aside(cot_hbm, own_cot, 0, 1), aside(cot_hbm, own_cot, 1, -1)]
    opposite = [aside(upper, upper, 2, 1), aside(lower, lower, 3, -1)]
    for copy in beside:
        copy.start()

    @pl.when(y < 3)
    def _():
        near_v.start()

    @pl.when(y == 3)
    def _():
        over_first.start()

    direct_slot = 1 + 4 * core
    direct_to = at(t + 1 + 4 * core)
    direct_k = keys(k_hbm, direct_slot, 3, direct_to)
    direct_v = values(v_hbm, direct_slot, 4, direct_to)

    @pl.when(core == 0)
    def _():
        direct_k.start()
        direct_v.start()

    chain_k = keys(key_part(2), 4, 5, at(t + 2))
    relay_second = values(relay, 4, 6, at(before))
    pass_near = 3 - 2 * core
    pass_far = 5 - 2 * core
    pass_near_k = keys(key_part(2), pass_near, 7, mate)
    pass_near_v = values(value_part(2), pass_near, 8, mate)
    pass_far_k = keys(key_part(4), pass_far, 9, mate)
    pass_far_v = values(value_part(4), pass_far, 10, mate)

    segments = units_ref.shape[1]
    units = jnp.broadcast_to(units_ref[...].astype(F32), (8, segments)).astype(BF16)
    lefts = jnp.broadcast_to(left_ref[...].astype(F32), (8, segments)).astype(BF16)
    down = lax.broadcasted_iota(jnp.int32, (segments, 128), 0)
    over = lax.broadcasted_iota(jnp.int32, (segments, 128), 1)
    until = jnp.where(down <= over, 1.0, 0.0).astype(BF16)
    ahead = jnp.where(down < over, 1.0, 0.0).astype(BF16)
    same = jnp.where(down == over, 1.0, 0.0).astype(BF16)
    end_row = jnp.dot(units, until, preferred_element_type=F32)[0:1, :] * UNIT
    start_row = jnp.dot(units, ahead, preferred_element_type=F32)[0:1, :] * UNIT
    columns = (((0,), (1,)), ((), ()))
    end_col = lax.dot_general(until, units, columns, preferred_element_type=F32)[:, 0:1] * UNIT
    left_col = lax.dot_general(same, lefts, columns, preferred_element_type=F32)[:, 0:1]
    frame_row = (t * BLK + lax.broadcasted_iota(jnp.int32, (1, BLK), 1)).astype(F32)
    own_seg = jnp.sum(jnp.where(end_col <= frame_row, 1.0, 0.0), axis=0, keepdims=True)
    seg_down = lax.broadcasted_iota(jnp.int32, (128, BLK), 0).astype(F32)
    reach = jnp.sum(jnp.where(seg_down == own_seg, left_col, 0.0), axis=0, keepdims=True)
    lowest = jnp.maximum(own_seg - reach, 0.0)
    bias = jnp.where((seg_down >= lowest) & (seg_down <= own_seg), 0.0, HIDDEN).astype(BF16)

    blank = jnp.zeros((HS, BLK), BF16)
    lane = lax.broadcasted_iota(jnp.int32, (BLK, 128), 1)

    def spread(j, upright, transposed):
        g, half = divmod(j, 2)
        both = [transposed, blank] if half == 0 else [blank, transposed]
        if j < HEADS:
            rhs[j] = jnp.concatenate(both + [bias], axis=0)
        else:
            gt[j - HEADS] = jnp.concatenate(both, axis=0)
        zeros = jnp.zeros((BLK, HS), BF16)
        pair = [upright, zeros] if half == 0 else [zeros, upright]
        rows[g, BLK * half : BLK * (half + 1), :] = jnp.concatenate(pair, axis=1)

    loads[2].wait()
    queries_t = (q_ref[...].astype(F32) * HS**-0.5).astype(BF16)
    for j in range(HEADS):
        mine = queries_t[HS * j : HS * (j + 1), :]
        spread(j, mine.T, mine)
    m_run[...] = jnp.full(m_run.shape, LOWEST, F32)
    l_run[...] = jnp.zeros(l_run.shape, F32)
    out_t[...] = jnp.zeros(out_t.shape, F32)
    dq_t[...] = jnp.zeros(dq_t.shape, F32)
    loads[0].wait()
    loads[1].wait()

    def wait_slot(slot):
        keys(k_hbm, slot, 0, mate).wait_recv()
        values(v_hbm, slot, 1, mate).wait_recv()

    def near_event():
        relay_first.wait_recv()
        relay_second.start()

        near_k.wait_recv()
        chain_k.start()
        pass_near_k.start()
        for arrived, onward in zip(beside, opposite):
            arrived.wait_recv()
            onward.start()
        near_v.wait_recv()
        pass_near_v.start()

    def forward(step, carry):
        @pl.when((step == 1) & (core == 1))
        def _():
            direct_k.start()
            direct_v.start()

        @pl.when((step == 1) & (y == 3))
        def _():
            over_first.wait_recv()
            over_second.start()

        swapped = jnp.where(step == 0, 0, jnp.where(step < 3, 3 - step, 8 - step))
        slot = jnp.where(core == 0, swapped, step)

        @pl.when(step == 1 + core)
        def _():
            near_event()

        @pl.when((step == 2 - core) | (step == 3) | (step == 5))
        def _():
            wait_slot(slot)

        @pl.when(step == 4)
        def _():
            loads[3].wait()
            loads[4].wait()
            for copy in opposite:
                copy.wait_recv()
            grad_t = jnp.dot(w_ref[...], cot_all[...], preferred_element_type=F32).astype(BF16)
            for j in range(HEADS):
                mine = grad_t[HS * j : HS * (j + 1), :]
                spread(j + HEADS, mine.T, mine)

        @pl.when(step == 4)
        def _():
            keys(k_hbm, 4, 0, mate).wait_recv()
            pass_far_k.start()
            values(v_hbm, 4, 1, mate).wait_recv()
            pass_far_v.start()

        def upright(g):
            group = slice(128 * g, 128 * (g + 1))
            turned = slots[slot, group, :].T
            kv_all[2 * slot, :, group] = turned[0:HALF]
            kv_all[2 * slot + 1, :, group] = turned[HALF:BLK]

        first = ((t + tm_count - slot) % tm_count) * BLK
        frames = (first + lax.broadcasted_iota(jnp.int32, (BLK, 128), 0)).astype(F32)
        hot = jnp.where((frames >= start_row) & (frames < end_row), 1.0, 0.0).astype(BF16)
        upright(0)
        pieces = BLK // WIDE
        units_of = HEADS * pieces
        top = None
        for turn in range(units_of + 1):
            last = top
            if turn < units_of:
                h, c = divmod(turn, pieces)
                cols = slice(WIDE * c, WIDE * (c + 1))
                g = h // 2
                group = slice(128 * g, 128 * (g + 1))
                keys_here = [kv_all[2 * slot, :, group], kv_all[2 * slot + 1, :, group]]
                lhs = jnp.concatenate([jnp.concatenate(keys_here, axis=0), hot], axis=1)
                scores = jnp.dot(lhs, rhs[h, :, cols], preferred_element_type=F32)
                square[turn % 2] = scores
                top = jnp.max(scores.reshape(BLK // 8, 8, WIDE), axis=0)
                if turn < HEADS - 1:
                    upright(turn + 1)
            if turn == 0:
                continue
            h, c = divmod(turn - 1, pieces)
            cols = slice(WIDE * c, WIDE * (c + 1))
            m_old = m_run[h, 0:1, cols]
            m_new = jnp.maximum(m_old, jnp.max(last, axis=0, keepdims=True))
            factor = jnp.exp(m_old - m_new)
            m_run[h, 0:1, cols] = m_new
            m_all[slot, h, 0:1, cols] = m_new
            total = l_run[h, :, cols] * factor
            for r in range(0, BLK, STRIP):
                p = jnp.exp(square[(turn - 1) % 2, r : r + STRIP, :] - m_new)
                total = total + jnp.sum(p.reshape(STRIP // 8, 8, WIDE), axis=0)
                half, row = divmod(r, HALF)
                probs[2 * slot + half, h, row : row + STRIP, cols] = p.astype(BF16)
            l_run[h, :, cols] = total
            here = slice(HS * h, HS * (h + 1))
            added = out_t[here, cols] * factor
            for half in range(2):
                added += jnp.dot(
                    slots[slot, WIDTH + HS * h : WIDTH + HS * (h + 1), half * HALF : (half + 1) * HALF],
                    probs[2 * slot + half, h, :, cols],
                    preferred_element_type=F32,
                )
            out_t[here, cols] = added
        return carry

    lax.fori_loop(0, BACK + 1, forward, 0)

    for h in range(HEADS):
        here = slice(HS * h, HS * (h + 1))
        total = jnp.sum(l_run[h], axis=0, keepdims=True)
        out = out_t[here, :] / total
        out_t[here, :] = out
        side = HS * ((h + HEADS) % 2)
        own_grad = gt[h, side : side + HS, :].astype(F32)
        delta[h, 0:1, :] = jnp.sum(out * own_grad, axis=0, keepdims=True)
        l_run[h, 0:1, :] = m_run[h, 0:1, :] + jnp.log(total)

    z_copies = [
        push(
            wt.at[(z + i) % 4], z_in.at[i - 1], z_sent.at[i - 1], z_got.at[i - 1], at(t + 8 * i)
        )
        for i in range(1, 4)
    ]
    y_copies = [
        push(
            z_out.at[(low + i) % 8],
            y_in.at[i - 1],
            y_sent.at[i - 1],
            y_got.at[i - 1],
            at(8 * z + (low + i) % 8),
        )
        for i in range(1, 8)
    ]

    def piece(slot, half):
        return dkv.at[2 * slot + half]

    def to_mate(pair, half):
        number = 2 * pair + half
        return push(
            piece(3 + 2 * core - 2 * pair, half),
            from_mate.at[number],
            mate_sent.at[number],
            mate_got.at[number],
            mate,
        )

    mated = [[to_mate(pair, half) for half in range(2)] for pair in range(2)]
    chain = push(sums.at[0], chain_in, back_sent.at[0], back_got.at[0], at(t - 2))
    back_first = push(sums.at[1], relay_back, back_sent.at[1], back_got.at[1], at(back_to))
    back_second = push(relay_back, home_far, back_sent.at[2], back_got.at[2], at(after))
    home_a = push(sums.at[2], home_near.at[0], back_sent.at[3], back_got.at[3], at(t - 2))
    home_b = push(sums.at[3], home_near.at[1], back_sent.at[4], back_got.at[4], at(t - 2))
    over_back = push(sums.at[3], cross_back, back_sent.at[4], back_got.at[5], at(t - 8))
    over_home = push(cross_back, home_near.at[1], back_sent.at[5], back_got.at[4], at(t + 6))
    edge_copies = [
        push(
            piece(5 - 4 * core, half),
            edge.at[half],
            back_sent.at[6 + half],
            back_got.at[6 + half],
            at(t - 5 + 4 * core),
        )
        for half in range(2)
    ]

    def backward(step, carry):
        pair, within = step // 4, step % 4
        paired = jnp.where(within % 2 == 0, 3 + 2 * core, 4) - 2 * pair
        slot = jnp.where(step < 8, paired, jnp.where(step < 10, 5 - 4 * core, 0))
        half = jnp.where(step < 8, within // 2, step % 2)
        here = 2 * slot + half
        pieces = BLK // WIDE
        units_of = HEADS * pieces
        for turn in range(units_of + 1):
            if turn < units_of:
                h, c = divmod(turn, pieces)
                g = (h + HEADS) // 2
                square[turn % 2, 0:HALF] = jnp.dot(
                    kv_all[here, :, 128 * g : 128 * (g + 1)],
                    gt[h, :, WIDE * c : WIDE * (c + 1)],
                    preferred_element_type=F32,
                )
            if turn == 0:
                continue
            h, c = divmod(turn - 1, pieces)
            cols = slice(WIDE * c, WIDE * (c + 1))
            scale = jnp.exp(m_all[slot, h, 0:1, cols] - l_run[h, 0:1, cols])
            shift = delta[h, 0:1, cols]
            ds_at = BLK * (h % 2) + WIDE * c
            p_at = BLK * ((h + HEADS) % 2) + WIDE * c
            for r in range(0, HALF, STRIP):
                down = slice(r, r + STRIP)
                p = probs[here, h, down, cols].astype(F32) * scale
                ds = p * (square[(turn - 1) % 2, down, :] - shift)
                work[h // 2, down, ds_at : ds_at + WIDE] = ds.astype(BF16)
                work[(h + HEADS) // 2, down, p_at : p_at + WIDE] = p.astype(BF16)
            mine = slice(HS * h, HS * (h + 1))
            dq_t[mine, cols] += jnp.dot(
                slots[slot, mine, pl.ds(pl.multiple_of(HALF * half, HALF), HALF)],
                work[h // 2, :, ds_at : ds_at + WIDE],
                preferred_element_type=F32,
            )
            if c < pieces - 1:
                continue
            for g in ((), (0,), (3,), (1,), (2, 4))[h]:
                dkv[here, :, 128 * g : 128 * (g + 1)] = jnp.dot(
                    work[g], rows[g], preferred_element_type=F32
                ).astype(BF16)

        for j in range(2):
            for k in range(2):

                @pl.when(step == 4 * j + 2 * k)
                def _(j=j, k=k):
                    mated[j][k].start()

        def summed(pair, half):
            mated[pair][half].wait_recv()
            kept = dkv[2 * (4 - 2 * pair) + half].astype(F32)
            return kept + from_mate[2 * pair + half].astype(F32)

        @pl.when(step == 1)
        def _():
            sums[0] = summed(0, 0).astype(BF16)
            chain.start()
            attn = jnp.concatenate(
                [out_t[...].T.astype(BF16), jnp.zeros((BLK, WEIGHT_WIDTH - WIDTH), BF16)], axis=1
            )
            for part in range(4):
                some = slice(WIDTH * part, WIDTH * (part + 1))
                term = jnp.dot(cot_all[some, :], attn, preferred_element_type=F32)
                wt[part] = term.astype(BF16)
            for copy in z_copies:
                copy.start()

        @pl.when(step == 3)
        def _():
            sums[1] = summed(0, 1).astype(BF16)
            back_first.start()

        @pl.when(step == 5)
        def _():
            both = summed(1, 0)
            chain.wait_recv()
            sums[2] = (both + chain_in[...].astype(F32)).astype(BF16)
            home_a.start()

        @pl.when(step == 6)
        def _():
            for copy in z_copies:
                copy.wait_recv()
            z_sum[...] = wt[z].astype(F32)
            for i in range(3):
                z_sum[...] += z_in[i].astype(F32)
            for i in range(8):
                block = z_sum[40 * i : 40 * (i + 1), :]
                rest = jnp.zeros((8, WEIGHT_WIDTH), F32)
                z_out[i] = jnp.concatenate([block, rest], axis=0).astype(BF16)
            for copy in y_copies:
                copy.start()

        @pl.when(step == 7)
        def _():
            sums[3] = summed(1, 1).astype(BF16)

            @pl.when(y > 0)
            def _():
                home_b.start()

            @pl.when(y == 0)
            def _():
                over_back.start()

            back_first.wait_recv()
            back_second.start()

        @pl.when(step == 8)
        def _():
            edge_copies[0].start()

        @pl.when(step == 9)
        def _():
            edge_copies[1].start()

        @pl.when((step == 9) & (y == 0))
        def _():
            over_back.wait_recv()
            over_home.start()

        return carry

    lax.fori_loop(0, 2 * (BACK + 1), backward, 0)

    dq_ref[...] = (dq_t[...] * HS**-0.5).astype(BF16)
    total = z_sum[pl.ds(pl.multiple_of(40 * low, 8), 40), :]
    for i, copy in enumerate(y_copies):
        copy.wait_recv()
        total = total + y_in[i].astype(F32)[0:40]
    dw_ref[...] = total[:, :WIDTH]

    for copy in edge_copies + [home_a, home_b, back_second]:
        copy.wait_recv()
    for half in range(2):
        part = slice(HALF * half, HALF * (half + 1))
        total = dkv[half].astype(F32) + edge[half].astype(F32) + home_near[half].astype(F32)
        if half == 1:
            total = total + home_far[...].astype(F32)
        total_t = total.T.astype(BF16)
        dk_ref[:, part] = total_t[:WIDTH]
        dv_ref[:, part] = total_t[WIDTH:]

    copies = [near_k, near_v, relay_first, direct_k, direct_v, chain_k, relay_second]
    copies += [pass_near_k, pass_near_v, pass_far_k, pass_far_v]
    copies += mated[0] + mated[1] + edge_copies
    copies += [chain, back_first, back_second, home_a, home_b]
    for copy in beside + opposite + copies + z_copies + y_copies:
        copy.wait_send()

    @pl.when(y == 3)
    def _():
        over_second.wait_send()

    @pl.when(y == 0)
    def _():
        over_home.wait_send()


def shards(queries, key_rows, value_rows, cotangent, out_weight, segment_units, left_segments):
    tm_count = lax.axis_size("tm")
    head_count = lax.axis_size("head")
    anywhere = pl.BlockSpec(memory_space=pl.ANY)
    vmem = pl.BlockSpec(memory_space=pltpu.VMEM)
    dma = pltpu.SemaphoreType.DMA
    out_t = jax.ShapeDtypeStruct((WIDTH, BLK), BF16)
    both = 2 * WIDTH
    blocks = BACK + 1
    query_t, key_t, value_t, weight_t = pl.pallas_call(
        functools.partial(kernel, tm_count, head_count),
        out_shape=(out_t, out_t, out_t, jax.ShapeDtypeStruct((40, WIDTH), F32)),
        in_specs=[vmem] * 2 + [anywhere] * 5,
        out_specs=(vmem, vmem, vmem, vmem),
        scratch_shapes=[
            pltpu.VMEM((blocks, both, BLK), BF16),
            pltpu.VMEM((WIDTH, BLK), BF16),
            pltpu.VMEM((WIDTH, BLK), BF16),
            pltpu.VMEM((2 * blocks, HALF, both), BF16),
            pltpu.VMEM((2 * blocks, HEADS, HALF, BLK), BF16),
            pltpu.VMEM((head_count * WIDTH, BLK), BF16),
            pltpu.VMEM((WIDTH, head_count * WIDTH), BF16),
            pltpu.VMEM((WIDTH, BLK), BF16),
            pltpu.VMEM((HEADS, 256, BLK), BF16),
            pltpu.VMEM((HEADS, 128, BLK), BF16),
            pltpu.VMEM((HEADS, 2 * BLK, 128), BF16),
            pltpu.VMEM((2, BLK, WIDE), F32),
            pltpu.VMEM((HEADS, HALF, 2 * BLK), BF16),
            pltpu.VMEM((WIDTH, BLK), F32),
            pltpu.VMEM((WIDTH, BLK), F32),
            pltpu.VMEM((blocks, HEADS, 8, BLK), F32),
            pltpu.VMEM((HEADS, 8, BLK), F32),
            pltpu.VMEM((HEADS, 8, BLK), F32),
            pltpu.VMEM((HEADS, 8, BLK), F32),
            pltpu.VMEM((2 * blocks, HALF, both), BF16),
            pltpu.VMEM((4, HALF, both), BF16),
            pltpu.VMEM((4, HALF, both), BF16),
            pltpu.VMEM((2, HALF, both), BF16),
            pltpu.VMEM((HALF, both), BF16),
            pltpu.VMEM((HALF, both), BF16),
            pltpu.VMEM((HALF, both), BF16),
            pltpu.VMEM((HALF, both), BF16),
            pltpu.VMEM((2, HALF, both), BF16),
            pltpu.VMEM((4, WIDTH, WEIGHT_WIDTH), BF16),
            pltpu.VMEM((3, WIDTH, WEIGHT_WIDTH), BF16),
            pltpu.VMEM((WIDTH, WEIGHT_WIDTH), F32),
            pltpu.VMEM((8, 48, WEIGHT_WIDTH), BF16),
            pltpu.VMEM((7, 48, WEIGHT_WIDTH), BF16),
            dma((5,)),
            dma((12,)),
            dma((blocks,)),
            dma((blocks,)),
            dma((2,)),
            dma((4,)),
            dma((4,)),
            dma((8,)),
            dma((8,)),
            dma((4,)),
            dma((4,)),
            dma((3,)),
            dma((3,)),
            dma((7,)),
            dma((7,)),
        ],
        compiler_params=pltpu.CompilerParams(
            collective_id=0, has_side_effects=True, vmem_limit_bytes=60 << 20
        ),
    )(
        segment_units.reshape(1, -1),
        left_segments.reshape(1, -1),
        queries.T,
        key_rows.T,
        value_rows.T,
        cotangent.T,
        out_weight,
    )
    return (query_t.T, key_t.T, value_t.T, weight_t.T)


def solution(mesh):
    placed = (
        P("tm", "head"),
        P("tm", "head"),
        P("tm", "head"),
        P("tm", "head"),
        P("head", None),
        P(),
        P(),
    )
    return jax.shard_map(
        shards,
        mesh=mesh,
        in_specs=placed,
        out_specs=(P("tm", "head"), P("tm", "head"), P("tm", "head"), P("head", "tm")),
        check_vma=False,
    )
```

```python
import functools

import jax
import jax.numpy as jnp
from jax import lax
from jax.experimental import pallas as pl
from jax.experimental.pallas import tpu as pltpu
from jax.sharding import PartitionSpec as P

HS = 64
UNIT = 16
BLK = 512
HEADS = 5
WIDTH = HEADS * HS
BACK = 5
HALF = BLK // 2
WEIGHT_WIDTH = 384
STRIP = 128
WIDE = 256
HIDDEN = -2e30
LOWEST = -1e30
F32 = jnp.float32
BF16 = jnp.bfloat16
MESH = pl.DeviceIdType.MESH


def kernel(
    tm_count,
    head_count,
    units_ref,
    left_ref,
    q_hbm,
    k_hbm,
    v_hbm,
    cot_hbm,
    w_hbm,
    dq_ref,
    dk_ref,
    dv_ref,
    dw_ref,
    slots,
    relay,
    cross,
    kv_all,
    probs,
    cot_all,
    w_ref,
    q_ref,
    rhs,
    gt,
    rows,
    square,
    work,
    out_t,
    dq_t,
    m_all,
    m_run,
    l_run,
    delta,
    dkv,
    from_mate,
    sums,
    home_near,
    home_far,
    chain_in,
    relay_back,
    cross_back,
    edge,
    wt,
    z_in,
    z_sum,
    z_out,
    y_in,
    local,
    sent,
    got_k,
    got_v,
    got_relay,
    side_sent,
    side_got,
    back_sent,
    back_got,
    z_sent,
    z_got,
    y_sent,
    y_got,
):
    t = lax.axis_index("tm")
    x = lax.axis_index("head")
    core = t % 2
    z = t // 8
    y = (t // 2) % 4
    low = t % 8

    def at(place):
        return {"tm": (place + tm_count) % tm_count}

    def chip(z_place, y_place):
        return (((z_place + 4) % 4) * 4 + y_place % 4) * 2 + core

    mate = at(t + 1 - 2 * core)
    before, after = chip(z, y + 3), chip(z, y + 1)
    inner = jnp.where((y == 1) | (y == 2), 1, 0)
    relay_to = chip(z + jnp.where(y >= 2, 1, 0), y + 3)
    relay_from = chip(z - inner, y + 1)
    back_to = chip(z - jnp.where(y < 2, 1, 0), y + 1)
    back_from = chip(z + inner, y + 3)

    greeted = [at(t - 2), at(t + 2), at(relay_from), at(back_from)]
    greeted += [{"head": (x + head_count + by) % head_count} for by in (-1, 1)]
    greeted += [at(t - 8 * i) for i in range(1, 4)]
    greeted += [at(8 * z + (low + 8 - i) % 8) for i in range(1, 8)]
    barrier = pltpu.get_barrier_semaphore()
    for target in greeted:
        pl.semaphore_signal(barrier, inc=1, device_id=target, device_id_type=MESH)
    edge_source = at(t + 5 * (2 * core - 1))
    pl.semaphore_signal(barrier, inc=1, device_id=edge_source, device_id_type=MESH)

    loads = [
        pltpu.make_async_copy(k_hbm, slots.at[0, 0:WIDTH], local.at[0]),
        pltpu.make_async_copy(v_hbm, slots.at[0, WIDTH : 2 * WIDTH], local.at[1]),
        pltpu.make_async_copy(q_hbm, q_ref, local.at[2]),
        pltpu.make_async_copy(
            cot_hbm, cot_all.at[pl.ds(pl.multiple_of(WIDTH * x, 64), WIDTH)], local.at[3]
        ),
        pltpu.make_async_copy(w_hbm, w_ref, local.at[4]),
    ]
    for load in loads:
        load.start()
    pl.semaphore_wait(barrier, len(greeted) + 1)

    def push(src, dst, send_sem, recv_sem, target):
        return pltpu.make_async_remote_copy(
            src_ref=src,
            dst_ref=dst,
            send_sem=send_sem,
            recv_sem=recv_sem,
            device_id=target,
            device_id_type=MESH,
        )

    def keys(src, slot, number, target):
        return push(src, slots.at[slot, 0:WIDTH], sent.at[number], got_k.at[slot], target)

    def values(src, slot, number, target):
        return push(
            src, slots.at[slot, WIDTH : 2 * WIDTH], sent.at[number], got_v.at[slot], target
        )

    def key_part(slot):
        return slots.at[slot, 0:WIDTH]

    def value_part(slot):
        return slots.at[slot, WIDTH : 2 * WIDTH]

    near_k = keys(k_hbm, 2, 0, at(t + 2))
    near_v = values(v_hbm, 2, 1, at(t + 2))
    over_first = push(v_hbm, cross, sent.at[1], got_relay.at[1], at(t + 8))
    over_second = values(cross, 2, 11, at(t - 6))
    relay_first = push(v_hbm, relay, sent.at[2], got_relay.at[0], at(relay_to))
    near_k.start()
    relay_first.start()
    def cot_rows(place, first, count):
        start = WIDTH * (place % head_count) + first
        return cot_all.at[pl.ds(pl.multiple_of(start, 32), count)]

    def aside(src, rows_there, number, by):
        place = {"head": (x + head_count + by) % head_count}
        return push(src, rows_there, side_sent.at[number], side_got.at[number], place)

    own_cot = cot_rows(x, 0, WIDTH)
    upper = cot_rows(x + head_count - 1, 0, WIDTH // 2)
    lower = cot_rows(x + 1, WIDTH // 2, WIDTH // 2)
    beside = [aside(cot_hbm, own_cot, 0, 1), aside(cot_hbm, own_cot, 1, -1)]
    opposite = [aside(upper, upper, 2, 1), aside(lower, lower, 3, -1)]
    for copy in beside:
        copy.start()

    @pl.when(y < 3)
    def _():
        near_v.start()

    @pl.when(y == 3)
    def _():
        over_first.start()

    direct_slot = 1 + 4 * core
    direct_to = at(t + 1 + 4 * core)
    direct_k = keys(k_hbm, direct_slot, 3, direct_to)
    direct_v = values(v_hbm, direct_slot, 4, direct_to)

    @pl.when(core == 0)
    def _():
        direct_k.start()
        direct_v.start()

    chain_k = keys(key_part(2), 4, 5, at(t + 2))
    relay_second = values(relay, 4, 6, at(before))
    pass_near = 3 - 2 * core
    pass_far = 5 - 2 * core
    pass_near_k = keys(key_part(2), pass_near, 7, mate)
    pass_near_v = values(value_part(2), pass_near, 8, mate)
    pass_far_k = keys(key_part(4), pass_far, 9, mate)
    pass_far_v = values(value_part(4), pass_far, 10, mate)

    segments = units_ref.shape[1]
    units = jnp.broadcast_to(units_ref[...].astype(F32), (8, segments)).astype(BF16)
    lefts = jnp.broadcast_to(left_ref[...].astype(F32), (8, segments)).astype(BF16)
    down = lax.broadcasted_iota(jnp.int32, (segments, 128), 0)
    over = lax.broadcasted_iota(jnp.int32, (segments, 128), 1)
    until = jnp.where(down <= over, 1.0, 0.0).astype(BF16)
    ahead = jnp.where(down < over, 1.0, 0.0).astype(BF16)
    same = jnp.where(down == over, 1.0, 0.0).astype(BF16)
    end_row = jnp.dot(units, until, preferred_element_type=F32)[0:1, :] * UNIT
    start_row = jnp.dot(units, ahead, preferred_element_type=F32)[0:1, :] * UNIT
    columns = (((0,), (1,)), ((), ()))
    end_col = lax.dot_general(until, units, columns, preferred_element_type=F32)[:, 0:1] * UNIT
    left_col = lax.dot_general(same, lefts, columns, preferred_element_type=F32)[:, 0:1]
    frame_row = (t * BLK + lax.broadcasted_iota(jnp.int32, (1, BLK), 1)).astype(F32)
    own_seg = jnp.sum(jnp.where(end_col <= frame_row, 1.0, 0.0), axis=0, keepdims=True)
    seg_down = lax.broadcasted_iota(jnp.int32, (128, BLK), 0).astype(F32)
    reach = jnp.sum(jnp.where(seg_down == own_seg, left_col, 0.0), axis=0, keepdims=True)
    lowest = jnp.maximum(own_seg - reach, 0.0)
    bias = jnp.where((seg_down >= lowest) & (seg_down <= own_seg), 0.0, HIDDEN).astype(BF16)

    blank = jnp.zeros((HS, BLK), BF16)
    lane = lax.broadcasted_iota(jnp.int32, (BLK, 128), 1)

    def spread(j, upright, transposed):
        g, half = divmod(j, 2)
        both = [transposed, blank] if half == 0 else [blank, transposed]
        if j < HEADS:
            rhs[j] = jnp.concatenate(both + [bias], axis=0)
        else:
            gt[j - HEADS] = jnp.concatenate(both, axis=0)
        zeros = jnp.zeros((BLK, HS), BF16)
        pair = [upright, zeros] if half == 0 else [zeros, upright]
        rows[g, BLK * half : BLK * (half + 1), :] = jnp.concatenate(pair, axis=1)

    loads[2].wait()
    queries_t = (q_ref[...].astype(F32) * HS**-0.5).astype(BF16)
    for j in range(HEADS):
        mine = queries_t[HS * j : HS * (j + 1), :]
        spread(j, mine.T, mine)
    m_run[...] = jnp.full(m_run.shape, LOWEST, F32)
    l_run[...] = jnp.zeros(l_run.shape, F32)
    out_t[...] = jnp.zeros(out_t.shape, F32)
    dq_t[...] = jnp.zeros(dq_t.shape, F32)
    loads[0].wait()
    loads[1].wait()

    def wait_slot(slot):
        keys(k_hbm, slot, 0, mate).wait_recv()
        values(v_hbm, slot, 1, mate).wait_recv()

    def near_event():
        relay_first.wait_recv()
        relay_second.start()

        near_k.wait_recv()
        chain_k.start()
        pass_near_k.start()
        for arrived, onward in zip(beside, opposite):
            arrived.wait_recv()
            onward.start()
        near_v.wait_recv()
        pass_near_v.start()

    def forward(step, carry):
        @pl.when((step == 1) & (core == 1))
        def _():
            direct_k.start()
            direct_v.start()

        @pl.when((step == 1) & (y == 3))
        def _():
            over_first.wait_recv()
            over_second.start()

        swapped = jnp.where(step == 0, 0, jnp.where(step < 3, 3 - step, 8 - step))
        slot = jnp.where(core == 0, swapped, step)

        @pl.when(step == 1 + core)
        def _():
            near_event()

        @pl.when((step == 2 - core) | (step == 3) | (step == 5))
        def _():
            wait_slot(slot)

        @pl.when(step == 4)
        def _():
            loads[3].wait()
            loads[4].wait()
            for copy in opposite:
                copy.wait_recv()
            grad_t = jnp.dot(w_ref[...], cot_all[...], preferred_element_type=F32).astype(BF16)
            for j in range(HEADS):
                mine = grad_t[HS * j : HS * (j + 1), :]
                spread(j + HEADS, mine.T, mine)

        @pl.when(step == 4)
        def _():
            keys(k_hbm, 4, 0, mate).wait_recv()
            pass_far_k.start()
            values(v_hbm, 4, 1, mate).wait_recv()
            pass_far_v.start()

        def upright(g):
            group = slice(128 * g, 128 * (g + 1))
            kv_all[slot, :, group] = slots[slot, group, :].T

        first = ((t + tm_count - slot) % tm_count) * BLK
        frames = (first + lax.broadcasted_iota(jnp.int32, (BLK, 128), 0)).astype(F32)
        hot = jnp.where((frames >= start_row) & (frames < end_row), 1.0, 0.0).astype(BF16)
        upright(0)
        pieces = BLK // WIDE
        units_of = HEADS * pieces
        top = None
        for turn in range(units_of + 1):
            last = top
            if turn < units_of:
                h, c = divmod(turn, pieces)
                cols = slice(WIDE * c, WIDE * (c + 1))
                g = h // 2
                lhs = jnp.concatenate([kv_all[slot, :, 128 * g : 128 * (g + 1)], hot], axis=1)
                scores = jnp.dot(lhs, rhs[h, :, cols], preferred_element_type=F32)
                square[turn % 2] = scores
                top = jnp.max(scores.reshape(BLK // 8, 8, WIDE), axis=0)
                if turn < HEADS - 1:
                    upright(turn + 1)
            if turn == 0:
                continue
            h, c = divmod(turn - 1, pieces)
            cols = slice(WIDE * c, WIDE * (c + 1))
            m_old = m_run[h, 0:1, cols]
            m_new = jnp.maximum(m_old, jnp.max(last, axis=0, keepdims=True))
            factor = jnp.exp(m_old - m_new)
            m_run[h, 0:1, cols] = m_new
            m_all[slot, h, 0:1, cols] = m_new
            total = l_run[h, :, cols] * factor
            for r in range(0, BLK, STRIP):
                p = jnp.exp(square[(turn - 1) % 2, r : r + STRIP, :] - m_new)
                total = total + jnp.sum(p.reshape(STRIP // 8, 8, WIDE), axis=0)
                probs[slot, h, r : r + STRIP, cols] = p.astype(BF16)
            l_run[h, :, cols] = total
            here = slice(HS * h, HS * (h + 1))
            out_t[here, cols] = out_t[here, cols] * factor + jnp.dot(
                slots[slot, WIDTH + HS * h : WIDTH + HS * (h + 1), :],
                probs[slot, h, :, cols],
                preferred_element_type=F32,
            )
        return carry

    lax.fori_loop(0, BACK + 1, forward, 0)

    for h in range(HEADS):
        here = slice(HS * h, HS * (h + 1))
        total = jnp.sum(l_run[h], axis=0, keepdims=True)
        out = out_t[here, :] / total
        out_t[here, :] = out
        side = HS * ((h + HEADS) % 2)
        own_grad = gt[h, side : side + HS, :].astype(F32)
        delta[h, 0:1, :] = jnp.sum(out * own_grad, axis=0, keepdims=True)
        l_run[h, 0:1, :] = m_run[h, 0:1, :] + jnp.log(total)

    z_copies = [
        push(
            wt.at[(z + i) % 4], z_in.at[i - 1], z_sent.at[i - 1], z_got.at[i - 1], at(t + 8 * i)
        )
        for i in range(1, 4)
    ]
    attn = jnp.concatenate(
        [out_t[...].T.astype(BF16), jnp.zeros((BLK, WEIGHT_WIDTH - WIDTH), BF16)], axis=1
    )
    for part in range(4):
        piece = slice(WIDTH * part, WIDTH * (part + 1))
        wt[part] = jnp.dot(cot_all[piece, :], attn, preferred_element_type=F32).astype(BF16)
    for copy in z_copies:
        copy.start()
    y_copies = [
        push(
            z_out.at[(low + i) % 8],
            y_in.at[i - 1],
            y_sent.at[i - 1],
            y_got.at[i - 1],
            at(8 * z + (low + i) % 8),
        )
        for i in range(1, 8)
    ]

    far_slot, near_slot, edge_slot = 3 + 2 * core, 1 + 2 * core, 5 - 4 * core
    to_far = push(dkv.at[far_slot], from_mate.at[0], back_sent.at[0], back_got.at[0], mate)
    to_near = push(dkv.at[near_slot], from_mate.at[1], back_sent.at[1], back_got.at[1], mate)
    chain = push(sums.at[0, 0:HALF], chain_in, back_sent.at[2], back_got.at[2], at(t - 2))
    back_first = push(
        sums.at[0, HALF:BLK], relay_back, back_sent.at[3], back_got.at[3], at(back_to)
    )
    back_second = push(relay_back, home_far, back_sent.at[4], back_got.at[4], at(after))
    home_a = push(
        sums.at[1, 0:HALF], home_near.at[0:HALF], back_sent.at[5], back_got.at[5], at(t - 2)
    )
    home_b = push(
        sums.at[1, HALF:BLK], home_near.at[HALF:BLK], back_sent.at[7], back_got.at[7], at(t - 2)
    )
    over_back = push(sums.at[1, HALF:BLK], cross_back, back_sent.at[7], back_got.at[8], at(t - 8))
    over_home = push(
        cross_back, home_near.at[HALF:BLK], back_sent.at[8], back_got.at[7], at(t + 6)
    )
    edge_to = at(t - 5 + 4 * core)
    edge_copy = push(dkv.at[edge_slot], edge, back_sent.at[6], back_got.at[6], edge_to)

    def backward(step, carry):
        crossed = jnp.where(
            step < 2, 3 + step, jnp.where(step < 4, step - 1, jnp.where(step == 4, 5, 0))
        )
        slot = jnp.where(core == 0, crossed, 5 - step)
        pieces = BLK // WIDE
        units_of = HEADS * pieces
        for turn in range(units_of + 1):
            if turn < units_of:
                h, c = divmod(turn, pieces)
                g = (h + HEADS) // 2
                square[turn % 2] = jnp.dot(
                    kv_all[slot, :, 128 * g : 128 * (g + 1)],
                    gt[h, :, WIDE * c : WIDE * (c + 1)],
                    preferred_element_type=F32,
                )
            if turn == 0:
                continue
            h, c = divmod(turn - 1, pieces)
            cols = slice(WIDE * c, WIDE * (c + 1))
            scale = jnp.exp(m_all[slot, h, 0:1, cols] - l_run[h, 0:1, cols])
            shift = delta[h, 0:1, cols]
            ds_at = BLK * (h % 2) + WIDE * c
            p_at = BLK * ((h + HEADS) % 2) + WIDE * c
            for r in range(0, BLK, STRIP):
                down = slice(r, r + STRIP)
                p = probs[slot, h, down, cols].astype(F32) * scale
                ds = p * (square[(turn - 1) % 2, down, :] - shift)
                work[h // 2, down, ds_at : ds_at + WIDE] = ds.astype(BF16)
                work[(h + HEADS) // 2, down, p_at : p_at + WIDE] = p.astype(BF16)
            here = slice(HS * h, HS * (h + 1))
            dq_t[here, cols] += jnp.dot(
                slots[slot, here, :],
                work[h // 2, :, ds_at : ds_at + WIDE],
                preferred_element_type=F32,
            )
            if c < pieces - 1:
                continue
            for g in ((), (0,), (3,), (1,), (2, 4))[h]:
                dkv[slot, :, 128 * g : 128 * (g + 1)] = jnp.dot(
                    work[g], rows[g], preferred_element_type=F32
                ).astype(BF16)

        @pl.when(step == 0)
        def _():
            to_far.start()

        @pl.when(step == 1)
        def _():
            to_far.wait_recv()
            sums[0] = (dkv[4].astype(F32) + from_mate[0].astype(F32)).astype(BF16)
            chain.start()
            back_first.start()

        @pl.when(step == 2)
        def _():
            to_near.start()

        @pl.when(step == 3)
        def _():
            to_near.wait_recv()
            both = dkv[2].astype(F32) + from_mate[1].astype(F32)
            chain.wait_recv()
            sums[1, 0:HALF] = (both[0:HALF] + chain_in[...].astype(F32)).astype(BF16)
            sums[1, HALF:BLK] = both[HALF:BLK].astype(BF16)
            home_a.start()

            @pl.when(y > 0)
            def _():
                home_b.start()

            @pl.when(y == 0)
            def _():
                over_back.start()

            back_first.wait_recv()
            back_second.start()
            for copy in z_copies:
                copy.wait_recv()
            z_sum[...] = wt[z].astype(F32)
            for i in range(3):
                z_sum[...] += z_in[i].astype(F32)
            for i in range(8):
                block = z_sum[40 * i : 40 * (i + 1), :]
                rest = jnp.zeros((8, WEIGHT_WIDTH), F32)
                z_out[i] = jnp.concatenate([block, rest], axis=0).astype(BF16)
            for copy in y_copies:
                copy.start()

        @pl.when(step == 4)
        def _():
            edge_copy.start()

            @pl.when(y == 0)
            def _():
                over_back.wait_recv()
                over_home.start()

        return carry

    lax.fori_loop(0, BACK + 1, backward, 0)

    dq_ref[...] = (dq_t[...] * HS**-0.5).astype(BF16)
    total = z_sum[pl.ds(pl.multiple_of(40 * low, 8), 40), :]
    for i, copy in enumerate(y_copies):
        copy.wait_recv()
        total = total + y_in[i].astype(F32)[0:40]
    dw_ref[...] = total[:, :WIDTH]

    edge_copy.wait_recv()
    home_a.wait_recv()
    home_b.wait_recv()
    back_second.wait_recv()
    for half in range(2):
        part = slice(HALF * half, HALF * (half + 1))
        total = dkv[0, part].astype(F32) + edge[part].astype(F32) + home_near[part].astype(F32)
        if half == 1:
            total = total + home_far[...].astype(F32)
        total_t = total.T.astype(BF16)
        dk_ref[:, part] = total_t[:WIDTH]
        dv_ref[:, part] = total_t[WIDTH:]

    copies = [near_k, near_v, relay_first, direct_k, direct_v, chain_k, relay_second]
    copies += [pass_near_k, pass_near_v, pass_far_k, pass_far_v]
    copies += [to_far, to_near, chain, back_first, back_second, home_a, home_b, edge_copy]
    for copy in beside + opposite + copies + z_copies + y_copies:
        copy.wait_send()

    @pl.when(y == 3)
    def _():
        over_second.wait_send()

    @pl.when(y == 0)
    def _():
        over_home.wait_send()


def shards(queries, key_rows, value_rows, cotangent, out_weight, segment_units, left_segments):
    tm_count = lax.axis_size("tm")
    head_count = lax.axis_size("head")
    anywhere = pl.BlockSpec(memory_space=pl.ANY)
    vmem = pl.BlockSpec(memory_space=pltpu.VMEM)
    dma = pltpu.SemaphoreType.DMA
    out_t = jax.ShapeDtypeStruct((WIDTH, BLK), BF16)
    both = 2 * WIDTH
    blocks = BACK + 1
    query_t, key_t, value_t, weight_t = pl.pallas_call(
        functools.partial(kernel, tm_count, head_count),
        out_shape=(out_t, out_t, out_t, jax.ShapeDtypeStruct((40, WIDTH), F32)),
        in_specs=[vmem] * 2 + [anywhere] * 5,
        out_specs=(vmem, vmem, vmem, vmem),
        scratch_shapes=[
            pltpu.VMEM((blocks, both, BLK), BF16),
            pltpu.VMEM((WIDTH, BLK), BF16),
            pltpu.VMEM((WIDTH, BLK), BF16),
            pltpu.VMEM((blocks, BLK, both), BF16),
            pltpu.VMEM((blocks, HEADS, BLK, BLK), BF16),
            pltpu.VMEM((head_count * WIDTH, BLK), BF16),
            pltpu.VMEM((WIDTH, head_count * WIDTH), BF16),
            pltpu.VMEM((WIDTH, BLK), BF16),
            pltpu.VMEM((HEADS, 256, BLK), BF16),
            pltpu.VMEM((HEADS, 128, BLK), BF16),
            pltpu.VMEM((HEADS, 2 * BLK, 128), BF16),
            pltpu.VMEM((2, BLK, WIDE), F32),
            pltpu.VMEM((HEADS, BLK, 2 * BLK), BF16),
            pltpu.VMEM((WIDTH, BLK), F32),
            pltpu.VMEM((WIDTH, BLK), F32),
            pltpu.VMEM((blocks, HEADS, 8, BLK), F32),
            pltpu.VMEM((HEADS, 8, BLK), F32),
            pltpu.VMEM((HEADS, 8, BLK), F32),
            pltpu.VMEM((HEADS, 8, BLK), F32),
            pltpu.VMEM((blocks, BLK, both), BF16),
            pltpu.VMEM((2, BLK, both), BF16),
            pltpu.VMEM((2, BLK, both), BF16),
            pltpu.VMEM((BLK, both), BF16),
            pltpu.VMEM((HALF, both), BF16),
            pltpu.VMEM((HALF, both), BF16),
            pltpu.VMEM((HALF, both), BF16),
            pltpu.VMEM((HALF, both), BF16),
            pltpu.VMEM((BLK, both), BF16),
            pltpu.VMEM((4, WIDTH, WEIGHT_WIDTH), BF16),
            pltpu.VMEM((3, WIDTH, WEIGHT_WIDTH), BF16),
            pltpu.VMEM((WIDTH, WEIGHT_WIDTH), F32),
            pltpu.VMEM((8, 48, WEIGHT_WIDTH), BF16),
            pltpu.VMEM((7, 48, WEIGHT_WIDTH), BF16),
            dma((5,)),
            dma((12,)),
            dma((blocks,)),
            dma((blocks,)),
            dma((2,)),
            dma((4,)),
            dma((4,)),
            dma((9,)),
            dma((9,)),
            dma((3,)),
            dma((3,)),
            dma((7,)),
            dma((7,)),
        ],
        compiler_params=pltpu.CompilerParams(
            collective_id=0, has_side_effects=True, vmem_limit_bytes=60 << 20
        ),
    )(
        segment_units.reshape(1, -1),
        left_segments.reshape(1, -1),
        queries.T,
        key_rows.T,
        value_rows.T,
        cotangent.T,
        out_weight,
    )
    return (query_t.T, key_t.T, value_t.T, weight_t.T)


def solution(mesh):
    placed = (
        P("tm", "head"),
        P("tm", "head"),
        P("tm", "head"),
        P("tm", "head"),
        P("head", None),
        P(),
        P(),
    )
    return jax.shard_map(
        shards,
        mesh=mesh,
        in_specs=placed,
        out_specs=(P("tm", "head"), P("tm", "head"), P("tm", "head"), P("head", "tm")),
        check_vma=False,
    )
```

```python
import functools

import jax
import jax.numpy as jnp
from jax import lax
from jax.experimental import pallas as pl
from jax.experimental.pallas import tpu as pltpu
from jax.sharding import PartitionSpec as P

HS = 64
UNIT = 16
BLK = 512
HEADS = 5
WIDTH = HEADS * HS
BACK = 5
HALF = BLK // 2
WEIGHT_WIDTH = 384
STRIP = 128
WIDE = 256
HIDDEN = -2e30
LOWEST = -1e30
F32 = jnp.float32
BF16 = jnp.bfloat16
MESH = pl.DeviceIdType.MESH


def kernel(
    tm_count,
    head_count,
    units_ref,
    left_ref,
    q_hbm,
    k_hbm,
    v_hbm,
    cot_hbm,
    w_hbm,
    dq_ref,
    dw_ref,
    own_ref,
    home_near,
    home_far,
    edge,
    slots,
    relay,
    cross,
    kv_all,
    probs,
    cot_all,
    w_ref,
    q_ref,
    rhs,
    gt,
    rows,
    square,
    work,
    out_t,
    dq_t,
    m_all,
    m_run,
    l_run,
    delta,
    dkv,
    from_mate,
    sums,
    chain_in,
    relay_back,
    cross_back,
    wt,
    z_in,
    z_sum,
    pair_out,
    pair_in,
    y_out,
    y_in,
    local,
    sent,
    got_k,
    got_v,
    got_relay,
    side_sent,
    side_got,
    back_sent,
    back_got,
    z_sent,
    z_got,
    pair_sent,
    pair_got,
    y_sent,
    y_got,
):
    t = lax.axis_index("tm")
    x = lax.axis_index("head")
    core = t % 2
    z = t // 8
    y = (t // 2) % 4
    low = t % 8

    def at(place):
        return {"tm": (place + tm_count) % tm_count}

    def chip(z_place, y_place):
        return (((z_place + 4) % 4) * 4 + y_place % 4) * 2 + core

    mate = at(t + 1 - 2 * core)
    before, after = chip(z, y + 3), chip(z, y + 1)
    inner = jnp.where((y == 1) | (y == 2), 1, 0)
    relay_to = chip(z + jnp.where(y >= 2, 1, 0), y + 3)
    relay_from = chip(z - inner, y + 1)
    back_to = chip(z - jnp.where(y < 2, 1, 0), y + 1)
    back_from = chip(z + inner, y + 3)

    greeted = [at(t - 2), at(t + 2), at(relay_from), at(back_from)]
    greeted += [{"head": (x + head_count + by) % head_count} for by in (-1, 1)]
    greeted += [at(t - 8 * i) for i in range(1, 4)]
    greeted += [at(8 * z + (low + 8 - i) % 8) for i in range(1, 8)]
    barrier = pltpu.get_barrier_semaphore()
    for target in greeted:
        pl.semaphore_signal(barrier, inc=1, device_id=target, device_id_type=MESH)
    edge_source = at(t + 5 * (2 * core - 1))
    pl.semaphore_signal(barrier, inc=1, device_id=edge_source, device_id_type=MESH)

    loads = [
        pltpu.make_async_copy(k_hbm, slots.at[0, 0:WIDTH], local.at[0]),
        pltpu.make_async_copy(v_hbm, slots.at[0, WIDTH : 2 * WIDTH], local.at[1]),
        pltpu.make_async_copy(q_hbm, q_ref, local.at[2]),
        pltpu.make_async_copy(
            cot_hbm, cot_all.at[pl.ds(pl.multiple_of(WIDTH * x, 64), WIDTH)], local.at[3]
        ),
        pltpu.make_async_copy(w_hbm, w_ref, local.at[4]),
    ]
    for load in loads:
        load.start()
    pl.semaphore_wait(barrier, len(greeted) + 1)

    def push(src, dst, send_sem, recv_sem, target):
        return pltpu.make_async_remote_copy(
            src_ref=src,
            dst_ref=dst,
            send_sem=send_sem,
            recv_sem=recv_sem,
            device_id=target,
            device_id_type=MESH,
        )

    def keys(src, slot, number, target):
        return push(src, slots.at[slot, 0:WIDTH], sent.at[number], got_k.at[slot], target)

    def values(src, slot, number, target):
        return push(
            src, slots.at[slot, WIDTH : 2 * WIDTH], sent.at[number], got_v.at[slot], target
        )

    def key_part(slot):
        return slots.at[slot, 0:WIDTH]

    def value_part(slot):
        return slots.at[slot, WIDTH : 2 * WIDTH]

    near_k = keys(k_hbm, 2, 0, at(t + 2))
    near_v = values(v_hbm, 2, 1, at(t + 2))
    over_first = push(v_hbm, cross, sent.at[1], got_relay.at[1], at(t + 8))
    over_second = values(cross, 2, 11, at(t - 6))
    relay_first = push(v_hbm, relay, sent.at[2], got_relay.at[0], at(relay_to))
    near_k.start()
    relay_first.start()
    def cot_rows(place, first, count):
        start = WIDTH * (place % head_count) + first
        return cot_all.at[pl.ds(pl.multiple_of(start, 32), count)]

    def aside(src, rows_there, number, by):
        place = {"head": (x + head_count + by) % head_count}
        return push(src, rows_there, side_sent.at[number], side_got.at[number], place)

    own_cot = cot_rows(x, 0, WIDTH)
    upper = cot_rows(x + head_count - 1, 0, WIDTH // 2)
    lower = cot_rows(x + 1, WIDTH // 2, WIDTH // 2)
    beside = [aside(cot_hbm, own_cot, 0, 1), aside(cot_hbm, own_cot, 1, -1)]
    opposite = [aside(upper, upper, 2, 1), aside(lower, lower, 3, -1)]
    for copy in beside:
        copy.start()

    @pl.when(y < 3)
    def _():
        near_v.start()

    @pl.when(y == 3)
    def _():
        over_first.start()

    direct_slot = 1 + 4 * core
    direct_to = at(t + 1 + 4 * core)
    direct_k = keys(k_hbm, direct_slot, 3, direct_to)
    direct_v = values(v_hbm, direct_slot, 4, direct_to)

    @pl.when(core == 0)
    def _():
        direct_k.start()
        direct_v.start()

    chain_k = keys(key_part(2), 4, 5, at(t + 2))
    relay_second = values(relay, 4, 6, at(before))
    pass_near = 3 - 2 * core
    pass_far = 5 - 2 * core
    pass_near_k = keys(key_part(2), pass_near, 7, mate)
    pass_near_v = values(value_part(2), pass_near, 8, mate)
    pass_far_k = keys(key_part(4), pass_far, 9, mate)
    pass_far_v = values(value_part(4), pass_far, 10, mate)

    segments = units_ref.shape[1]
    units = jnp.broadcast_to(units_ref[...].astype(F32), (8, segments)).astype(BF16)
    lefts = jnp.broadcast_to(left_ref[...].astype(F32), (8, segments)).astype(BF16)
    down = lax.broadcasted_iota(jnp.int32, (segments, 128), 0)
    over = lax.broadcasted_iota(jnp.int32, (segments, 128), 1)
    until = jnp.where(down <= over, 1.0, 0.0).astype(BF16)
    ahead = jnp.where(down < over, 1.0, 0.0).astype(BF16)
    same = jnp.where(down == over, 1.0, 0.0).astype(BF16)
    end_row = jnp.dot(units, until, preferred_element_type=F32)[0:1, :] * UNIT
    start_row = jnp.dot(units, ahead, preferred_element_type=F32)[0:1, :] * UNIT
    columns = (((0,), (1,)), ((), ()))
    end_col = lax.dot_general(until, units, columns, preferred_element_type=F32)[:, 0:1] * UNIT
    left_col = lax.dot_general(same, lefts, columns, preferred_element_type=F32)[:, 0:1]
    frame_row = (t * BLK + lax.broadcasted_iota(jnp.int32, (1, BLK), 1)).astype(F32)
    own_seg = jnp.sum(jnp.where(end_col <= frame_row, 1.0, 0.0), axis=0, keepdims=True)
    seg_down = lax.broadcasted_iota(jnp.int32, (128, BLK), 0).astype(F32)
    reach = jnp.sum(jnp.where(seg_down == own_seg, left_col, 0.0), axis=0, keepdims=True)
    lowest = jnp.maximum(own_seg - reach, 0.0)
    bias = jnp.where((seg_down >= lowest) & (seg_down <= own_seg), 0.0, HIDDEN).astype(BF16)

    blank = jnp.zeros((HS, BLK), BF16)
    lane = lax.broadcasted_iota(jnp.int32, (BLK, 128), 1)

    def spread(j, upright, transposed):
        g, half = divmod(j, 2)
        both = [transposed, blank] if half == 0 else [blank, transposed]
        if j < HEADS:
            rhs[j] = jnp.concatenate(both + [bias], axis=0)
        else:
            gt[j - HEADS] = jnp.concatenate(both, axis=0)
        zeros = jnp.zeros((BLK, HS), BF16)
        pair = [upright, zeros] if half == 0 else [zeros, upright]
        rows[g, BLK * half : BLK * (half + 1), :] = jnp.concatenate(pair, axis=1)

    loads[2].wait()
    queries_t = (q_ref[...].astype(F32) * HS**-0.5).astype(BF16)
    for j in range(HEADS):
        mine = queries_t[HS * j : HS * (j + 1), :]
        spread(j, mine.T, mine)
    m_run[...] = jnp.full(m_run.shape, LOWEST, F32)
    l_run[...] = jnp.zeros(l_run.shape, F32)
    out_t[...] = jnp.zeros(out_t.shape, F32)
    dq_t[...] = jnp.zeros(dq_t.shape, F32)
    loads[0].wait()
    loads[1].wait()

    def wait_slot(slot):
        keys(k_hbm, slot, 0, mate).wait_recv()
        values(v_hbm, slot, 1, mate).wait_recv()

    def near_event():
        relay_first.wait_recv()
        relay_second.start()

        near_k.wait_recv()
        chain_k.start()
        pass_near_k.start()
        for arrived, onward in zip(beside, opposite):
            arrived.wait_recv()
            onward.start()
        near_v.wait_recv()
        pass_near_v.start()

    def forward(step, carry):
        @pl.when((step == 1) & (core == 1))
        def _():
            direct_k.start()
            direct_v.start()

        @pl.when((step == 1) & (y == 3))
        def _():
            over_first.wait_recv()
            over_second.start()

        swapped = jnp.where(step == 0, 0, jnp.where(step < 3, 3 - step, 8 - step))
        slot = jnp.where(core == 0, swapped, step)

        @pl.when(step == 1 + core)
        def _():
            near_event()

        @pl.when((step == 2 - core) | (step == 3) | (step == 5))
        def _():
            wait_slot(slot)

        @pl.when(step == 4)
        def _():
            loads[3].wait()
            loads[4].wait()
            for copy in opposite:
                copy.wait_recv()
            grad_t = jnp.dot(w_ref[...], cot_all[...], preferred_element_type=F32).astype(BF16)
            for j in range(HEADS):
                mine = grad_t[HS * j : HS * (j + 1), :]
                spread(j + HEADS, mine.T, mine)

        @pl.when(step == 4)
        def _():
            keys(k_hbm, 4, 0, mate).wait_recv()
            pass_far_k.start()
            values(v_hbm, 4, 1, mate).wait_recv()
            pass_far_v.start()

        def upright(g):
            group = slice(128 * g, 128 * (g + 1))
            kv_all[slot, :, group] = slots[slot, group, :].T

        first = ((t + tm_count - slot) % tm_count) * BLK
        frames = (first + lax.broadcasted_iota(jnp.int32, (BLK, 128), 0)).astype(F32)
        hot = jnp.where((frames >= start_row) & (frames < end_row), 1.0, 0.0).astype(BF16)
        upright(0)
        pieces = BLK // WIDE
        units_of = HEADS * pieces
        top = None
        for turn in range(units_of + 1):
            last = top
            if turn < units_of:
                h, c = divmod(turn, pieces)
                cols = slice(WIDE * c, WIDE * (c + 1))
                g = h // 2
                lhs = jnp.concatenate([kv_all[slot, :, 128 * g : 128 * (g + 1)], hot], axis=1)
                scores = jnp.dot(lhs, rhs[h, :, cols], preferred_element_type=F32)
                square[turn % 2] = scores
                top = jnp.max(scores.reshape(BLK // 8, 8, WIDE), axis=0)
                if turn < HEADS - 1:
                    upright(turn + 1)
            if turn == 0:
                continue
            h, c = divmod(turn - 1, pieces)
            cols = slice(WIDE * c, WIDE * (c + 1))
            m_old = m_run[h, 0:1, cols]
            m_new = jnp.maximum(m_old, jnp.max(last, axis=0, keepdims=True))
            factor = jnp.exp(m_old - m_new)
            m_run[h, 0:1, cols] = m_new
            m_all[slot, h, 0:1, cols] = m_new
            total = l_run[h, :, cols] * factor
            for r in range(0, BLK, STRIP):
                p = jnp.exp(square[(turn - 1) % 2, r : r + STRIP, :] - m_new)
                total = total + jnp.sum(p.reshape(STRIP // 8, 8, WIDE), axis=0)
                probs[slot, h, r : r + STRIP, cols] = p.astype(BF16)
            l_run[h, :, cols] = total
            here = slice(HS * h, HS * (h + 1))
            out_t[here, cols] = out_t[here, cols] * factor + jnp.dot(
                slots[slot, WIDTH + HS * h : WIDTH + HS * (h + 1), :],
                probs[slot, h, :, cols],
                preferred_element_type=F32,
            )
        return carry

    lax.fori_loop(0, BACK + 1, forward, 0)

    for h in range(HEADS):
        here = slice(HS * h, HS * (h + 1))
        total = jnp.sum(l_run[h], axis=0, keepdims=True)
        out = out_t[here, :] / total
        out_t[here, :] = out
        side = HS * ((h + HEADS) % 2)
        own_grad = gt[h, side : side + HS, :].astype(F32)
        delta[h, 0:1, :] = jnp.sum(out * own_grad, axis=0, keepdims=True)
        l_run[h, 0:1, :] = m_run[h, 0:1, :] + jnp.log(total)

    z_copies = [
        push(
            wt.at[(z + i) % 4], z_in.at[i - 1], z_sent.at[i - 1], z_got.at[i - 1], at(t + 8 * i)
        )
        for i in range(1, 4)
    ]
    attn = jnp.concatenate(
        [out_t[...].T.astype(BF16), jnp.zeros((BLK, WEIGHT_WIDTH - WIDTH), BF16)], axis=1
    )
    for part in range(4):
        piece = slice(WIDTH * part, WIDTH * (part + 1))
        wt[part] = jnp.dot(cot_all[piece, :], attn, preferred_element_type=F32).astype(BF16)
    for copy in z_copies:
        copy.start()
    pair_copy = push(pair_out, pair_in, pair_sent.at[0], pair_got.at[0], mate)
    y_copies = [
        push(
            y_out.at[(y + i) % 4],
            y_in.at[i - 1],
            y_sent.at[i - 1],
            y_got.at[i - 1],
            at(chip(z, y + i)),
        )
        for i in range(1, 4)
    ]

    def weight_rows(ring_place, parity):
        first = pl.multiple_of(80 * ring_place + 40 * parity, 8)
        block = z_sum[pl.ds(first, 40), :]
        return jnp.concatenate([block, jnp.zeros((8, WEIGHT_WIDTH), F32)], axis=0)

    far_slot, near_slot, edge_slot = 3 + 2 * core, 1 + 2 * core, 5 - 4 * core
    to_far = push(dkv.at[far_slot], from_mate.at[0], back_sent.at[0], back_got.at[0], mate)
    to_near = push(dkv.at[near_slot], from_mate.at[1], back_sent.at[1], back_got.at[1], mate)
    chain = push(sums.at[0, 0:HALF], chain_in, back_sent.at[2], back_got.at[2], at(t - 2))
    back_first = push(
        sums.at[0, HALF:BLK], relay_back, back_sent.at[3], back_got.at[3], at(back_to)
    )
    back_second = push(relay_back, home_far, back_sent.at[4], back_got.at[4], at(after))
    home_a = push(
        sums.at[1, 0:HALF], home_near.at[0:HALF], back_sent.at[5], back_got.at[5], at(t - 2)
    )
    home_b = push(
        sums.at[1, HALF:BLK], home_near.at[HALF:BLK], back_sent.at[7], back_got.at[7], at(t - 2)
    )
    over_back = push(sums.at[1, HALF:BLK], cross_back, back_sent.at[7], back_got.at[8], at(t - 8))
    over_home = push(
        cross_back, home_near.at[HALF:BLK], back_sent.at[8], back_got.at[7], at(t + 6)
    )
    edge_to = at(t - 5 + 4 * core)
    edge_copy = push(dkv.at[edge_slot], edge, back_sent.at[6], back_got.at[6], edge_to)

    def backward(step, carry):
        crossed = jnp.where(
            step < 2, 3 + step, jnp.where(step < 4, step - 1, jnp.where(step == 4, 5, 0))
        )
        slot = jnp.where(core == 0, crossed, 5 - step)
        pieces = BLK // WIDE
        units_of = HEADS * pieces
        for turn in range(units_of + 1):
            if turn < units_of:
                h, c = divmod(turn, pieces)
                g = (h + HEADS) // 2
                square[turn % 2] = jnp.dot(
                    kv_all[slot, :, 128 * g : 128 * (g + 1)],
                    gt[h, :, WIDE * c : WIDE * (c + 1)],
                    preferred_element_type=F32,
                )
            if turn == 0:
                continue
            h, c = divmod(turn - 1, pieces)
            cols = slice(WIDE * c, WIDE * (c + 1))
            scale = jnp.exp(m_all[slot, h, 0:1, cols] - l_run[h, 0:1, cols])
            shift = delta[h, 0:1, cols]
            ds_at = BLK * (h % 2) + WIDE * c
            p_at = BLK * ((h + HEADS) % 2) + WIDE * c
            for r in range(0, BLK, STRIP):
                down = slice(r, r + STRIP)
                p = probs[slot, h, down, cols].astype(F32) * scale
                ds = p * (square[(turn - 1) % 2, down, :] - shift)
                work[h // 2, down, ds_at : ds_at + WIDE] = ds.astype(BF16)
                work[(h + HEADS) // 2, down, p_at : p_at + WIDE] = p.astype(BF16)
            here = slice(HS * h, HS * (h + 1))
            dq_t[here, cols] += jnp.dot(
                slots[slot, here, :],
                work[h // 2, :, ds_at : ds_at + WIDE],
                preferred_element_type=F32,
            )
            if c < pieces - 1:
                continue
            for g in ((), (0,), (3,), (1,), (2, 4))[h]:
                dkv[slot, :, 128 * g : 128 * (g + 1)] = jnp.dot(
                    work[g], rows[g], preferred_element_type=F32
                ).astype(BF16)

        @pl.when(step == 0)
        def _():
            to_far.start()

        @pl.when(step == 1)
        def _():
            to_far.wait_recv()
            sums[0] = (dkv[4].astype(F32) + from_mate[0].astype(F32)).astype(BF16)
            chain.start()
            back_first.start()

        @pl.when(step == 2)
        def _():
            to_near.start()

        @pl.when(step == 3)
        def _():
            to_near.wait_recv()
            both = dkv[2].astype(F32) + from_mate[1].astype(F32)
            chain.wait_recv()
            sums[1, 0:HALF] = (both[0:HALF] + chain_in[...].astype(F32)).astype(BF16)
            sums[1, HALF:BLK] = both[HALF:BLK].astype(BF16)
            home_a.start()

            @pl.when(y > 0)
            def _():
                home_b.start()

            @pl.when(y == 0)
            def _():
                over_back.start()

            back_first.wait_recv()
            back_second.start()
            for copy in z_copies:
                copy.wait_recv()
            z_sum[...] = wt[z].astype(F32)
            for i in range(3):
                z_sum[...] += z_in[i].astype(F32)
            for i in range(4):
                pair_out[i] = weight_rows(i, 1 - core).astype(BF16)
            pair_copy.start()

        @pl.when(step == 4)
        def _():
            edge_copy.start()
            pair_copy.wait_recv()
            for i in range(4):
                y_out[i] = (weight_rows(i, core) + pair_in[i].astype(F32)).astype(BF16)
            for copy in y_copies:
                copy.start()

            @pl.when(y == 0)
            def _():
                over_back.wait_recv()
                over_home.start()

        return carry

    lax.fori_loop(0, BACK + 1, backward, 0)

    keep = pltpu.make_async_copy(dkv.at[0], own_ref, local.at[0])
    keep.start()
    dq_ref[...] = (dq_t[...] * HS**-0.5).astype(BF16)
    total = weight_rows(y, core) + pair_in[y].astype(F32)
    for i, copy in enumerate(y_copies):
        copy.wait_recv()
        total = total + y_in[i].astype(F32)
    dw_ref[...] = total
    for copy in [edge_copy, home_a, home_b, back_second, keep]:
        if copy is keep:
            copy.wait()
        else:
            copy.wait_recv()

    copies = [near_k, near_v, relay_first, direct_k, direct_v, chain_k, relay_second]
    copies += [pass_near_k, pass_near_v, pass_far_k, pass_far_v]
    copies += [to_far, to_near, chain, back_first, back_second, home_a, home_b, edge_copy]
    for copy in beside + opposite + copies + z_copies + y_copies + [pair_copy]:
        copy.wait_send()

    @pl.when(y == 3)
    def _():
        over_second.wait_send()

    @pl.when(y == 0)
    def _():
        over_home.wait_send()


def finish_kernel(dq, dw, own, near, far, edge, dq_ref, dk_ref, dv_ref, dw_ref):
    dq_ref[...] = dq[...]
    dw_ref[...] = dw[0:40, :WIDTH]
    for half in range(2):
        part = slice(HALF * half, HALF * (half + 1))
        total = own[part].astype(F32) + edge[part].astype(F32) + near[part].astype(F32)
        if half == 1:
            total = total + far[...].astype(F32)
        total_t = total.T.astype(BF16)
        dk_ref[:, part] = total_t[:WIDTH]
        dv_ref[:, part] = total_t[WIDTH:]


def shards(queries, key_rows, value_rows, cotangent, out_weight, segment_units, left_segments):
    tm_count = lax.axis_size("tm")
    head_count = lax.axis_size("head")
    anywhere = pl.BlockSpec(memory_space=pl.ANY)
    vmem = pl.BlockSpec(memory_space=pltpu.VMEM)
    dma = pltpu.SemaphoreType.DMA
    out_t = jax.ShapeDtypeStruct((WIDTH, BLK), BF16)
    both = 2 * WIDTH
    blocks = BACK + 1
    block = jax.ShapeDtypeStruct((BLK, both), BF16)
    pieces = pl.pallas_call(
        functools.partial(kernel, tm_count, head_count),
        out_shape=(
            out_t,
            jax.ShapeDtypeStruct((48, WEIGHT_WIDTH), F32),
            block,
            block,
            jax.ShapeDtypeStruct((HALF, both), BF16),
            block,
        ),
        in_specs=[vmem] * 2 + [anywhere] * 5,
        out_specs=(vmem, vmem, anywhere, anywhere, anywhere, anywhere),
        scratch_shapes=[
            pltpu.VMEM((blocks, both, BLK), BF16),
            pltpu.VMEM((WIDTH, BLK), BF16),
            pltpu.VMEM((WIDTH, BLK), BF16),
            pltpu.VMEM((blocks, BLK, both), BF16),
            pltpu.VMEM((blocks, HEADS, BLK, BLK), BF16),
            pltpu.VMEM((head_count * WIDTH, BLK), BF16),
            pltpu.VMEM((WIDTH, head_count * WIDTH), BF16),
            pltpu.VMEM((WIDTH, BLK), BF16),
            pltpu.VMEM((HEADS, 256, BLK), BF16),
            pltpu.VMEM((HEADS, 128, BLK), BF16),
            pltpu.VMEM((HEADS, 2 * BLK, 128), BF16),
            pltpu.VMEM((2, BLK, WIDE), F32),
            pltpu.VMEM((HEADS, BLK, 2 * BLK), BF16),
            pltpu.VMEM((WIDTH, BLK), F32),
            pltpu.VMEM((WIDTH, BLK), F32),
            pltpu.VMEM((blocks, HEADS, 8, BLK), F32),
            pltpu.VMEM((HEADS, 8, BLK), F32),
            pltpu.VMEM((HEADS, 8, BLK), F32),
            pltpu.VMEM((HEADS, 8, BLK), F32),
            pltpu.VMEM((blocks, BLK, both), BF16),
            pltpu.VMEM((2, BLK, both), BF16),
            pltpu.VMEM((2, BLK, both), BF16),
            pltpu.VMEM((HALF, both), BF16),
            pltpu.VMEM((HALF, both), BF16),
            pltpu.VMEM((HALF, both), BF16),
            pltpu.VMEM((4, WIDTH, WEIGHT_WIDTH), BF16),
            pltpu.VMEM((3, WIDTH, WEIGHT_WIDTH), BF16),
            pltpu.VMEM((WIDTH, WEIGHT_WIDTH), F32),
            pltpu.VMEM((4, 48, WEIGHT_WIDTH), BF16),
            pltpu.VMEM((4, 48, WEIGHT_WIDTH), BF16),
            pltpu.VMEM((4, 48, WEIGHT_WIDTH), BF16),
            pltpu.VMEM((3, 48, WEIGHT_WIDTH), BF16),
            dma((5,)),
            dma((12,)),
            dma((blocks,)),
            dma((blocks,)),
            dma((2,)),
            dma((4,)),
            dma((4,)),
            dma((9,)),
            dma((9,)),
            dma((3,)),
            dma((3,)),
            dma((1,)),
            dma((1,)),
            dma((3,)),
            dma((3,)),
        ],
        compiler_params=pltpu.CompilerParams(
            collective_id=0, has_side_effects=True, vmem_limit_bytes=60 << 20
        ),
    )(
        segment_units.reshape(1, -1),
        left_segments.reshape(1, -1),
        queries.T,
        key_rows.T,
        value_rows.T,
        cotangent.T,
        out_weight,
    )
    query_t, key_t, value_t, weight_t = pl.pallas_call(
        finish_kernel,
        out_shape=(out_t, out_t, out_t, jax.ShapeDtypeStruct((40, WIDTH), F32)),
        in_specs=[vmem] * 6,
        out_specs=(vmem, vmem, vmem, vmem),
        compiler_params=pltpu.CompilerParams(vmem_limit_bytes=24 << 20),
    )(*pieces)
    return (query_t.T, key_t.T, value_t.T, weight_t.T)


def solution(mesh):
    placed = (
        P("tm", "head"),
        P("tm", "head"),
        P("tm", "head"),
        P("tm", "head"),
        P("head", None),
        P(),
        P(),
    )
    return jax.shard_map(
        shards,
        mesh=mesh,
        in_specs=placed,
        out_specs=(P("tm", "head"), P("tm", "head"), P("tm", "head"), P("head", "tm")),
        check_vma=False,
    )
```

```python
import functools

import jax
import jax.numpy as jnp
from jax import lax
from jax.experimental import pallas as pl
from jax.experimental.pallas import tpu as pltpu
from jax.sharding import PartitionSpec as P

HS = 64
UNIT = 16
BLK = 512
HEADS = 5
WIDTH = HEADS * HS
BACK = 5
HALF = BLK // 2
WEIGHT_WIDTH = 384
STRIP = 128
WIDE = 256
HIDDEN = -2e30
LOWEST = -1e30
F32 = jnp.float32
BF16 = jnp.bfloat16
MESH = pl.DeviceIdType.MESH


def kernel(
    tm_count,
    head_count,
    units_ref,
    left_ref,
    q_hbm,
    k_hbm,
    v_hbm,
    cot_hbm,
    w_hbm,
    dq_ref,
    dw_ref,
    own_ref,
    home_near,
    home_far,
    edge,
    slots,
    relay,
    cross,
    kv_all,
    probs,
    cot_all,
    w_ref,
    q_ref,
    rhs,
    gt,
    rows,
    square,
    work,
    out_t,
    dq_t,
    m_all,
    m_run,
    l_run,
    delta,
    dkv,
    from_mate,
    sums,
    chain_in,
    relay_back,
    cross_back,
    wt,
    z_in,
    z_sum,
    pair_out,
    pair_in,
    y_out,
    y_in,
    local,
    sent,
    got_k,
    got_v,
    got_relay,
    side_sent,
    side_got,
    back_sent,
    back_got,
    z_sent,
    z_got,
    pair_sent,
    pair_got,
    y_sent,
    y_got,
):
    t = lax.axis_index("tm")
    x = lax.axis_index("head")
    core = t % 2
    z = t // 8
    y = (t // 2) % 4
    low = t % 8

    def at(place):
        return {"tm": (place + tm_count) % tm_count}

    def chip(z_place, y_place):
        return (((z_place + 4) % 4) * 4 + y_place % 4) * 2 + core

    mate = at(t + 1 - 2 * core)
    before, after = chip(z, y + 3), chip(z, y + 1)
    inner = jnp.where((y == 1) | (y == 2), 1, 0)
    relay_to = chip(z + jnp.where(y >= 2, 1, 0), y + 3)
    relay_from = chip(z - inner, y + 1)
    back_to = chip(z - jnp.where(y < 2, 1, 0), y + 1)
    back_from = chip(z + inner, y + 3)

    greeted = [at(t - 2), at(t + 2), at(relay_from), at(back_from)]
    greeted += [{"head": (x + head_count + by) % head_count} for by in (-1, 1)]
    greeted += [at(t - 8 * i) for i in range(1, 4)]
    greeted += [at(8 * z + (low + 8 - i) % 8) for i in range(1, 8)]
    barrier = pltpu.get_barrier_semaphore()
    for target in greeted:
        pl.semaphore_signal(barrier, inc=1, device_id=target, device_id_type=MESH)
    edge_source = at(t + 5 * (2 * core - 1))
    pl.semaphore_signal(barrier, inc=1, device_id=edge_source, device_id_type=MESH)

    loads = [
        pltpu.make_async_copy(k_hbm, slots.at[0, 0:WIDTH], local.at[0]),
        pltpu.make_async_copy(v_hbm, slots.at[0, WIDTH : 2 * WIDTH], local.at[1]),
        pltpu.make_async_copy(q_hbm, q_ref, local.at[2]),
        pltpu.make_async_copy(
            cot_hbm, cot_all.at[pl.ds(pl.multiple_of(WIDTH * x, 64), WIDTH)], local.at[3]
        ),
        pltpu.make_async_copy(w_hbm, w_ref, local.at[4]),
    ]
    for load in loads:
        load.start()
    pl.semaphore_wait(barrier, len(greeted) + 1)

    def push(src, dst, send_sem, recv_sem, target):
        return pltpu.make_async_remote_copy(
            src_ref=src,
            dst_ref=dst,
            send_sem=send_sem,
            recv_sem=recv_sem,
            device_id=target,
            device_id_type=MESH,
        )

    def keys(src, slot, number, target):
        return push(src, slots.at[slot, 0:WIDTH], sent.at[number], got_k.at[slot], target)

    def values(src, slot, number, target):
        return push(
            src, slots.at[slot, WIDTH : 2 * WIDTH], sent.at[number], got_v.at[slot], target
        )

    def key_part(slot):
        return slots.at[slot, 0:WIDTH]

    def value_part(slot):
        return slots.at[slot, WIDTH : 2 * WIDTH]

    near_k = keys(k_hbm, 2, 0, at(t + 2))
    near_v = values(v_hbm, 2, 1, at(t + 2))
    over_first = push(v_hbm, cross, sent.at[1], got_relay.at[1], at(t + 8))
    over_second = values(cross, 2, 11, at(t - 6))
    relay_first = push(v_hbm, relay, sent.at[2], got_relay.at[0], at(relay_to))
    near_k.start()
    relay_first.start()
    def cot_rows(place, first, count):
        start = WIDTH * (place % head_count) + first
        return cot_all.at[pl.ds(pl.multiple_of(start, 32), count)]

    def aside(src, rows_there, number, by):
        place = {"head": (x + head_count + by) % head_count}
        return push(src, rows_there, side_sent.at[number], side_got.at[number], place)

    own_cot = cot_rows(x, 0, WIDTH)
    upper = cot_rows(x + head_count - 1, 0, WIDTH // 2)
    lower = cot_rows(x + 1, WIDTH // 2, WIDTH // 2)
    beside = [aside(cot_hbm, own_cot, 0, 1), aside(cot_hbm, own_cot, 1, -1)]
    opposite = [aside(upper, upper, 2, 1), aside(lower, lower, 3, -1)]
    for copy in beside:
        copy.start()

    @pl.when(y < 3)
    def _():
        near_v.start()

    @pl.when(y == 3)
    def _():
        over_first.start()

    direct_slot = 1 + 4 * core
    direct_to = at(t + 1 + 4 * core)
    direct_k = keys(k_hbm, direct_slot, 3, direct_to)
    direct_v = values(v_hbm, direct_slot, 4, direct_to)

    @pl.when(core == 0)
    def _():
        direct_k.start()
        direct_v.start()

    chain_k = keys(key_part(2), 4, 5, at(t + 2))
    relay_second = values(relay, 4, 6, at(before))
    pass_near = 3 - 2 * core
    pass_far = 5 - 2 * core
    pass_near_k = keys(key_part(2), pass_near, 7, mate)
    pass_near_v = values(value_part(2), pass_near, 8, mate)
    pass_far_k = keys(key_part(4), pass_far, 9, mate)
    pass_far_v = values(value_part(4), pass_far, 10, mate)

    segments = units_ref.shape[1]
    units = jnp.broadcast_to(units_ref[...].astype(F32), (8, segments)).astype(BF16)
    lefts = jnp.broadcast_to(left_ref[...].astype(F32), (8, segments)).astype(BF16)
    down = lax.broadcasted_iota(jnp.int32, (segments, 128), 0)
    over = lax.broadcasted_iota(jnp.int32, (segments, 128), 1)
    until = jnp.where(down <= over, 1.0, 0.0).astype(BF16)
    ahead = jnp.where(down < over, 1.0, 0.0).astype(BF16)
    same = jnp.where(down == over, 1.0, 0.0).astype(BF16)
    end_row = jnp.dot(units, until, preferred_element_type=F32)[0:1, :] * UNIT
    start_row = jnp.dot(units, ahead, preferred_element_type=F32)[0:1, :] * UNIT
    columns = (((0,), (1,)), ((), ()))
    end_col = lax.dot_general(until, units, columns, preferred_element_type=F32)[:, 0:1] * UNIT
    left_col = lax.dot_general(same, lefts, columns, preferred_element_type=F32)[:, 0:1]
    frame_row = (t * BLK + lax.broadcasted_iota(jnp.int32, (1, BLK), 1)).astype(F32)
    own_seg = jnp.sum(jnp.where(end_col <= frame_row, 1.0, 0.0), axis=0, keepdims=True)
    seg_down = lax.broadcasted_iota(jnp.int32, (128, BLK), 0).astype(F32)
    reach = jnp.sum(jnp.where(seg_down == own_seg, left_col, 0.0), axis=0, keepdims=True)
    lowest = jnp.maximum(own_seg - reach, 0.0)
    bias = jnp.where((seg_down >= lowest) & (seg_down <= own_seg), 0.0, HIDDEN).astype(BF16)

    blank = jnp.zeros((HS, BLK), BF16)
    lane = lax.broadcasted_iota(jnp.int32, (BLK, 128), 1)

    def spread(j, upright, transposed):
        g, half = divmod(j, 2)
        both = [transposed, blank] if half == 0 else [blank, transposed]
        if j < HEADS:
            rhs[j] = jnp.concatenate(both + [bias], axis=0)
        else:
            gt[j - HEADS] = jnp.concatenate(both, axis=0)
        zeros = jnp.zeros((BLK, HS), BF16)
        pair = [upright, zeros] if half == 0 else [zeros, upright]
        rows[g, BLK * half : BLK * (half + 1), :] = jnp.concatenate(pair, axis=1)

    loads[2].wait()
    queries_t = (q_ref[...].astype(F32) * HS**-0.5).astype(BF16)
    for j in range(HEADS):
        mine = queries_t[HS * j : HS * (j + 1), :]
        spread(j, mine.T, mine)
    m_run[...] = jnp.full(m_run.shape, LOWEST, F32)
    l_run[...] = jnp.zeros(l_run.shape, F32)
    out_t[...] = jnp.zeros(out_t.shape, F32)
    dq_t[...] = jnp.zeros(dq_t.shape, F32)
    loads[0].wait()
    loads[1].wait()

    def wait_slot(slot):
        keys(k_hbm, slot, 0, mate).wait_recv()
        values(v_hbm, slot, 1, mate).wait_recv()

    def near_event():
        relay_first.wait_recv()
        relay_second.start()

        near_k.wait_recv()
        chain_k.start()
        pass_near_k.start()
        for arrived, onward in zip(beside, opposite):
            arrived.wait_recv()
            onward.start()
        near_v.wait_recv()
        pass_near_v.start()

    def forward(step, carry):
        @pl.when((step == 1) & (core == 1))
        def _():
            direct_k.start()
            direct_v.start()

        @pl.when((step == 1) & (y == 3))
        def _():
            over_first.wait_recv()
            over_second.start()

        swapped = jnp.where(step == 0, 0, jnp.where(step < 3, 3 - step, 8 - step))
        slot = jnp.where(core == 0, swapped, step)

        @pl.when(step == 1 + core)
        def _():
            near_event()

        @pl.when((step == 2 - core) | (step == 3) | (step == 5))
        def _():
            wait_slot(slot)

        @pl.when(step == 4)
        def _():
            loads[3].wait()
            loads[4].wait()
            for copy in opposite:
                copy.wait_recv()
            grad_t = jnp.dot(w_ref[...], cot_all[...], preferred_element_type=F32).astype(BF16)
            for j in range(HEADS):
                mine = grad_t[HS * j : HS * (j + 1), :]
                spread(j + HEADS, mine.T, mine)

        @pl.when(step == 4)
        def _():
            keys(k_hbm, 4, 0, mate).wait_recv()
            pass_far_k.start()
            values(v_hbm, 4, 1, mate).wait_recv()
            pass_far_v.start()

        def upright(g):
            group = slice(128 * g, 128 * (g + 1))
            kv_all[slot, :, group] = slots[slot, group, :].T

        first = ((t + tm_count - slot) % tm_count) * BLK
        frames = (first + lax.broadcasted_iota(jnp.int32, (BLK, 128), 0)).astype(F32)
        hot = jnp.where((frames >= start_row) & (frames < end_row), 1.0, 0.0).astype(BF16)
        upright(0)
        pieces = BLK // WIDE
        units_of = HEADS * pieces
        top = None
        for turn in range(units_of + 1):
            last = top
            if turn < units_of:
                h, c = divmod(turn, pieces)
                cols = slice(WIDE * c, WIDE * (c + 1))
                g = h // 2
                lhs = jnp.concatenate([kv_all[slot, :, 128 * g : 128 * (g + 1)], hot], axis=1)
                scores = jnp.dot(lhs, rhs[h, :, cols], preferred_element_type=F32)
                square[turn % 2] = scores
                top = jnp.max(scores.reshape(BLK // 8, 8, WIDE), axis=0)
                if turn < HEADS - 1:
                    upright(turn + 1)
            if turn == 0:
                continue
            h, c = divmod(turn - 1, pieces)
            cols = slice(WIDE * c, WIDE * (c + 1))
            m_old = m_run[h, 0:1, cols]
            m_new = jnp.maximum(m_old, jnp.max(last, axis=0, keepdims=True))
            factor = jnp.exp(m_old - m_new)
            m_run[h, 0:1, cols] = m_new
            m_all[slot, h, 0:1, cols] = m_new
            total = l_run[h, :, cols] * factor
            for r in range(0, BLK, STRIP):
                p = jnp.exp(square[(turn - 1) % 2, r : r + STRIP, :] - m_new)
                total = total + jnp.sum(p.reshape(STRIP // 8, 8, WIDE), axis=0)
                probs[slot, h, r : r + STRIP, cols] = p.astype(BF16)
            l_run[h, :, cols] = total
            here = slice(HS * h, HS * (h + 1))
            out_t[here, cols] = out_t[here, cols] * factor + jnp.dot(
                slots[slot, WIDTH + HS * h : WIDTH + HS * (h + 1), :],
                probs[slot, h, :, cols],
                preferred_element_type=F32,
            )
        return carry

    lax.fori_loop(0, BACK + 1, forward, 0)

    for h in range(HEADS):
        here = slice(HS * h, HS * (h + 1))
        total = jnp.sum(l_run[h], axis=0, keepdims=True)
        out = out_t[here, :] / total
        out_t[here, :] = out
        side = HS * ((h + HEADS) % 2)
        own_grad = gt[h, side : side + HS, :].astype(F32)
        delta[h, 0:1, :] = jnp.sum(out * own_grad, axis=0, keepdims=True)
        l_run[h, 0:1, :] = m_run[h, 0:1, :] + jnp.log(total)

    z_copies = [
        push(
            wt.at[(z + i) % 4], z_in.at[i - 1], z_sent.at[i - 1], z_got.at[i - 1], at(t + 8 * i)
        )
        for i in range(1, 4)
    ]
    attn = jnp.concatenate(
        [out_t[...].T.astype(BF16), jnp.zeros((BLK, WEIGHT_WIDTH - WIDTH), BF16)], axis=1
    )
    for part in range(4):
        piece = slice(WIDTH * part, WIDTH * (part + 1))
        wt[part] = jnp.dot(cot_all[piece, :], attn, preferred_element_type=F32).astype(BF16)
    for copy in z_copies:
        copy.start()
    pair_copy = push(pair_out, pair_in, pair_sent.at[0], pair_got.at[0], mate)
    y_copies = [
        push(
            y_out.at[(y + i) % 4],
            y_in.at[i - 1],
            y_sent.at[i - 1],
            y_got.at[i - 1],
            at(chip(z, y + i)),
        )
        for i in range(1, 4)
    ]

    def weight_rows(ring_place, parity):
        first = pl.multiple_of(80 * ring_place + 40 * parity, 8)
        block = z_sum[pl.ds(first, 40), :]
        return jnp.concatenate([block, jnp.zeros((8, WEIGHT_WIDTH), F32)], axis=0)

    far_slot, near_slot, edge_slot = 3 + 2 * core, 1 + 2 * core, 5 - 4 * core
    to_far = push(dkv.at[far_slot], from_mate.at[0], back_sent.at[0], back_got.at[0], mate)
    to_near = push(dkv.at[near_slot], from_mate.at[1], back_sent.at[1], back_got.at[1], mate)
    chain = push(sums.at[0, 0:HALF], chain_in, back_sent.at[2], back_got.at[2], at(t - 2))
    back_first = push(
        sums.at[0, HALF:BLK], relay_back, back_sent.at[3], back_got.at[3], at(back_to)
    )
    back_second = push(relay_back, home_far, back_sent.at[4], back_got.at[4], at(after))
    home_a = push(
        sums.at[1, 0:HALF], home_near.at[0:HALF], back_sent.at[5], back_got.at[5], at(t - 2)
    )
    home_b = push(
        sums.at[1, HALF:BLK], home_near.at[HALF:BLK], back_sent.at[7], back_got.at[7], at(t - 2)
    )
    over_back = push(sums.at[1, HALF:BLK], cross_back, back_sent.at[7], back_got.at[8], at(t - 8))
    over_home = push(
        cross_back, home_near.at[HALF:BLK], back_sent.at[8], back_got.at[7], at(t + 6)
    )
    edge_to = at(t - 5 + 4 * core)
    edge_copy = push(dkv.at[edge_slot], edge, back_sent.at[6], back_got.at[6], edge_to)

    def backward(step, carry):
        crossed = jnp.where(
            step < 2, 3 + step, jnp.where(step < 4, step - 1, jnp.where(step == 4, 5, 0))
        )
        slot = jnp.where(core == 0, crossed, 5 - step)
        pieces = BLK // WIDE
        units_of = HEADS * pieces
        for turn in range(units_of + 1):
            if turn < units_of:
                h, c = divmod(turn, pieces)
                g = (h + HEADS) // 2
                square[turn % 2] = jnp.dot(
                    kv_all[slot, :, 128 * g : 128 * (g + 1)],
                    gt[h, :, WIDE * c : WIDE * (c + 1)],
                    preferred_element_type=F32,
                )
            if turn == 0:
                continue
            h, c = divmod(turn - 1, pieces)
            cols = slice(WIDE * c, WIDE * (c + 1))
            scale = jnp.exp(m_all[slot, h, 0:1, cols] - l_run[h, 0:1, cols])
            shift = delta[h, 0:1, cols]
            ds_at = BLK * (h % 2) + WIDE * c
            p_at = BLK * ((h + HEADS) % 2) + WIDE * c
            for r in range(0, BLK, STRIP):
                down = slice(r, r + STRIP)
                p = probs[slot, h, down, cols].astype(F32) * scale
                ds = p * (square[(turn - 1) % 2, down, :] - shift)
                work[h // 2, down, ds_at : ds_at + WIDE] = ds.astype(BF16)
                work[(h + HEADS) // 2, down, p_at : p_at + WIDE] = p.astype(BF16)
            here = slice(HS * h, HS * (h + 1))
            dq_t[here, cols] += jnp.dot(
                slots[slot, here, :],
                work[h // 2, :, ds_at : ds_at + WIDE],
                preferred_element_type=F32,
            )
            if c < pieces - 1:
                continue
            for g in ((), (0,), (3,), (1,), (2, 4))[h]:
                dkv[slot, :, 128 * g : 128 * (g + 1)] = jnp.dot(
                    work[g], rows[g], preferred_element_type=F32
                ).astype(BF16)

        @pl.when(step == 0)
        def _():
            to_far.start()

        @pl.when(step == 1)
        def _():
            to_far.wait_recv()
            sums[0] = (dkv[4].astype(F32) + from_mate[0].astype(F32)).astype(BF16)
            chain.start()
            back_first.start()

        @pl.when(step == 2)
        def _():
            to_near.start()

        @pl.when(step == 3)
        def _():
            to_near.wait_recv()
            both = dkv[2, HALF:BLK].astype(F32) + from_mate[1, HALF:BLK].astype(F32)
            sums[1, HALF:BLK] = both.astype(BF16)

            @pl.when(y > 0)
            def _():
                home_b.start()

            @pl.when(y == 0)
            def _():
                over_back.start()

            back_first.wait_recv()
            back_second.start()
            for copy in z_copies:
                copy.wait_recv()
            z_sum[...] = wt[z].astype(F32)
            for i in range(3):
                z_sum[...] += z_in[i].astype(F32)
            for i in range(4):
                pair_out[i] = weight_rows(i, 1 - core).astype(BF16)
            pair_copy.start()

        @pl.when(step == 4)
        def _():
            edge_copy.start()
            chain.wait_recv()
            near = dkv[2, 0:HALF].astype(F32) + from_mate[1, 0:HALF].astype(F32)
            sums[1, 0:HALF] = (near + chain_in[...].astype(F32)).astype(BF16)
            home_a.start()
            pair_copy.wait_recv()
            for i in range(4):
                y_out[i] = (weight_rows(i, core) + pair_in[i].astype(F32)).astype(BF16)
            for copy in y_copies:
                copy.start()

            @pl.when(y == 0)
            def _():
                over_back.wait_recv()
                over_home.start()

        return carry

    lax.fori_loop(0, BACK + 1, backward, 0)

    keep = pltpu.make_async_copy(dkv.at[0], own_ref, local.at[0])
    keep.start()
    dq_ref[...] = (dq_t[...] * HS**-0.5).astype(BF16)
    total = weight_rows(y, core) + pair_in[y].astype(F32)
    for i, copy in enumerate(y_copies):
        copy.wait_recv()
        total = total + y_in[i].astype(F32)
    dw_ref[...] = total[0:40, :WIDTH]
    for copy in [edge_copy, home_a, home_b, back_second, keep]:
        if copy is keep:
            copy.wait()
        else:
            copy.wait_recv()

    copies = [near_k, near_v, relay_first, direct_k, direct_v, chain_k, relay_second]
    copies += [pass_near_k, pass_near_v, pass_far_k, pass_far_v]
    copies += [to_far, to_near, chain, back_first, back_second, home_a, home_b, edge_copy]
    for copy in beside + opposite + copies + z_copies + y_copies + [pair_copy]:
        copy.wait_send()

    @pl.when(y == 3)
    def _():
        over_second.wait_send()

    @pl.when(y == 0)
    def _():
        over_home.wait_send()


def finish_kernel(
    dq, dw, own, near, far, edge, dq_ref, dk_ref, dv_ref, dw_ref, own_v, near_v, far_v, edge_v, sems
):
    pairs = ((own, own_v), (edge, edge_v), (near, near_v), (far, far_v), (dq, dq_ref), (dw, dw_ref))
    copies = [pltpu.make_async_copy(src, dst, sems.at[i]) for i, (src, dst) in enumerate(pairs)]
    for copy in copies:
        copy.start()
    for copy in copies[:4]:
        copy.wait()
    for half in range(2):
        part = slice(HALF * half, HALF * (half + 1))
        total = own_v[part].astype(F32) + edge_v[part].astype(F32) + near_v[part].astype(F32)
        if half == 1:
            total = total + far_v[...].astype(F32)
        total_t = total.T.astype(BF16)
        dk_ref[:, part] = total_t[:WIDTH]
        dv_ref[:, part] = total_t[WIDTH:]
    for copy in copies[4:]:
        copy.wait()


def shards(queries, key_rows, value_rows, cotangent, out_weight, segment_units, left_segments):
    tm_count = lax.axis_size("tm")
    head_count = lax.axis_size("head")
    anywhere = pl.BlockSpec(memory_space=pl.ANY)
    vmem = pl.BlockSpec(memory_space=pltpu.VMEM)
    dma = pltpu.SemaphoreType.DMA
    out_t = jax.ShapeDtypeStruct((WIDTH, BLK), BF16)
    both = 2 * WIDTH
    blocks = BACK + 1
    block = jax.ShapeDtypeStruct((BLK, both), BF16)
    pieces = pl.pallas_call(
        functools.partial(kernel, tm_count, head_count),
        out_shape=(
            out_t,
            jax.ShapeDtypeStruct((40, WIDTH), F32),
            block,
            block,
            jax.ShapeDtypeStruct((HALF, both), BF16),
            block,
        ),
        in_specs=[vmem] * 2 + [anywhere] * 5,
        out_specs=(vmem, vmem, anywhere, anywhere, anywhere, anywhere),
        scratch_shapes=[
            pltpu.VMEM((blocks, both, BLK), BF16),
            pltpu.VMEM((WIDTH, BLK), BF16),
            pltpu.VMEM((WIDTH, BLK), BF16),
            pltpu.VMEM((blocks, BLK, both), BF16),
            pltpu.VMEM((blocks, HEADS, BLK, BLK), BF16),
            pltpu.VMEM((head_count * WIDTH, BLK), BF16),
            pltpu.VMEM((WIDTH, head_count * WIDTH), BF16),
            pltpu.VMEM((WIDTH, BLK), BF16),
            pltpu.VMEM((HEADS, 256, BLK), BF16),
            pltpu.VMEM((HEADS, 128, BLK), BF16),
            pltpu.VMEM((HEADS, 2 * BLK, 128), BF16),
            pltpu.VMEM((2, BLK, WIDE), F32),
            pltpu.VMEM((HEADS, BLK, 2 * BLK), BF16),
            pltpu.VMEM((WIDTH, BLK), F32),
            pltpu.VMEM((WIDTH, BLK), F32),
            pltpu.VMEM((blocks, HEADS, 8, BLK), F32),
            pltpu.VMEM((HEADS, 8, BLK), F32),
            pltpu.VMEM((HEADS, 8, BLK), F32),
            pltpu.VMEM((HEADS, 8, BLK), F32),
            pltpu.VMEM((blocks, BLK, both), BF16),
            pltpu.VMEM((2, BLK, both), BF16),
            pltpu.VMEM((2, BLK, both), BF16),
            pltpu.VMEM((HALF, both), BF16),
            pltpu.VMEM((HALF, both), BF16),
            pltpu.VMEM((HALF, both), BF16),
            pltpu.VMEM((4, WIDTH, WEIGHT_WIDTH), BF16),
            pltpu.VMEM((3, WIDTH, WEIGHT_WIDTH), BF16),
            pltpu.VMEM((WIDTH, WEIGHT_WIDTH), F32),
            pltpu.VMEM((4, 48, WEIGHT_WIDTH), BF16),
            pltpu.VMEM((4, 48, WEIGHT_WIDTH), BF16),
            pltpu.VMEM((4, 48, WEIGHT_WIDTH), BF16),
            pltpu.VMEM((3, 48, WEIGHT_WIDTH), BF16),
            dma((5,)),
            dma((12,)),
            dma((blocks,)),
            dma((blocks,)),
            dma((2,)),
            dma((4,)),
            dma((4,)),
            dma((9,)),
            dma((9,)),
            dma((3,)),
            dma((3,)),
            dma((1,)),
            dma((1,)),
            dma((3,)),
            dma((3,)),
        ],
        compiler_params=pltpu.CompilerParams(
            collective_id=0, has_side_effects=True, vmem_limit_bytes=60 << 20
        ),
    )(
        segment_units.reshape(1, -1),
        left_segments.reshape(1, -1),
        queries.T,
        key_rows.T,
        value_rows.T,
        cotangent.T,
        out_weight,
    )
    query_t, key_t, value_t, weight_t = pl.pallas_call(
        finish_kernel,
        out_shape=(out_t, out_t, out_t, jax.ShapeDtypeStruct((40, WIDTH), F32)),
        in_specs=[anywhere] * 6,
        out_specs=(vmem, vmem, vmem, vmem),
        scratch_shapes=[
            pltpu.VMEM((BLK, both), BF16),
            pltpu.VMEM((BLK, both), BF16),
            pltpu.VMEM((HALF, both), BF16),
            pltpu.VMEM((BLK, both), BF16),
            dma((6,)),
        ],
        compiler_params=pltpu.CompilerParams(vmem_limit_bytes=60 << 20),
    )(*pieces)
    return (query_t.T, key_t.T, value_t.T, weight_t.T)


def solution(mesh):
    placed = (
        P("tm", "head"),
        P("tm", "head"),
        P("tm", "head"),
        P("tm", "head"),
        P("head", None),
        P(),
        P(),
    )
    return jax.shard_map(
        shards,
        mesh=mesh,
        in_specs=placed,
        out_specs=(P("tm", "head"), P("tm", "head"), P("tm", "head"), P("head", "tm")),
        check_vma=False,
    )
```

```python
import functools

import jax
import jax.numpy as jnp
from jax import lax
from jax.experimental import pallas as pl
from jax.experimental.pallas import tpu as pltpu
from jax.sharding import PartitionSpec as P

HS = 64
UNIT = 16
BLK = 512
HEADS = 5
WIDTH = HEADS * HS
BACK = 5
HALF = BLK // 2
WEIGHT_WIDTH = 384
STRIP = 128
WIDE = 512
HIDDEN = -2e30
LOWEST = -1e30
F32 = jnp.float32
BF16 = jnp.bfloat16
MESH = pl.DeviceIdType.MESH


def kernel(
    tm_count,
    head_count,
    units_ref,
    left_ref,
    q_hbm,
    k_hbm,
    v_hbm,
    cot_hbm,
    w_hbm,
    dq_ref,
    dw_ref,
    own_ref,
    home_near,
    home_far,
    edge,
    slots,
    relay,
    cross,
    kv_all,
    probs,
    cot_all,
    w_ref,
    q_ref,
    rhs,
    gt,
    rows,
    square,
    work,
    out_t,
    dq_t,
    m_all,
    m_run,
    l_run,
    delta,
    dkv,
    from_mate,
    sums,
    chain_in,
    relay_back,
    cross_back,
    wt,
    z_in,
    z_sum,
    pair_out,
    pair_in,
    y_out,
    y_in,
    local,
    sent,
    got_k,
    got_v,
    got_relay,
    side_sent,
    side_got,
    back_sent,
    back_got,
    z_sent,
    z_got,
    pair_sent,
    pair_got,
    y_sent,
    y_got,
):
    t = lax.axis_index("tm")
    x = lax.axis_index("head")
    core = t % 2
    z = t // 8
    y = (t // 2) % 4
    low = t % 8

    def at(place):
        return {"tm": (place + tm_count) % tm_count}

    def chip(z_place, y_place):
        return (((z_place + 4) % 4) * 4 + y_place % 4) * 2 + core

    mate = at(t + 1 - 2 * core)
    before, after = chip(z, y + 3), chip(z, y + 1)
    inner = jnp.where((y == 1) | (y == 2), 1, 0)
    relay_to = chip(z + jnp.where(y >= 2, 1, 0), y + 3)
    relay_from = chip(z - inner, y + 1)
    back_to = chip(z - jnp.where(y < 2, 1, 0), y + 1)
    back_from = chip(z + inner, y + 3)

    greeted = [at(t - 2), at(t + 2), at(relay_from), at(back_from)]
    greeted += [{"head": (x + head_count + by) % head_count} for by in (-1, 1)]
    greeted += [at(t - 8 * i) for i in range(1, 4)]
    greeted += [at(8 * z + (low + 8 - i) % 8) for i in range(1, 8)]
    barrier = pltpu.get_barrier_semaphore()
    for target in greeted:
        pl.semaphore_signal(barrier, inc=1, device_id=target, device_id_type=MESH)
    edge_source = at(t + 5 * (2 * core - 1))
    pl.semaphore_signal(barrier, inc=1, device_id=edge_source, device_id_type=MESH)

    loads = [
        pltpu.make_async_copy(k_hbm, slots.at[0, 0:WIDTH], local.at[0]),
        pltpu.make_async_copy(v_hbm, slots.at[0, WIDTH : 2 * WIDTH], local.at[1]),
        pltpu.make_async_copy(q_hbm, q_ref, local.at[2]),
        pltpu.make_async_copy(
            cot_hbm, cot_all.at[pl.ds(pl.multiple_of(WIDTH * x, 64), WIDTH)], local.at[3]
        ),
        pltpu.make_async_copy(w_hbm, w_ref, local.at[4]),
    ]
    for load in loads:
        load.start()
    pl.semaphore_wait(barrier, len(greeted) + 1)

    def push(src, dst, send_sem, recv_sem, target):
        return pltpu.make_async_remote_copy(
            src_ref=src,
            dst_ref=dst,
            send_sem=send_sem,
            recv_sem=recv_sem,
            device_id=target,
            device_id_type=MESH,
        )

    def keys(src, slot, number, target):
        return push(src, slots.at[slot, 0:WIDTH], sent.at[number], got_k.at[slot], target)

    def values(src, slot, number, target):
        return push(
            src, slots.at[slot, WIDTH : 2 * WIDTH], sent.at[number], got_v.at[slot], target
        )

    def key_part(slot):
        return slots.at[slot, 0:WIDTH]

    def value_part(slot):
        return slots.at[slot, WIDTH : 2 * WIDTH]

    near_k = keys(k_hbm, 2, 0, at(t + 2))
    near_v = values(v_hbm, 2, 1, at(t + 2))
    over_first = push(v_hbm, cross, sent.at[1], got_relay.at[1], at(t + 8))
    over_second = values(cross, 2, 11, at(t - 6))
    relay_first = push(v_hbm, relay, sent.at[2], got_relay.at[0], at(relay_to))
    near_k.start()
    relay_first.start()
    def cot_rows(place, first, count):
        start = WIDTH * (place % head_count) + first
        return cot_all.at[pl.ds(pl.multiple_of(start, 32), count)]

    def aside(src, rows_there, number, by):
        place = {"head": (x + head_count + by) % head_count}
        return push(src, rows_there, side_sent.at[number], side_got.at[number], place)

    own_cot = cot_rows(x, 0, WIDTH)
    upper = cot_rows(x + head_count - 1, 0, WIDTH // 2)
    lower = cot_rows(x + 1, WIDTH // 2, WIDTH // 2)
    beside = [aside(cot_hbm, own_cot, 0, 1), aside(cot_hbm, own_cot, 1, -1)]
    opposite = [aside(upper, upper, 2, 1), aside(lower, lower, 3, -1)]
    for copy in beside:
        copy.start()

    @pl.when(y < 3)
    def _():
        near_v.start()

    @pl.when(y == 3)
    def _():
        over_first.start()

    direct_slot = 1 + 4 * core
    direct_to = at(t + 1 + 4 * core)
    direct_k = keys(k_hbm, direct_slot, 3, direct_to)
    direct_v = values(v_hbm, direct_slot, 4, direct_to)

    @pl.when(core == 0)
    def _():
        direct_k.start()
        direct_v.start()

    chain_k = keys(key_part(2), 4, 5, at(t + 2))
    relay_second = values(relay, 4, 6, at(before))
    pass_near = 3 - 2 * core
    pass_far = 5 - 2 * core
    pass_near_k = keys(key_part(2), pass_near, 7, mate)
    pass_near_v = values(value_part(2), pass_near, 8, mate)
    pass_far_k = keys(key_part(4), pass_far, 9, mate)
    pass_far_v = values(value_part(4), pass_far, 10, mate)

    segments = units_ref.shape[1]
    units = jnp.broadcast_to(units_ref[...].astype(F32), (8, segments)).astype(BF16)
    lefts = jnp.broadcast_to(left_ref[...].astype(F32), (8, segments)).astype(BF16)
    down = lax.broadcasted_iota(jnp.int32, (segments, 128), 0)
    over = lax.broadcasted_iota(jnp.int32, (segments, 128), 1)
    until = jnp.where(down <= over, 1.0, 0.0).astype(BF16)
    ahead = jnp.where(down < over, 1.0, 0.0).astype(BF16)
    same = jnp.where(down == over, 1.0, 0.0).astype(BF16)
    end_row = jnp.dot(units, until, preferred_element_type=F32)[0:1, :] * UNIT
    start_row = jnp.dot(units, ahead, preferred_element_type=F32)[0:1, :] * UNIT
    columns = (((0,), (1,)), ((), ()))
    end_col = lax.dot_general(until, units, columns, preferred_element_type=F32)[:, 0:1] * UNIT
    left_col = lax.dot_general(same, lefts, columns, preferred_element_type=F32)[:, 0:1]
    frame_row = (t * BLK + lax.broadcasted_iota(jnp.int32, (1, BLK), 1)).astype(F32)
    own_seg = jnp.sum(jnp.where(end_col <= frame_row, 1.0, 0.0), axis=0, keepdims=True)
    seg_down = lax.broadcasted_iota(jnp.int32, (128, BLK), 0).astype(F32)
    reach = jnp.sum(jnp.where(seg_down == own_seg, left_col, 0.0), axis=0, keepdims=True)
    lowest = jnp.maximum(own_seg - reach, 0.0)
    bias = jnp.where((seg_down >= lowest) & (seg_down <= own_seg), 0.0, HIDDEN).astype(BF16)

    blank = jnp.zeros((HS, BLK), BF16)
    lane = lax.broadcasted_iota(jnp.int32, (BLK, 128), 1)

    def spread(j, upright, transposed):
        g, half = divmod(j, 2)
        both = [transposed, blank] if half == 0 else [blank, transposed]
        if j < HEADS:
            rhs[j] = jnp.concatenate(both + [bias], axis=0)
        else:
            gt[j - HEADS] = jnp.concatenate(both, axis=0)
        zeros = jnp.zeros((BLK, HS), BF16)
        pair = [upright, zeros] if half == 0 else [zeros, upright]
        rows[g, BLK * half : BLK * (half + 1), :] = jnp.concatenate(pair, axis=1)

    loads[2].wait()
    queries_t = (q_ref[...].astype(F32) * HS**-0.5).astype(BF16)
    for j in range(HEADS):
        mine = queries_t[HS * j : HS * (j + 1), :]
        spread(j, mine.T, mine)
    m_run[...] = jnp.full(m_run.shape, LOWEST, F32)
    l_run[...] = jnp.zeros(l_run.shape, F32)
    out_t[...] = jnp.zeros(out_t.shape, F32)
    dq_t[...] = jnp.zeros(dq_t.shape, F32)
    loads[0].wait()
    loads[1].wait()

    def wait_slot(slot):
        keys(k_hbm, slot, 0, mate).wait_recv()
        values(v_hbm, slot, 1, mate).wait_recv()

    def near_event():
        relay_first.wait_recv()
        relay_second.start()

        near_k.wait_recv()
        chain_k.start()
        pass_near_k.start()
        for arrived, onward in zip(beside, opposite):
            arrived.wait_recv()
            onward.start()
        near_v.wait_recv()
        pass_near_v.start()

    def forward(step, carry):
        @pl.when((step == 1) & (core == 1))
        def _():
            direct_k.start()
            direct_v.start()

        @pl.when((step == 1) & (y == 3))
        def _():
            over_first.wait_recv()
            over_second.start()

        swapped = jnp.where(step == 0, 0, jnp.where(step < 3, 3 - step, 8 - step))
        slot = jnp.where(core == 0, swapped, step)

        @pl.when(step == 1 + core)
        def _():
            near_event()

        @pl.when((step == 2 - core) | (step == 3) | (step == 5))
        def _():
            wait_slot(slot)

        @pl.when(step == 4)
        def _():
            loads[3].wait()
            loads[4].wait()
            for copy in opposite:
                copy.wait_recv()
            grad_t = jnp.dot(w_ref[...], cot_all[...], preferred_element_type=F32).astype(BF16)
            for j in range(HEADS):
                mine = grad_t[HS * j : HS * (j + 1), :]
                spread(j + HEADS, mine.T, mine)

        @pl.when(step == 4)
        def _():
            keys(k_hbm, 4, 0, mate).wait_recv()
            pass_far_k.start()
            values(v_hbm, 4, 1, mate).wait_recv()
            pass_far_v.start()

        def upright(g):
            group = slice(128 * g, 128 * (g + 1))
            kv_all[slot, :, group] = slots[slot, group, :].T

        first = ((t + tm_count - slot) % tm_count) * BLK
        frames = (first + lax.broadcasted_iota(jnp.int32, (BLK, 128), 0)).astype(F32)
        hot = jnp.where((frames >= start_row) & (frames < end_row), 1.0, 0.0).astype(BF16)
        upright(0)
        pieces = BLK // WIDE
        units_of = HEADS * pieces
        top = None
        late = []
        for turn in range(units_of + 1):
            last = top
            if turn < units_of:
                h, c = divmod(turn, pieces)
                cols = slice(WIDE * c, WIDE * (c + 1))
                g = h // 2
                lhs = jnp.concatenate([kv_all[slot, :, 128 * g : 128 * (g + 1)], hot], axis=1)
                scores = jnp.dot(lhs, rhs[h, :, cols], preferred_element_type=F32)
                square[turn % 2] = scores
                top = jnp.max(scores.reshape(BLK // 8, 8, WIDE), axis=0)
                if turn < HEADS - 1:
                    upright(turn + 1)
            if turn == 0:
                continue
            h, c = divmod(turn - 1, pieces)
            cols = slice(WIDE * c, WIDE * (c + 1))
            m_old = m_run[h, 0:1, cols]
            m_new = jnp.maximum(m_old, jnp.max(last, axis=0, keepdims=True))
            factor = jnp.exp(m_old - m_new)
            m_run[h, 0:1, cols] = m_new
            m_all[slot, h, 0:1, cols] = m_new
            total = l_run[h, :, cols] * factor
            for r in range(0, BLK, STRIP):
                p = jnp.exp(square[(turn - 1) % 2, r : r + STRIP, :] - m_new)
                total = total + jnp.sum(p.reshape(STRIP // 8, 8, WIDE), axis=0)
                probs[slot, h, r : r + STRIP, cols] = p.astype(BF16)
            l_run[h, :, cols] = total
            late.append((h, cols, factor))
            if turn < 2:
                continue
            for h, cols, factor in late[-2:] if turn == units_of else late[-2:-1]:
                here = slice(HS * h, HS * (h + 1))
                out_t[here, cols] = out_t[here, cols] * factor + jnp.dot(
                    slots[slot, WIDTH + HS * h : WIDTH + HS * (h + 1), :],
                    probs[slot, h, :, cols],
                    preferred_element_type=F32,
                )
        return carry

    lax.fori_loop(0, BACK + 1, forward, 0)

    for h in range(HEADS):
        here = slice(HS * h, HS * (h + 1))
        total = jnp.sum(l_run[h], axis=0, keepdims=True)
        out = out_t[here, :] / total
        out_t[here, :] = out
        side = HS * ((h + HEADS) % 2)
        own_grad = gt[h, side : side + HS, :].astype(F32)
        delta[h, 0:1, :] = jnp.sum(out * own_grad, axis=0, keepdims=True)
        l_run[h, 0:1, :] = m_run[h, 0:1, :] + jnp.log(total)

    z_copies = [
        push(
            wt.at[(z + i) % 4], z_in.at[i - 1], z_sent.at[i - 1], z_got.at[i - 1], at(t + 8 * i)
        )
        for i in range(1, 4)
    ]
    attn = jnp.concatenate(
        [out_t[...].T.astype(BF16), jnp.zeros((BLK, WEIGHT_WIDTH - WIDTH), BF16)], axis=1
    )
    for part in range(4):
        piece = slice(WIDTH * part, WIDTH * (part + 1))
        wt[part] = jnp.dot(cot_all[piece, :], attn, preferred_element_type=F32).astype(BF16)
    for copy in z_copies:
        copy.start()
    pair_copy = push(pair_out, pair_in, pair_sent.at[0], pair_got.at[0], mate)
    y_copies = [
        push(
            y_out.at[(y + i) % 4],
            y_in.at[i - 1],
            y_sent.at[i - 1],
            y_got.at[i - 1],
            at(chip(z, y + i)),
        )
        for i in range(1, 4)
    ]

    def weight_rows(ring_place, parity):
        first = pl.multiple_of(80 * ring_place + 40 * parity, 8)
        block = z_sum[pl.ds(first, 40), :]
        return jnp.concatenate([block, jnp.zeros((8, WEIGHT_WIDTH), F32)], axis=0)

    far_slot, near_slot, edge_slot = 3 + 2 * core, 1 + 2 * core, 5 - 4 * core
    to_far = push(dkv.at[far_slot], from_mate.at[0], back_sent.at[0], back_got.at[0], mate)
    to_near = push(dkv.at[near_slot], from_mate.at[1], back_sent.at[1], back_got.at[1], mate)
    chain = push(sums.at[0, 0:HALF], chain_in, back_sent.at[2], back_got.at[2], at(t - 2))
    back_first = push(
        sums.at[0, HALF:BLK], relay_back, back_sent.at[3], back_got.at[3], at(back_to)
    )
    back_second = push(relay_back, home_far, back_sent.at[4], back_got.at[4], at(after))
    home_a = push(
        sums.at[1, 0:HALF], home_near.at[0:HALF], back_sent.at[5], back_got.at[5], at(t - 2)
    )
    home_b = push(
        sums.at[1, HALF:BLK], home_near.at[HALF:BLK], back_sent.at[7], back_got.at[7], at(t - 2)
    )
    over_back = push(sums.at[1, HALF:BLK], cross_back, back_sent.at[7], back_got.at[8], at(t - 8))
    over_home = push(
        cross_back, home_near.at[HALF:BLK], back_sent.at[8], back_got.at[7], at(t + 6)
    )
    edge_to = at(t - 5 + 4 * core)
    edge_copy = push(dkv.at[edge_slot], edge, back_sent.at[6], back_got.at[6], edge_to)

    def backward(step, carry):
        crossed = jnp.where(
            step < 2, 3 + step, jnp.where(step < 4, step - 1, jnp.where(step == 4, 5, 0))
        )
        slot = jnp.where(core == 0, crossed, 5 - step)
        pieces = BLK // WIDE
        units_of = HEADS * pieces
        done = []
        for turn in range(units_of + 1):
            if turn < units_of:
                h, c = divmod(turn, pieces)
                g = (h + HEADS) // 2
                square[turn % 2] = jnp.dot(
                    kv_all[slot, :, 128 * g : 128 * (g + 1)],
                    gt[h, :, WIDE * c : WIDE * (c + 1)],
                    preferred_element_type=F32,
                )
            if turn == 0:
                continue
            h, c = divmod(turn - 1, pieces)
            cols = slice(WIDE * c, WIDE * (c + 1))
            scale = jnp.exp(m_all[slot, h, 0:1, cols] - l_run[h, 0:1, cols])
            shift = delta[h, 0:1, cols]
            ds_at = BLK * (h % 2) + WIDE * c
            p_at = BLK * ((h + HEADS) % 2) + WIDE * c
            for r in range(0, BLK, STRIP):
                down = slice(r, r + STRIP)
                p = probs[slot, h, down, cols].astype(F32) * scale
                ds = p * (square[(turn - 1) % 2, down, :] - shift)
                work[h // 2, down, ds_at : ds_at + WIDE] = ds.astype(BF16)
                work[(h + HEADS) // 2, down, p_at : p_at + WIDE] = p.astype(BF16)
            done.append(h)
            if turn < 2:
                continue
            for h in done[-2:] if turn == units_of else done[-2:-1]:
                here = slice(HS * h, HS * (h + 1))
                dq_t[here, :] += jnp.dot(
                    slots[slot, here, :],
                    work[h // 2, :, BLK * (h % 2) : BLK * (h % 2 + 1)],
                    preferred_element_type=F32,
                )
                for g in ((), (0,), (3,), (1,), (2, 4))[h]:
                    dkv[slot, :, 128 * g : 128 * (g + 1)] = (
                        jnp.dot(work[g, :, 0:BLK], rows[g, 0:BLK], preferred_element_type=F32)
                        + jnp.dot(work[g, :, BLK:], rows[g, BLK:], preferred_element_type=F32)
                    ).astype(BF16)

        @pl.when(step == 0)
        def _():
            to_far.start()

        @pl.when(step == 1)
        def _():
            to_far.wait_recv()
            sums[0] = (dkv[4].astype(F32) + from_mate[0].astype(F32)).astype(BF16)
            chain.start()
            back_first.start()

        @pl.when(step == 2)
        def _():
            to_near.start()

        @pl.when(step == 3)
        def _():
            to_near.wait_recv()
            both = dkv[2, HALF:BLK].astype(F32) + from_mate[1, HALF:BLK].astype(F32)
            sums[1, HALF:BLK] = both.astype(BF16)

            @pl.when(y > 0)
            def _():
                home_b.start()

            @pl.when(y == 0)
            def _():
                over_back.start()

            back_first.wait_recv()
            back_second.start()
            for copy in z_copies:
                copy.wait_recv()
            z_sum[...] = wt[z].astype(F32)
            for i in range(3):
                z_sum[...] += z_in[i].astype(F32)
            for i in range(4):
                pair_out[i] = weight_rows(i, 1 - core).astype(BF16)
            pair_copy.start()

        @pl.when(step == 4)
        def _():
            edge_copy.start()
            chain.wait_recv()
            near = dkv[2, 0:HALF].astype(F32) + from_mate[1, 0:HALF].astype(F32)
            sums[1, 0:HALF] = (near + chain_in[...].astype(F32)).astype(BF16)
            home_a.start()
            pair_copy.wait_recv()
            for i in range(4):
                y_out[i] = (weight_rows(i, core) + pair_in[i].astype(F32)).astype(BF16)
            for copy in y_copies:
                copy.start()

            @pl.when(y == 0)
            def _():
                over_back.wait_recv()
                over_home.start()

        return carry

    lax.fori_loop(0, BACK + 1, backward, 0)

    keep = pltpu.make_async_copy(dkv.at[0], own_ref, local.at[0])
    keep.start()
    dq_ref[...] = (dq_t[...] * HS**-0.5).astype(BF16)
    total = weight_rows(y, core) + pair_in[y].astype(F32)
    for i, copy in enumerate(y_copies):
        copy.wait_recv()
        total = total + y_in[i].astype(F32)
    dw_ref[...] = total[0:40, :WIDTH]
    for copy in [edge_copy, home_a, home_b, back_second, keep]:
        if copy is keep:
            copy.wait()
        else:
            copy.wait_recv()

    copies = [near_k, near_v, relay_first, direct_k, direct_v, chain_k, relay_second]
    copies += [pass_near_k, pass_near_v, pass_far_k, pass_far_v]
    copies += [to_far, to_near, chain, back_first, back_second, home_a, home_b, edge_copy]
    for copy in beside + opposite + copies + z_copies + y_copies + [pair_copy]:
        copy.wait_send()

    @pl.when(y == 3)
    def _():
        over_second.wait_send()

    @pl.when(y == 0)
    def _():
        over_home.wait_send()


def finish_kernel(
    dq, dw, own, near, far, edge, dq_ref, dk_ref, dv_ref, dw_ref, held, far_v, done, sems, out_sems
):
    through = [
        pltpu.make_async_copy(dq, dq_ref, out_sems.at[0]),
        pltpu.make_async_copy(dw, dw_ref, out_sems.at[1]),
    ]
    halves = [slice(HALF * half, HALF * (half + 1)) for half in range(2)]
    loads = [
        [
            pltpu.make_async_copy(src.at[part], held.at[i, part], sems.at[3 * half + i])
            for i, src in enumerate((own, edge, near))
        ]
        for half, part in enumerate(halves)
    ]
    loads[1].append(pltpu.make_async_copy(far, far_v, sems.at[6]))
    for copy in loads[0] + loads[1] + through:
        copy.start()
    for half, part in enumerate(halves):
        for copy in loads[half]:
            copy.wait()
        total = held[0, part].astype(F32) + held[1, part].astype(F32) + held[2, part].astype(F32)
        if half == 1:
            total = total + far_v[...].astype(F32)
        done[:, part] = total.T.astype(BF16)
        for i, dst in enumerate((dk_ref, dv_ref)):
            rows = slice(WIDTH * i, WIDTH * (i + 1))
            copy = pltpu.make_async_copy(
                done.at[rows, part], dst.at[:, part], out_sems.at[2 + 2 * half + i]
            )
            copy.start()
            through.append(copy)
    for copy in through:
        copy.wait()


def shards(queries, key_rows, value_rows, cotangent, out_weight, segment_units, left_segments):
    tm_count = lax.axis_size("tm")
    head_count = lax.axis_size("head")
    anywhere = pl.BlockSpec(memory_space=pl.ANY)
    vmem = pl.BlockSpec(memory_space=pltpu.VMEM)
    dma = pltpu.SemaphoreType.DMA
    out_t = jax.ShapeDtypeStruct((WIDTH, BLK), BF16)
    both = 2 * WIDTH
    blocks = BACK + 1
    block = jax.ShapeDtypeStruct((BLK, both), BF16)
    pieces = pl.pallas_call(
        functools.partial(kernel, tm_count, head_count),
        out_shape=(
            out_t,
            jax.ShapeDtypeStruct((40, WIDTH), F32),
            block,
            block,
            jax.ShapeDtypeStruct((HALF, both), BF16),
            block,
        ),
        in_specs=[vmem] * 2 + [anywhere] * 5,
        out_specs=(vmem, vmem, anywhere, anywhere, anywhere, anywhere),
        scratch_shapes=[
            pltpu.VMEM((blocks, both, BLK), BF16),
            pltpu.VMEM((WIDTH, BLK), BF16),
            pltpu.VMEM((WIDTH, BLK), BF16),
            pltpu.VMEM((blocks, BLK, both), BF16),
            pltpu.VMEM((blocks, HEADS, BLK, BLK), BF16),
            pltpu.VMEM((head_count * WIDTH, BLK), BF16),
            pltpu.VMEM((WIDTH, head_count * WIDTH), BF16),
            pltpu.VMEM((WIDTH, BLK), BF16),
            pltpu.VMEM((HEADS, 256, BLK), BF16),
            pltpu.VMEM((HEADS, 128, BLK), BF16),
            pltpu.VMEM((HEADS, 2 * BLK, 128), BF16),
            pltpu.VMEM((2, BLK, WIDE), F32),
            pltpu.VMEM((HEADS, BLK, 2 * BLK), BF16),
            pltpu.VMEM((WIDTH, BLK), F32),
            pltpu.VMEM((WIDTH, BLK), F32),
            pltpu.VMEM((blocks, HEADS, 8, BLK), F32),
            pltpu.VMEM((HEADS, 8, BLK), F32),
            pltpu.VMEM((HEADS, 8, BLK), F32),
            pltpu.VMEM((HEADS, 8, BLK), F32),
            pltpu.VMEM((blocks, BLK, both), BF16),
            pltpu.VMEM((2, BLK, both), BF16),
            pltpu.VMEM((2, BLK, both), BF16),
            pltpu.VMEM((HALF, both), BF16),
            pltpu.VMEM((HALF, both), BF16),
            pltpu.VMEM((HALF, both), BF16),
            pltpu.VMEM((4, WIDTH, WEIGHT_WIDTH), BF16),
            pltpu.VMEM((3, WIDTH, WEIGHT_WIDTH), BF16),
            pltpu.VMEM((WIDTH, WEIGHT_WIDTH), F32),
            pltpu.VMEM((4, 48, WEIGHT_WIDTH), BF16),
            pltpu.VMEM((4, 48, WEIGHT_WIDTH), BF16),
            pltpu.VMEM((4, 48, WEIGHT_WIDTH), BF16),
            pltpu.VMEM((3, 48, WEIGHT_WIDTH), BF16),
            dma((5,)),
            dma((12,)),
            dma((blocks,)),
            dma((blocks,)),
            dma((2,)),
            dma((4,)),
            dma((4,)),
            dma((9,)),
            dma((9,)),
            dma((3,)),
            dma((3,)),
            dma((1,)),
            dma((1,)),
            dma((3,)),
            dma((3,)),
        ],
        compiler_params=pltpu.CompilerParams(
            collective_id=0, has_side_effects=True, vmem_limit_bytes=60 << 20
        ),
    )(
        segment_units.reshape(1, -1),
        left_segments.reshape(1, -1),
        queries.T,
        key_rows.T,
        value_rows.T,
        cotangent.T,
        out_weight,
    )
    query_t, key_t, value_t, weight_t = pl.pallas_call(
        finish_kernel,
        out_shape=(out_t, out_t, out_t, jax.ShapeDtypeStruct((40, WIDTH), F32)),
        in_specs=[anywhere] * 6,
        out_specs=(anywhere, anywhere, anywhere, anywhere),
        scratch_shapes=[
            pltpu.VMEM((3, BLK, both), BF16),
            pltpu.VMEM((HALF, both), BF16),
            pltpu.VMEM((both, BLK), BF16),
            dma((7,)),
            dma((6,)),
        ],
        compiler_params=pltpu.CompilerParams(vmem_limit_bytes=60 << 20),
    )(*pieces)
    return (query_t.T, key_t.T, value_t.T, weight_t.T)


def solution(mesh):
    placed = (
        P("tm", "head"),
        P("tm", "head"),
        P("tm", "head"),
        P("tm", "head"),
        P("head", None),
        P(),
        P(),
    )
    return jax.shard_map(
        shards,
        mesh=mesh,
        in_specs=placed,
        out_specs=(P("tm", "head"), P("tm", "head"), P("tm", "head"), P("head", "tm")),
        check_vma=False,
    )
```

```python
import functools

import jax
import jax.numpy as jnp
from jax import lax
from jax.experimental import pallas as pl
from jax.experimental.pallas import tpu as pltpu
from jax.sharding import PartitionSpec as P

HS = 64
UNIT = 16
BLK = 512
HEADS = 5
WIDTH = HEADS * HS
BACK = 5
HALF = BLK // 2
WEIGHT_WIDTH = 384
STRIP = 128
WIDE = 512
HIDDEN = -2e30
LOWEST = -1e30
F32 = jnp.float32
BF16 = jnp.bfloat16
MESH = pl.DeviceIdType.MESH


def kernel(
    tm_count,
    head_count,
    units_ref,
    left_ref,
    q_hbm,
    k_hbm,
    v_hbm,
    cot_hbm,
    w_hbm,
    dq_ref,
    dw_ref,
    own_ref,
    home_near,
    home_far,
    edge,
    slots,
    relay,
    cross,
    kv_all,
    probs,
    cot_all,
    w_ref,
    q_ref,
    rhs,
    gt,
    rows,
    square,
    work,
    out_t,
    dq_t,
    m_all,
    m_run,
    l_run,
    delta,
    dkv,
    from_mate,
    sums,
    chain_in,
    relay_back,
    cross_back,
    wt,
    z_in,
    z_sum,
    pair_out,
    pair_in,
    y_out,
    y_in,
    local,
    sent,
    got_k,
    got_v,
    got_relay,
    side_sent,
    side_got,
    back_sent,
    back_got,
    z_sent,
    z_got,
    pair_sent,
    pair_got,
    y_sent,
    y_got,
):
    t = lax.axis_index("tm")
    x = lax.axis_index("head")
    core = t % 2
    z = t // 8
    y = (t // 2) % 4
    low = t % 8

    def at(place):
        return {"tm": (place + tm_count) % tm_count}

    def chip(z_place, y_place):
        return (((z_place + 4) % 4) * 4 + y_place % 4) * 2 + core

    mate = at(t + 1 - 2 * core)
    before, after = chip(z, y + 3), chip(z, y + 1)
    inner = jnp.where((y == 1) | (y == 2), 1, 0)
    relay_to = chip(z + jnp.where(y >= 2, 1, 0), y + 3)
    relay_from = chip(z - inner, y + 1)
    back_to = chip(z - jnp.where(y < 2, 1, 0), y + 1)
    back_from = chip(z + inner, y + 3)

    greeted = [at(t - 2), at(t + 2), at(relay_from), at(back_from)]
    greeted += [{"head": (x + head_count + by) % head_count} for by in (-1, 1)]
    greeted += [at(t - 8 * i) for i in range(1, 4)]
    greeted += [at(8 * z + (low + 8 - i) % 8) for i in range(1, 8)]
    barrier = pltpu.get_barrier_semaphore()
    for target in greeted:
        pl.semaphore_signal(barrier, inc=1, device_id=target, device_id_type=MESH)
    edge_source = at(t + 5 * (2 * core - 1))
    pl.semaphore_signal(barrier, inc=1, device_id=edge_source, device_id_type=MESH)

    loads = [
        pltpu.make_async_copy(k_hbm, slots.at[0, 0:WIDTH], local.at[0]),
        pltpu.make_async_copy(v_hbm, slots.at[0, WIDTH : 2 * WIDTH], local.at[1]),
        pltpu.make_async_copy(q_hbm, q_ref, local.at[2]),
        pltpu.make_async_copy(
            cot_hbm, cot_all.at[pl.ds(pl.multiple_of(WIDTH * x, 64), WIDTH)], local.at[3]
        ),
        pltpu.make_async_copy(w_hbm, w_ref, local.at[4]),
    ]
    for load in loads:
        load.start()
    pl.semaphore_wait(barrier, len(greeted) + 1)

    def push(src, dst, send_sem, recv_sem, target):
        return pltpu.make_async_remote_copy(
            src_ref=src,
            dst_ref=dst,
            send_sem=send_sem,
            recv_sem=recv_sem,
            device_id=target,
            device_id_type=MESH,
        )

    def keys(src, slot, number, target):
        return push(src, slots.at[slot, 0:WIDTH], sent.at[number], got_k.at[slot], target)

    def values(src, slot, number, target):
        return push(
            src, slots.at[slot, WIDTH : 2 * WIDTH], sent.at[number], got_v.at[slot], target
        )

    def key_part(slot):
        return slots.at[slot, 0:WIDTH]

    def value_part(slot):
        return slots.at[slot, WIDTH : 2 * WIDTH]

    near_k = keys(k_hbm, 2, 0, at(t + 2))
    near_v = values(v_hbm, 2, 1, at(t + 2))
    over_first = push(v_hbm, cross, sent.at[1], got_relay.at[1], at(t + 8))
    over_second = values(cross, 2, 11, at(t - 6))
    relay_first = push(v_hbm, relay, sent.at[2], got_relay.at[0], at(relay_to))
    near_k.start()
    relay_first.start()
    def cot_rows(place, first, count):
        start = WIDTH * (place % head_count) + first
        return cot_all.at[pl.ds(pl.multiple_of(start, 32), count)]

    def aside(src, rows_there, number, by):
        place = {"head": (x + head_count + by) % head_count}
        return push(src, rows_there, side_sent.at[number], side_got.at[number], place)

    own_cot = cot_rows(x, 0, WIDTH)
    upper = cot_rows(x + head_count - 1, 0, WIDTH // 2)
    lower = cot_rows(x + 1, WIDTH // 2, WIDTH // 2)
    beside = [aside(cot_hbm, own_cot, 0, 1), aside(cot_hbm, own_cot, 1, -1)]
    opposite = [aside(upper, upper, 2, 1), aside(lower, lower, 3, -1)]
    for copy in beside:
        copy.start()

    @pl.when(y < 3)
    def _():
        near_v.start()

    @pl.when(y == 3)
    def _():
        over_first.start()

    direct_slot = 1 + 4 * core
    direct_to = at(t + 1 + 4 * core)
    direct_k = keys(k_hbm, direct_slot, 3, direct_to)
    direct_v = values(v_hbm, direct_slot, 4, direct_to)

    @pl.when(core == 0)
    def _():
        direct_k.start()
        direct_v.start()

    chain_k = keys(key_part(2), 4, 5, at(t + 2))
    relay_second = values(relay, 4, 6, at(before))
    pass_near = 3 - 2 * core
    pass_far = 5 - 2 * core
    pass_near_k = keys(key_part(2), pass_near, 7, mate)
    pass_near_v = values(value_part(2), pass_near, 8, mate)
    pass_far_k = keys(key_part(4), pass_far, 9, mate)
    pass_far_v = values(value_part(4), pass_far, 10, mate)

    segments = units_ref.shape[1]
    units = jnp.broadcast_to(units_ref[...].astype(F32), (8, segments)).astype(BF16)
    lefts = jnp.broadcast_to(left_ref[...].astype(F32), (8, segments)).astype(BF16)
    down = lax.broadcasted_iota(jnp.int32, (segments, 128), 0)
    over = lax.broadcasted_iota(jnp.int32, (segments, 128), 1)
    until = jnp.where(down <= over, 1.0, 0.0).astype(BF16)
    ahead = jnp.where(down < over, 1.0, 0.0).astype(BF16)
    same = jnp.where(down == over, 1.0, 0.0).astype(BF16)
    end_row = jnp.dot(units, until, preferred_element_type=F32)[0:1, :] * UNIT
    start_row = jnp.dot(units, ahead, preferred_element_type=F32)[0:1, :] * UNIT
    columns = (((0,), (1,)), ((), ()))
    end_col = lax.dot_general(until, units, columns, preferred_element_type=F32)[:, 0:1] * UNIT
    left_col = lax.dot_general(same, lefts, columns, preferred_element_type=F32)[:, 0:1]
    frame_row = (t * BLK + lax.broadcasted_iota(jnp.int32, (1, BLK), 1)).astype(F32)
    own_seg = jnp.sum(jnp.where(end_col <= frame_row, 1.0, 0.0), axis=0, keepdims=True)
    seg_down = lax.broadcasted_iota(jnp.int32, (128, BLK), 0).astype(F32)
    reach = jnp.sum(jnp.where(seg_down == own_seg, left_col, 0.0), axis=0, keepdims=True)
    lowest = jnp.maximum(own_seg - reach, 0.0)
    bias = jnp.where((seg_down >= lowest) & (seg_down <= own_seg), 0.0, HIDDEN).astype(BF16)

    blank = jnp.zeros((HS, BLK), BF16)
    lane = lax.broadcasted_iota(jnp.int32, (BLK, 128), 1)

    def spread(j, upright, transposed):
        g, half = divmod(j, 2)
        both = [transposed, blank] if half == 0 else [blank, transposed]
        if j < HEADS:
            rhs[j] = jnp.concatenate(both + [bias], axis=0)
        else:
            gt[j - HEADS] = jnp.concatenate(both, axis=0)
        zeros = jnp.zeros((BLK, HS), BF16)
        pair = [upright, zeros] if half == 0 else [zeros, upright]
        rows[g, BLK * half : BLK * (half + 1), :] = jnp.concatenate(pair, axis=1)

    loads[2].wait()
    queries_t = (q_ref[...].astype(F32) * HS**-0.5).astype(BF16)
    for j in range(HEADS):
        mine = queries_t[HS * j : HS * (j + 1), :]
        spread(j, mine.T, mine)
    m_run[...] = jnp.full(m_run.shape, LOWEST, F32)
    l_run[...] = jnp.zeros(l_run.shape, F32)
    out_t[...] = jnp.zeros(out_t.shape, F32)
    dq_t[...] = jnp.zeros(dq_t.shape, F32)
    loads[0].wait()
    loads[1].wait()

    def wait_slot(slot):
        keys(k_hbm, slot, 0, mate).wait_recv()
        values(v_hbm, slot, 1, mate).wait_recv()

    def near_event():
        relay_first.wait_recv()
        relay_second.start()

        near_k.wait_recv()
        chain_k.start()
        pass_near_k.start()
        for arrived, onward in zip(beside, opposite):
            arrived.wait_recv()
            onward.start()
        near_v.wait_recv()
        pass_near_v.start()

    def forward(step, carry):
        @pl.when((step == 1) & (core == 1))
        def _():
            direct_k.start()
            direct_v.start()

        @pl.when((step == 1) & (y == 3))
        def _():
            over_first.wait_recv()
            over_second.start()

        swapped = jnp.where(step == 0, 0, jnp.where(step < 3, 3 - step, 8 - step))
        slot = jnp.where(core == 0, swapped, step)

        @pl.when(step == 1 + core)
        def _():
            near_event()

        @pl.when((step == 2 - core) | (step == 3) | (step == 5))
        def _():
            wait_slot(slot)

        @pl.when(step == 4)
        def _():
            loads[3].wait()
            loads[4].wait()
            for copy in opposite:
                copy.wait_recv()
            grad_t = jnp.dot(w_ref[...], cot_all[...], preferred_element_type=F32).astype(BF16)
            for j in range(HEADS):
                mine = grad_t[HS * j : HS * (j + 1), :]
                spread(j + HEADS, mine.T, mine)

        @pl.when(step == 4)
        def _():
            keys(k_hbm, 4, 0, mate).wait_recv()
            pass_far_k.start()
            values(v_hbm, 4, 1, mate).wait_recv()
            pass_far_v.start()

        def upright(g):
            group = slice(128 * g, 128 * (g + 1))
            kv_all[slot, :, group] = slots[slot, group, :].T

        first = ((t + tm_count - slot) % tm_count) * BLK
        frames = (first + lax.broadcasted_iota(jnp.int32, (BLK, 128), 0)).astype(F32)
        hot = jnp.where((frames >= start_row) & (frames < end_row), 1.0, 0.0).astype(BF16)
        upright(0)
        pieces = BLK // WIDE
        units_of = HEADS * pieces
        top = None
        late = []
        for turn in range(units_of + 1):
            last = top
            if turn < units_of:
                h, c = divmod(turn, pieces)
                cols = slice(WIDE * c, WIDE * (c + 1))
                g = h // 2
                lhs = jnp.concatenate([kv_all[slot, :, 128 * g : 128 * (g + 1)], hot], axis=1)
                scores = jnp.dot(lhs, rhs[h, :, cols], preferred_element_type=F32)
                square[turn % 2] = scores
                top = jnp.max(scores.reshape(BLK // 8, 8, WIDE), axis=0)
                if turn < HEADS - 1:
                    upright(turn + 1)
            if turn == 0:
                continue
            h, c = divmod(turn - 1, pieces)
            cols = slice(WIDE * c, WIDE * (c + 1))
            m_old = m_run[h, 0:1, cols]
            m_new = jnp.maximum(m_old, jnp.max(last, axis=0, keepdims=True))
            factor = jnp.exp(m_old - m_new)
            m_run[h, 0:1, cols] = m_new
            m_all[slot, h, 0:1, cols] = m_new
            total = l_run[h, :, cols] * factor
            for r in range(0, BLK, STRIP):
                p = jnp.exp(square[(turn - 1) % 2, r : r + STRIP, :] - m_new)
                total = total + jnp.sum(p.reshape(STRIP // 8, 8, WIDE), axis=0)
                probs[slot, h, r : r + STRIP, cols] = p.astype(BF16)
            l_run[h, :, cols] = total
            late.append((h, cols, factor))
            if turn < 2:
                continue
            for h, cols, factor in late[-2:] if turn == units_of else late[-2:-1]:
                here = slice(HS * h, HS * (h + 1))
                out_t[here, cols] = out_t[here, cols] * factor + jnp.dot(
                    slots[slot, WIDTH + HS * h : WIDTH + HS * (h + 1), :],
                    probs[slot, h, :, cols],
                    preferred_element_type=F32,
                )
        return carry

    lax.fori_loop(0, BACK + 1, forward, 0)

    for h in range(HEADS):
        here = slice(HS * h, HS * (h + 1))
        total = jnp.sum(l_run[h], axis=0, keepdims=True)
        out = out_t[here, :] / total
        out_t[here, :] = out
        side = HS * ((h + HEADS) % 2)
        own_grad = gt[h, side : side + HS, :].astype(F32)
        delta[h, 0:1, :] = jnp.sum(out * own_grad, axis=0, keepdims=True)
        l_run[h, 0:1, :] = m_run[h, 0:1, :] + jnp.log(total)

    z_copies = [
        push(
            wt.at[(z + i) % 4], z_in.at[i - 1], z_sent.at[i - 1], z_got.at[i - 1], at(t + 8 * i)
        )
        for i in range(1, 4)
    ]
    attn = jnp.concatenate(
        [out_t[...].T.astype(BF16), jnp.zeros((BLK, WEIGHT_WIDTH - WIDTH), BF16)], axis=1
    )
    for part in range(4):
        piece = slice(WIDTH * part, WIDTH * (part + 1))
        wt[part] = jnp.dot(cot_all[piece, :], attn, preferred_element_type=F32).astype(BF16)
    for copy in z_copies:
        copy.start()
    pair_copy = push(pair_out, pair_in, pair_sent.at[0], pair_got.at[0], mate)
    y_copies = [
        push(
            y_out.at[(y + i) % 4],
            y_in.at[i - 1],
            y_sent.at[i - 1],
            y_got.at[i - 1],
            at(chip(z, y + i)),
        )
        for i in range(1, 4)
    ]

    def weight_rows(ring_place, parity):
        first = pl.multiple_of(80 * ring_place + 40 * parity, 8)
        block = z_sum[pl.ds(first, 40), :]
        return jnp.concatenate([block, jnp.zeros((8, WEIGHT_WIDTH), F32)], axis=0)

    far_slot, near_slot, edge_slot = 3 + 2 * core, 1 + 2 * core, 5 - 4 * core
    to_far = push(dkv.at[far_slot], from_mate.at[0], back_sent.at[0], back_got.at[0], mate)
    to_near = push(dkv.at[near_slot], from_mate.at[1], back_sent.at[1], back_got.at[1], mate)
    chain = push(sums.at[0, 0:HALF], chain_in, back_sent.at[2], back_got.at[2], at(t - 2))
    back_first = push(
        sums.at[0, HALF:BLK], relay_back, back_sent.at[3], back_got.at[3], at(back_to)
    )
    back_second = push(relay_back, home_far, back_sent.at[4], back_got.at[4], at(after))
    home_a = push(
        sums.at[1, 0:HALF], home_near.at[0:HALF], back_sent.at[5], back_got.at[5], at(t - 2)
    )
    home_b = push(
        sums.at[1, HALF:BLK], home_near.at[HALF:BLK], back_sent.at[7], back_got.at[7], at(t - 2)
    )
    over_back = push(sums.at[1, HALF:BLK], cross_back, back_sent.at[7], back_got.at[8], at(t - 8))
    over_home = push(
        cross_back, home_near.at[HALF:BLK], back_sent.at[8], back_got.at[7], at(t + 6)
    )
    edge_to = at(t - 5 + 4 * core)
    edge_copy = push(dkv.at[edge_slot], edge, back_sent.at[6], back_got.at[6], edge_to)

    def backward(step, carry):
        crossed = jnp.where(
            step < 2, 3 + step, jnp.where(step < 4, step - 1, jnp.where(step == 4, 5, 0))
        )
        slot = jnp.where(core == 0, crossed, 5 - step)
        pieces = BLK // WIDE
        units_of = HEADS * pieces
        done = []
        for turn in range(units_of + 1):
            if turn < units_of:
                h, c = divmod(turn, pieces)
                g = (h + HEADS) // 2
                square[turn % 2] = jnp.dot(
                    kv_all[slot, :, 128 * g : 128 * (g + 1)],
                    gt[h, :, WIDE * c : WIDE * (c + 1)],
                    preferred_element_type=F32,
                )
            if turn == 0:
                continue
            h, c = divmod(turn - 1, pieces)
            cols = slice(WIDE * c, WIDE * (c + 1))
            scale = jnp.exp(m_all[slot, h, 0:1, cols] - l_run[h, 0:1, cols])
            shift = delta[h, 0:1, cols]
            ds_at = BLK * (h % 2) + WIDE * c
            p_at = BLK * ((h + HEADS) % 2) + WIDE * c
            for r in range(0, BLK, STRIP):
                down = slice(r, r + STRIP)
                p = probs[slot, h, down, cols].astype(F32) * scale
                ds = p * (square[(turn - 1) % 2, down, :] - shift)
                work[h // 2, down, ds_at : ds_at + WIDE] = ds.astype(BF16)
                work[(h + HEADS) // 2, down, p_at : p_at + WIDE] = p.astype(BF16)
            done.append(h)
            if turn < 2:
                continue
            for h in done[-2:] if turn == units_of else done[-2:-1]:
                here = slice(HS * h, HS * (h + 1))
                dq_t[here, :] += jnp.dot(
                    slots[slot, here, :],
                    work[h // 2, :, BLK * (h % 2) : BLK * (h % 2 + 1)],
                    preferred_element_type=F32,
                )
                for g in ((), (0,), (3,), (1,), (2, 4))[h]:
                    dkv[slot, :, 128 * g : 128 * (g + 1)] = (
                        jnp.dot(work[g, :, 0:BLK], rows[g, 0:BLK], preferred_element_type=F32)
                        + jnp.dot(work[g, :, BLK:], rows[g, BLK:], preferred_element_type=F32)
                    ).astype(BF16)

        @pl.when(step == 0)
        def _():
            to_far.start()

        @pl.when(step == 1)
        def _():
            to_far.wait_recv()
            for part, copy in ((slice(0, HALF), chain), (slice(HALF, BLK), back_first)):
                both = dkv[4, part].astype(F32) + from_mate[0, part].astype(F32)
                sums[0, part] = both.astype(BF16)
                copy.start()

        @pl.when(step == 2)
        def _():
            to_near.start()

        @pl.when(step == 3)
        def _():
            to_near.wait_recv()
            both = dkv[2, HALF:BLK].astype(F32) + from_mate[1, HALF:BLK].astype(F32)
            sums[1, HALF:BLK] = both.astype(BF16)

            @pl.when(y > 0)
            def _():
                home_b.start()

            @pl.when(y == 0)
            def _():
                over_back.start()

            back_first.wait_recv()
            back_second.start()
            for copy in z_copies:
                copy.wait_recv()
            z_sum[...] = wt[z].astype(F32)
            for i in range(3):
                z_sum[...] += z_in[i].astype(F32)
            for i in range(4):
                pair_out[i] = weight_rows(i, 1 - core).astype(BF16)
            pair_copy.start()

        @pl.when(step == 4)
        def _():
            edge_copy.start()
            chain.wait_recv()
            near = dkv[2, 0:HALF].astype(F32) + from_mate[1, 0:HALF].astype(F32)
            sums[1, 0:HALF] = (near + chain_in[...].astype(F32)).astype(BF16)
            home_a.start()
            pair_copy.wait_recv()
            for i in range(4):
                y_out[i] = (weight_rows(i, core) + pair_in[i].astype(F32)).astype(BF16)
            for copy in y_copies:
                copy.start()

            @pl.when(y == 0)
            def _():
                over_back.wait_recv()
                over_home.start()

        return carry

    lax.fori_loop(0, BACK + 1, backward, 0)

    keep = pltpu.make_async_copy(dkv.at[0], own_ref, local.at[0])
    keep.start()
    dq_ref[...] = (dq_t[...] * HS**-0.5).astype(BF16)
    total = weight_rows(y, core) + pair_in[y].astype(F32)
    for i, copy in enumerate(y_copies):
        copy.wait_recv()
        total = total + y_in[i].astype(F32)
    dw_ref[...] = total[0:40, :WIDTH]
    for copy in [edge_copy, home_a, home_b, back_second, keep]:
        if copy is keep:
            copy.wait()
        else:
            copy.wait_recv()

    copies = [near_k, near_v, relay_first, direct_k, direct_v, chain_k, relay_second]
    copies += [pass_near_k, pass_near_v, pass_far_k, pass_far_v]
    copies += [to_far, to_near, chain, back_first, back_second, home_a, home_b, edge_copy]
    for copy in beside + opposite + copies + z_copies + y_copies + [pair_copy]:
        copy.wait_send()

    @pl.when(y == 3)
    def _():
        over_second.wait_send()

    @pl.when(y == 0)
    def _():
        over_home.wait_send()


def finish_kernel(
    dq, dw, own, near, far, edge, dq_ref, dk_ref, dv_ref, dw_ref, held, far_v, sems
):
    halves = [slice(HALF * half, HALF * (half + 1)) for half in range(2)]
    loads = [
        [
            pltpu.make_async_copy(src.at[part], held.at[i, part], sems.at[3 * half + i])
            for i, src in enumerate((own, edge, near))
        ]
        for half, part in enumerate(halves)
    ]
    loads[1].append(pltpu.make_async_copy(far, far_v, sems.at[6]))
    through = [
        pltpu.make_async_copy(dq, dq_ref, sems.at[7]),
        pltpu.make_async_copy(dw, dw_ref, sems.at[8]),
    ]
    for copy in loads[0] + loads[1] + through:
        copy.start()
    for half, part in enumerate(halves):
        for copy in loads[half]:
            copy.wait()
        total = held[0, part].astype(F32) + held[1, part].astype(F32) + held[2, part].astype(F32)
        if half == 1:
            total = total + far_v[...].astype(F32)
        total_t = total.T.astype(BF16)
        dk_ref[:, part] = total_t[:WIDTH]
        dv_ref[:, part] = total_t[WIDTH:]
    for copy in through:
        copy.wait()


def shards(queries, key_rows, value_rows, cotangent, out_weight, segment_units, left_segments):
    tm_count = lax.axis_size("tm")
    head_count = lax.axis_size("head")
    anywhere = pl.BlockSpec(memory_space=pl.ANY)
    vmem = pl.BlockSpec(memory_space=pltpu.VMEM)
    dma = pltpu.SemaphoreType.DMA
    out_t = jax.ShapeDtypeStruct((WIDTH, BLK), BF16)
    both = 2 * WIDTH
    blocks = BACK + 1
    block = jax.ShapeDtypeStruct((BLK, both), BF16)
    pieces = pl.pallas_call(
        functools.partial(kernel, tm_count, head_count),
        out_shape=(
            out_t,
            jax.ShapeDtypeStruct((40, WIDTH), F32),
            block,
            block,
            jax.ShapeDtypeStruct((HALF, both), BF16),
            block,
        ),
        in_specs=[vmem] * 2 + [anywhere] * 5,
        out_specs=(vmem, vmem, anywhere, anywhere, anywhere, anywhere),
        scratch_shapes=[
            pltpu.VMEM((blocks, both, BLK), BF16),
            pltpu.VMEM((WIDTH, BLK), BF16),
            pltpu.VMEM((WIDTH, BLK), BF16),
            pltpu.VMEM((blocks, BLK, both), BF16),
            pltpu.VMEM((blocks, HEADS, BLK, BLK), BF16),
            pltpu.VMEM((head_count * WIDTH, BLK), BF16),
            pltpu.VMEM((WIDTH, head_count * WIDTH), BF16),
            pltpu.VMEM((WIDTH, BLK), BF16),
            pltpu.VMEM((HEADS, 256, BLK), BF16),
            pltpu.VMEM((HEADS, 128, BLK), BF16),
            pltpu.VMEM((HEADS, 2 * BLK, 128), BF16),
            pltpu.VMEM((2, BLK, WIDE), F32),
            pltpu.VMEM((HEADS, BLK, 2 * BLK), BF16),
            pltpu.VMEM((WIDTH, BLK), F32),
            pltpu.VMEM((WIDTH, BLK), F32),
            pltpu.VMEM((blocks, HEADS, 8, BLK), F32),
            pltpu.VMEM((HEADS, 8, BLK), F32),
            pltpu.VMEM((HEADS, 8, BLK), F32),
            pltpu.VMEM((HEADS, 8, BLK), F32),
            pltpu.VMEM((blocks, BLK, both), BF16),
            pltpu.VMEM((2, BLK, both), BF16),
            pltpu.VMEM((2, BLK, both), BF16),
            pltpu.VMEM((HALF, both), BF16),
            pltpu.VMEM((HALF, both), BF16),
            pltpu.VMEM((HALF, both), BF16),
            pltpu.VMEM((4, WIDTH, WEIGHT_WIDTH), BF16),
            pltpu.VMEM((3, WIDTH, WEIGHT_WIDTH), BF16),
            pltpu.VMEM((WIDTH, WEIGHT_WIDTH), F32),
            pltpu.VMEM((4, 48, WEIGHT_WIDTH), BF16),
            pltpu.VMEM((4, 48, WEIGHT_WIDTH), BF16),
            pltpu.VMEM((4, 48, WEIGHT_WIDTH), BF16),
            pltpu.VMEM((3, 48, WEIGHT_WIDTH), BF16),
            dma((5,)),
            dma((12,)),
            dma((blocks,)),
            dma((blocks,)),
            dma((2,)),
            dma((4,)),
            dma((4,)),
            dma((9,)),
            dma((9,)),
            dma((3,)),
            dma((3,)),
            dma((1,)),
            dma((1,)),
            dma((3,)),
            dma((3,)),
        ],
        compiler_params=pltpu.CompilerParams(
            collective_id=0, has_side_effects=True, vmem_limit_bytes=60 << 20
        ),
    )(
        segment_units.reshape(1, -1),
        left_segments.reshape(1, -1),
        queries.T,
        key_rows.T,
        value_rows.T,
        cotangent.T,
        out_weight,
    )
    query_t, key_t, value_t, weight_t = pl.pallas_call(
        finish_kernel,
        out_shape=(out_t, out_t, out_t, jax.ShapeDtypeStruct((40, WIDTH), F32)),
        in_specs=[anywhere] * 6,
        out_specs=(vmem, vmem, vmem, vmem),
        scratch_shapes=[
            pltpu.VMEM((3, BLK, both), BF16),
            pltpu.VMEM((HALF, both), BF16),
            dma((9,)),
        ],
        compiler_params=pltpu.CompilerParams(vmem_limit_bytes=60 << 20),
    )(*pieces)
    return (query_t.T, key_t.T, value_t.T, weight_t.T)


def solution(mesh):
    placed = (
        P("tm", "head"),
        P("tm", "head"),
        P("tm", "head"),
        P("tm", "head"),
        P("head", None),
        P(),
        P(),
    )
    return jax.shard_map(
        shards,
        mesh=mesh,
        in_specs=placed,
        out_specs=(P("tm", "head"), P("tm", "head"), P("tm", "head"), P("head", "tm")),
        check_vma=False,
    )
```

```python
import functools

import jax
import jax.numpy as jnp
from jax import lax
from jax.experimental import pallas as pl
from jax.experimental.pallas import tpu as pltpu
from jax.sharding import PartitionSpec as P

HS = 64
UNIT = 16
BLK = 512
HEADS = 5
WIDTH = HEADS * HS
BACK = 5
HALF = BLK // 2
WEIGHT_WIDTH = 384
STRIP = 128
WIDE = 512
HIDDEN = -2e30
LOWEST = -1e30
F32 = jnp.float32
BF16 = jnp.bfloat16
MESH = pl.DeviceIdType.MESH


def kernel(
    tm_count,
    head_count,
    units_ref,
    left_ref,
    q_hbm,
    k_hbm,
    v_hbm,
    cot_hbm,
    w_hbm,
    dq_ref,
    dw_ref,
    own_ref,
    home_near,
    home_far,
    edge,
    slots,
    relay,
    cross,
    kv_all,
    probs,
    cot_all,
    w_ref,
    q_ref,
    rhs,
    gt,
    rows,
    square,
    work,
    out_t,
    dq_t,
    m_all,
    m_run,
    l_run,
    delta,
    dkv,
    from_mate,
    sums,
    chain_in,
    relay_back,
    cross_back,
    wt,
    z_in,
    z_sum,
    pair_out,
    pair_in,
    z_out,
    y_out,
    y_in,
    local,
    sent,
    got_k,
    got_v,
    got_relay,
    side_sent,
    side_got,
    back_sent,
    back_got,
    z_sent,
    z_got,
    pair_sent,
    pair_got,
    y_sent,
    y_got,
):
    t = lax.axis_index("tm")
    x = lax.axis_index("head")
    core = t % 2
    z = t // 8
    y = (t // 2) % 4
    low = t % 8

    def at(place):
        return {"tm": (place + tm_count) % tm_count}

    def chip(z_place, y_place):
        return (((z_place + 4) % 4) * 4 + y_place % 4) * 2 + core

    mate = at(t + 1 - 2 * core)
    before, after = chip(z, y + 3), chip(z, y + 1)
    inner = jnp.where((y == 1) | (y == 2), 1, 0)
    relay_to = chip(z + jnp.where(y >= 2, 1, 0), y + 3)
    relay_from = chip(z - inner, y + 1)
    back_to = chip(z - jnp.where(y < 2, 1, 0), y + 1)
    back_from = chip(z + inner, y + 3)

    greeted = [at(t - 2), at(t + 2), at(relay_from), at(back_from)]
    greeted += [{"head": (x + head_count + by) % head_count} for by in (-1, 1)]
    greeted += [at(t - 8 * i) for i in range(1, 4)]
    greeted += [at(8 * z + (low + 8 - i) % 8) for i in range(1, 8)]
    barrier = pltpu.get_barrier_semaphore()
    for target in greeted:
        pl.semaphore_signal(barrier, inc=1, device_id=target, device_id_type=MESH)
    edge_source = at(t + 5 * (2 * core - 1))
    pl.semaphore_signal(barrier, inc=1, device_id=edge_source, device_id_type=MESH)

    loads = [
        pltpu.make_async_copy(k_hbm, slots.at[0, 0:WIDTH], local.at[0]),
        pltpu.make_async_copy(v_hbm, slots.at[0, WIDTH : 2 * WIDTH], local.at[1]),
        pltpu.make_async_copy(q_hbm, q_ref, local.at[2]),
        pltpu.make_async_copy(
            cot_hbm, cot_all.at[pl.ds(pl.multiple_of(WIDTH * x, 64), WIDTH)], local.at[3]
        ),
        pltpu.make_async_copy(w_hbm, w_ref, local.at[4]),
    ]
    for load in loads:
        load.start()
    pl.semaphore_wait(barrier, len(greeted) + 1)

    def push(src, dst, send_sem, recv_sem, target):
        return pltpu.make_async_remote_copy(
            src_ref=src,
            dst_ref=dst,
            send_sem=send_sem,
            recv_sem=recv_sem,
            device_id=target,
            device_id_type=MESH,
        )

    def keys(src, slot, number, target):
        return push(src, slots.at[slot, 0:WIDTH], sent.at[number], got_k.at[slot], target)

    def values(src, slot, number, target):
        return push(
            src, slots.at[slot, WIDTH : 2 * WIDTH], sent.at[number], got_v.at[slot], target
        )

    def key_part(slot):
        return slots.at[slot, 0:WIDTH]

    def value_part(slot):
        return slots.at[slot, WIDTH : 2 * WIDTH]

    near_k = keys(k_hbm, 2, 0, at(t + 2))
    near_v = values(v_hbm, 2, 1, at(t + 2))
    over_first = push(v_hbm, cross, sent.at[1], got_relay.at[1], at(t + 8))
    over_second = values(cross, 2, 11, at(t - 6))
    relay_first = push(v_hbm, relay, sent.at[2], got_relay.at[0], at(relay_to))
    near_k.start()
    relay_first.start()
    def cot_rows(place, first, count):
        start = WIDTH * (place % head_count) + first
        return cot_all.at[pl.ds(pl.multiple_of(start, 32), count)]

    def aside(src, rows_there, number, by):
        place = {"head": (x + head_count + by) % head_count}
        return push(src, rows_there, side_sent.at[number], side_got.at[number], place)

    own_cot = cot_rows(x, 0, WIDTH)
    upper = cot_rows(x + head_count - 1, 0, WIDTH // 2)
    lower = cot_rows(x + 1, WIDTH // 2, WIDTH // 2)
    beside = [aside(cot_hbm, own_cot, 0, 1), aside(cot_hbm, own_cot, 1, -1)]
    opposite = [aside(upper, upper, 2, 1), aside(lower, lower, 3, -1)]
    for copy in beside:
        copy.start()

    @pl.when(y < 3)
    def _():
        near_v.start()

    @pl.when(y == 3)
    def _():
        over_first.start()

    direct_slot = 1 + 4 * core
    direct_to = at(t + 1 + 4 * core)
    direct_k = keys(k_hbm, direct_slot, 3, direct_to)
    direct_v = values(v_hbm, direct_slot, 4, direct_to)

    @pl.when(core == 0)
    def _():
        direct_k.start()
        direct_v.start()

    chain_k = keys(key_part(2), 4, 5, at(t + 2))
    relay_second = values(relay, 4, 6, at(before))
    pass_near = 3 - 2 * core
    pass_far = 5 - 2 * core
    pass_near_k = keys(key_part(2), pass_near, 7, mate)
    pass_near_v = values(value_part(2), pass_near, 8, mate)
    pass_far_k = keys(key_part(4), pass_far, 9, mate)
    pass_far_v = values(value_part(4), pass_far, 10, mate)

    segments = units_ref.shape[1]
    units = jnp.broadcast_to(units_ref[...].astype(F32), (8, segments)).astype(BF16)
    lefts = jnp.broadcast_to(left_ref[...].astype(F32), (8, segments)).astype(BF16)
    down = lax.broadcasted_iota(jnp.int32, (segments, 128), 0)
    over = lax.broadcasted_iota(jnp.int32, (segments, 128), 1)
    until = jnp.where(down <= over, 1.0, 0.0).astype(BF16)
    ahead = jnp.where(down < over, 1.0, 0.0).astype(BF16)
    same = jnp.where(down == over, 1.0, 0.0).astype(BF16)
    end_row = jnp.dot(units, until, preferred_element_type=F32)[0:1, :] * UNIT
    start_row = jnp.dot(units, ahead, preferred_element_type=F32)[0:1, :] * UNIT
    columns = (((0,), (1,)), ((), ()))
    end_col = lax.dot_general(until, units, columns, preferred_element_type=F32)[:, 0:1] * UNIT
    left_col = lax.dot_general(same, lefts, columns, preferred_element_type=F32)[:, 0:1]
    frame_row = (t * BLK + lax.broadcasted_iota(jnp.int32, (1, BLK), 1)).astype(F32)
    own_seg = jnp.sum(jnp.where(end_col <= frame_row, 1.0, 0.0), axis=0, keepdims=True)
    seg_down = lax.broadcasted_iota(jnp.int32, (128, BLK), 0).astype(F32)
    reach = jnp.sum(jnp.where(seg_down == own_seg, left_col, 0.0), axis=0, keepdims=True)
    lowest = jnp.maximum(own_seg - reach, 0.0)
    bias = jnp.where((seg_down >= lowest) & (seg_down <= own_seg), 0.0, HIDDEN).astype(BF16)

    blank = jnp.zeros((HS, BLK), BF16)
    lane = lax.broadcasted_iota(jnp.int32, (BLK, 128), 1)

    def spread(j, upright, transposed):
        g, half = divmod(j, 2)
        both = [transposed, blank] if half == 0 else [blank, transposed]
        if j < HEADS:
            rhs[j] = jnp.concatenate(both + [bias], axis=0)
        else:
            gt[j - HEADS] = jnp.concatenate(both, axis=0)
        zeros = jnp.zeros((BLK, HS), BF16)
        pair = [upright, zeros] if half == 0 else [zeros, upright]
        rows[g, BLK * half : BLK * (half + 1), :] = jnp.concatenate(pair, axis=1)

    loads[2].wait()
    queries_t = (q_ref[...].astype(F32) * HS**-0.5).astype(BF16)
    for j in range(HEADS):
        mine = queries_t[HS * j : HS * (j + 1), :]
        spread(j, mine.T, mine)
    m_run[...] = jnp.full(m_run.shape, LOWEST, F32)
    l_run[...] = jnp.zeros(l_run.shape, F32)
    out_t[...] = jnp.zeros(out_t.shape, F32)
    dq_t[...] = jnp.zeros(dq_t.shape, F32)
    loads[0].wait()
    loads[1].wait()

    def wait_slot(slot):
        keys(k_hbm, slot, 0, mate).wait_recv()
        values(v_hbm, slot, 1, mate).wait_recv()

    def near_event():
        relay_first.wait_recv()
        relay_second.start()

        near_k.wait_recv()
        chain_k.start()
        pass_near_k.start()
        for arrived, onward in zip(beside, opposite):
            arrived.wait_recv()
            onward.start()
        near_v.wait_recv()
        pass_near_v.start()

    def forward(step, carry):
        @pl.when((step == 1) & (core == 1))
        def _():
            direct_k.start()
            direct_v.start()

        @pl.when((step == 1) & (y == 3))
        def _():
            over_first.wait_recv()
            over_second.start()

        swapped = jnp.where(step == 0, 0, jnp.where(step < 3, 3 - step, 8 - step))
        slot = jnp.where(core == 0, swapped, step)

        @pl.when(step == 1 + core)
        def _():
            near_event()

        @pl.when((step == 2 - core) | (step == 3) | (step == 5))
        def _():
            wait_slot(slot)

        @pl.when(step == 4)
        def _():
            loads[3].wait()
            loads[4].wait()
            for copy in opposite:
                copy.wait_recv()
            grad_t = jnp.dot(w_ref[...], cot_all[...], preferred_element_type=F32).astype(BF16)
            for j in range(HEADS):
                mine = grad_t[HS * j : HS * (j + 1), :]
                spread(j + HEADS, mine.T, mine)

        @pl.when(step == 4)
        def _():
            keys(k_hbm, 4, 0, mate).wait_recv()
            pass_far_k.start()
            values(v_hbm, 4, 1, mate).wait_recv()
            pass_far_v.start()

        def upright(g):
            group = slice(128 * g, 128 * (g + 1))
            kv_all[slot, :, group] = slots[slot, group, :].T

        first = ((t + tm_count - slot) % tm_count) * BLK
        frames = (first + lax.broadcasted_iota(jnp.int32, (BLK, 128), 0)).astype(F32)
        hot = jnp.where((frames >= start_row) & (frames < end_row), 1.0, 0.0).astype(BF16)
        upright(0)
        pieces = BLK // WIDE
        units_of = HEADS * pieces
        top = None
        late = []
        for turn in range(units_of + 1):
            last = top
            if turn < units_of:
                h, c = divmod(turn, pieces)
                cols = slice(WIDE * c, WIDE * (c + 1))
                g = h // 2
                lhs = jnp.concatenate([kv_all[slot, :, 128 * g : 128 * (g + 1)], hot], axis=1)
                scores = jnp.dot(lhs, rhs[h, :, cols], preferred_element_type=F32)
                square[turn % 2] = scores
                top = jnp.max(scores.reshape(BLK // 8, 8, WIDE), axis=0)
                if turn < HEADS - 1:
                    upright(turn + 1)
            if turn == 0:
                continue
            h, c = divmod(turn - 1, pieces)
            cols = slice(WIDE * c, WIDE * (c + 1))
            m_old = m_run[h, 0:1, cols]
            m_new = jnp.maximum(m_old, jnp.max(last, axis=0, keepdims=True))
            factor = jnp.exp(m_old - m_new)
            m_run[h, 0:1, cols] = m_new
            m_all[slot, h, 0:1, cols] = m_new
            total = l_run[h, :, cols] * factor
            for r in range(0, BLK, STRIP):
                p = jnp.exp(square[(turn - 1) % 2, r : r + STRIP, :] - m_new)
                total = total + jnp.sum(p.reshape(STRIP // 8, 8, WIDE), axis=0)
                probs[slot, h, r : r + STRIP, cols] = p.astype(BF16)
            l_run[h, :, cols] = total
            late.append((h, cols, factor))
            if turn < 2:
                continue
            for h, cols, factor in late[-2:] if turn == units_of else late[-2:-1]:
                here = slice(HS * h, HS * (h + 1))
                out_t[here, cols] = out_t[here, cols] * factor + jnp.dot(
                    slots[slot, WIDTH + HS * h : WIDTH + HS * (h + 1), :],
                    probs[slot, h, :, cols],
                    preferred_element_type=F32,
                )
        return carry

    lax.fori_loop(0, BACK + 1, forward, 0)

    for h in range(HEADS):
        here = slice(HS * h, HS * (h + 1))
        total = jnp.sum(l_run[h], axis=0, keepdims=True)
        out = out_t[here, :] / total
        out_t[here, :] = out
        side = HS * ((h + HEADS) % 2)
        own_grad = gt[h, side : side + HS, :].astype(F32)
        delta[h, 0:1, :] = jnp.sum(out * own_grad, axis=0, keepdims=True)
        l_run[h, 0:1, :] = m_run[h, 0:1, :] + jnp.log(total)

    pair_copy = push(pair_out, pair_in, pair_sent.at[0], pair_got.at[0], mate)
    z_copies = [
        push(
            z_out.at[(z + i) % 4], z_in.at[i - 1], z_sent.at[i - 1], z_got.at[i - 1], at(t + 8 * i)
        )
        for i in range(1, 4)
    ]
    y_copies = [
        push(
            y_out.at[(y + i) % 4],
            y_in.at[i - 1],
            y_sent.at[i - 1],
            y_got.at[i - 1],
            at(chip(z, y + i)),
        )
        for i in range(1, 4)
    ]

    def weight_rows(quarter, ring_place, parity):
        first = pl.multiple_of(80 * ring_place + 40 * parity, 8)
        block = wt[quarter, pl.ds(first, 40), :]
        return jnp.concatenate([block, jnp.zeros((8, WEIGHT_WIDTH), F32)], axis=0)

    far_slot, near_slot, edge_slot = 3 + 2 * core, 1 + 2 * core, 5 - 4 * core
    to_far = push(dkv.at[far_slot], from_mate.at[0], back_sent.at[0], back_got.at[0], mate)
    to_near = push(dkv.at[near_slot], from_mate.at[1], back_sent.at[1], back_got.at[1], mate)
    chain = push(sums.at[0, 0:HALF], chain_in, back_sent.at[2], back_got.at[2], at(t - 2))
    back_first = push(
        sums.at[0, HALF:BLK], relay_back, back_sent.at[3], back_got.at[3], at(back_to)
    )
    back_second = push(relay_back, home_far, back_sent.at[4], back_got.at[4], at(after))
    home_a = push(
        sums.at[1, 0:HALF], home_near.at[0:HALF], back_sent.at[5], back_got.at[5], at(t - 2)
    )
    home_b = push(
        sums.at[1, HALF:BLK], home_near.at[HALF:BLK], back_sent.at[7], back_got.at[7], at(t - 2)
    )
    over_back = push(sums.at[1, HALF:BLK], cross_back, back_sent.at[7], back_got.at[8], at(t - 8))
    over_home = push(
        cross_back, home_near.at[HALF:BLK], back_sent.at[8], back_got.at[7], at(t + 6)
    )
    edge_to = at(t - 5 + 4 * core)
    edge_copy = push(dkv.at[edge_slot], edge, back_sent.at[6], back_got.at[6], edge_to)

    def backward(step, carry):
        crossed = jnp.where(
            step < 2, 3 + step, jnp.where(step < 4, step - 1, jnp.where(step == 4, 5, 0))
        )
        slot = jnp.where(core == 0, crossed, 5 - step)
        pieces = BLK // WIDE
        units_of = HEADS * pieces
        done = []
        for turn in range(units_of + 1):
            if turn < units_of:
                h, c = divmod(turn, pieces)
                g = (h + HEADS) // 2
                square[turn % 2] = jnp.dot(
                    kv_all[slot, :, 128 * g : 128 * (g + 1)],
                    gt[h, :, WIDE * c : WIDE * (c + 1)],
                    preferred_element_type=F32,
                )
            if turn == 0:
                continue
            h, c = divmod(turn - 1, pieces)
            cols = slice(WIDE * c, WIDE * (c + 1))
            scale = jnp.exp(m_all[slot, h, 0:1, cols] - l_run[h, 0:1, cols])
            shift = delta[h, 0:1, cols]
            ds_at = BLK * (h % 2) + WIDE * c
            p_at = BLK * ((h + HEADS) % 2) + WIDE * c
            for r in range(0, BLK, STRIP):
                down = slice(r, r + STRIP)
                p = probs[slot, h, down, cols].astype(F32) * scale
                ds = p * (square[(turn - 1) % 2, down, :] - shift)
                work[h // 2, down, ds_at : ds_at + WIDE] = ds.astype(BF16)
                work[(h + HEADS) // 2, down, p_at : p_at + WIDE] = p.astype(BF16)
            done.append(h)
            if turn < 2:
                continue
            for h in done[-2:] if turn == units_of else done[-2:-1]:
                here = slice(HS * h, HS * (h + 1))
                dq_t[here, :] += jnp.dot(
                    slots[slot, here, :],
                    work[h // 2, :, BLK * (h % 2) : BLK * (h % 2 + 1)],
                    preferred_element_type=F32,
                )
                for g in ((), (0,), (3,), (1,), (2, 4))[h]:
                    dkv[slot, :, 128 * g : 128 * (g + 1)] = (
                        jnp.dot(work[g, :, 0:BLK], rows[g, 0:BLK], preferred_element_type=F32)
                        + jnp.dot(work[g, :, BLK:], rows[g, BLK:], preferred_element_type=F32)
                    ).astype(BF16)

        @pl.when(step == 0)
        def _():
            to_far.start()

        @pl.when(step == 1)
        def _():
            to_far.wait_recv()
            for part, copy in ((slice(0, HALF), chain), (slice(HALF, BLK), back_first)):
                both = dkv[4, part].astype(F32) + from_mate[0, part].astype(F32)
                sums[0, part] = both.astype(BF16)
                copy.start()

        @pl.when(step == 2)
        def _():
            to_near.start()

        @pl.when(step == 3)
        def _():
            to_near.wait_recv()
            both = dkv[2, HALF:BLK].astype(F32) + from_mate[1, HALF:BLK].astype(F32)
            sums[1, HALF:BLK] = both.astype(BF16)

            @pl.when(y > 0)
            def _():
                home_b.start()

            @pl.when(y == 0)
            def _():
                over_back.start()

            back_first.wait_recv()
            back_second.start()
            attn = jnp.concatenate(
                [out_t[...].T.astype(BF16), jnp.zeros((BLK, WEIGHT_WIDTH - WIDTH), BF16)], axis=1
            )
            for part in range(4):
                piece = slice(WIDTH * part, WIDTH * (part + 1))
                wt[part] = jnp.dot(cot_all[piece, :], attn, preferred_element_type=F32)
            for part in range(4):
                for i in range(4):
                    pair_out[part, i] = weight_rows(part, i, 1 - core).astype(BF16)
            pair_copy.start()

        @pl.when(step == 4)
        def _():
            edge_copy.start()
            chain.wait_recv()
            near = dkv[2, 0:HALF].astype(F32) + from_mate[1, 0:HALF].astype(F32)
            sums[1, 0:HALF] = (near + chain_in[...].astype(F32)).astype(BF16)
            home_a.start()
            pair_copy.wait_recv()
            for part in range(4):
                for i in range(4):
                    both = weight_rows(part, i, core) + pair_in[part, i].astype(F32)
                    z_out[part, i] = both.astype(BF16)
            for copy in z_copies:
                copy.start()

            @pl.when(y == 0)
            def _():
                over_back.wait_recv()
                over_home.start()

        return carry

    lax.fori_loop(0, BACK + 1, backward, 0)

    keep = pltpu.make_async_copy(dkv.at[0], own_ref, local.at[0])
    keep.start()
    dq_ref[...] = (dq_t[...] * HS**-0.5).astype(BF16)
    for copy in z_copies:
        copy.wait_recv()
    z_sum[...] = z_out[z].astype(F32)
    for i in range(3):
        z_sum[...] += z_in[i].astype(F32)
    y_out[...] = z_sum[...].astype(BF16)
    for copy in y_copies:
        copy.start()
    total = z_sum[y]
    for i, copy in enumerate(y_copies):
        copy.wait_recv()
        total = total + y_in[i].astype(F32)
    dw_ref[...] = total[0:40, :WIDTH]
    for copy in [edge_copy, home_a, home_b, back_second, keep]:
        if copy is keep:
            copy.wait()
        else:
            copy.wait_recv()

    copies = [near_k, near_v, relay_first, direct_k, direct_v, chain_k, relay_second]
    copies += [pass_near_k, pass_near_v, pass_far_k, pass_far_v]
    copies += [to_far, to_near, chain, back_first, back_second, home_a, home_b, edge_copy]
    for copy in beside + opposite + copies + z_copies + y_copies + [pair_copy]:
        copy.wait_send()

    @pl.when(y == 3)
    def _():
        over_second.wait_send()

    @pl.when(y == 0)
    def _():
        over_home.wait_send()


def finish_kernel(
    dq, dw, own, near, far, edge, dq_ref, dk_ref, dv_ref, dw_ref, held, far_v, sems
):
    halves = [slice(HALF * half, HALF * (half + 1)) for half in range(2)]
    loads = [
        [
            pltpu.make_async_copy(src.at[part], held.at[i, part], sems.at[3 * half + i])
            for i, src in enumerate((own, edge, near))
        ]
        for half, part in enumerate(halves)
    ]
    loads[1].append(pltpu.make_async_copy(far, far_v, sems.at[6]))
    through = [
        pltpu.make_async_copy(dq, dq_ref, sems.at[7]),
        pltpu.make_async_copy(dw, dw_ref, sems.at[8]),
    ]
    for copy in loads[0] + loads[1] + through:
        copy.start()
    for half, part in enumerate(halves):
        for copy in loads[half]:
            copy.wait()
        total = held[0, part].astype(F32) + held[1, part].astype(F32) + held[2, part].astype(F32)
        if half == 1:
            total = total + far_v[...].astype(F32)
        total_t = total.T.astype(BF16)
        dk_ref[:, part] = total_t[:WIDTH]
        dv_ref[:, part] = total_t[WIDTH:]
    for copy in through:
        copy.wait()


def shards(queries, key_rows, value_rows, cotangent, out_weight, segment_units, left_segments):
    tm_count = lax.axis_size("tm")
    head_count = lax.axis_size("head")
    anywhere = pl.BlockSpec(memory_space=pl.ANY)
    vmem = pl.BlockSpec(memory_space=pltpu.VMEM)
    dma = pltpu.SemaphoreType.DMA
    out_t = jax.ShapeDtypeStruct((WIDTH, BLK), BF16)
    both = 2 * WIDTH
    blocks = BACK + 1
    block = jax.ShapeDtypeStruct((BLK, both), BF16)
    pieces = pl.pallas_call(
        functools.partial(kernel, tm_count, head_count),
        out_shape=(
            out_t,
            jax.ShapeDtypeStruct((40, WIDTH), F32),
            block,
            block,
            jax.ShapeDtypeStruct((HALF, both), BF16),
            block,
        ),
        in_specs=[vmem] * 2 + [anywhere] * 5,
        out_specs=(vmem, vmem, anywhere, anywhere, anywhere, anywhere),
        scratch_shapes=[
            pltpu.VMEM((blocks, both, BLK), BF16),
            pltpu.VMEM((WIDTH, BLK), BF16),
            pltpu.VMEM((WIDTH, BLK), BF16),
            pltpu.VMEM((blocks, BLK, both), BF16),
            pltpu.VMEM((blocks, HEADS, BLK, BLK), BF16),
            pltpu.VMEM((head_count * WIDTH, BLK), BF16),
            pltpu.VMEM((WIDTH, head_count * WIDTH), BF16),
            pltpu.VMEM((WIDTH, BLK), BF16),
            pltpu.VMEM((HEADS, 256, BLK), BF16),
            pltpu.VMEM((HEADS, 128, BLK), BF16),
            pltpu.VMEM((HEADS, 2 * BLK, 128), BF16),
            pltpu.VMEM((2, BLK, WIDE), F32),
            pltpu.VMEM((HEADS, BLK, 2 * BLK), BF16),
            pltpu.VMEM((WIDTH, BLK), F32),
            pltpu.VMEM((WIDTH, BLK), F32),
            pltpu.VMEM((blocks, HEADS, 8, BLK), F32),
            pltpu.VMEM((HEADS, 8, BLK), F32),
            pltpu.VMEM((HEADS, 8, BLK), F32),
            pltpu.VMEM((HEADS, 8, BLK), F32),
            pltpu.VMEM((blocks, BLK, both), BF16),
            pltpu.VMEM((2, BLK, both), BF16),
            pltpu.VMEM((2, BLK, both), BF16),
            pltpu.VMEM((HALF, both), BF16),
            pltpu.VMEM((HALF, both), BF16),
            pltpu.VMEM((HALF, both), BF16),
            pltpu.VMEM((4, WIDTH, WEIGHT_WIDTH), F32),
            pltpu.VMEM((3, 4, 48, WEIGHT_WIDTH), BF16),
            pltpu.VMEM((4, 48, WEIGHT_WIDTH), F32),
            pltpu.VMEM((4, 4, 48, WEIGHT_WIDTH), BF16),
            pltpu.VMEM((4, 4, 48, WEIGHT_WIDTH), BF16),
            pltpu.VMEM((4, 4, 48, WEIGHT_WIDTH), BF16),
            pltpu.VMEM((4, 48, WEIGHT_WIDTH), BF16),
            pltpu.VMEM((3, 48, WEIGHT_WIDTH), BF16),
            dma((5,)),
            dma((12,)),
            dma((blocks,)),
            dma((blocks,)),
            dma((2,)),
            dma((4,)),
            dma((4,)),
            dma((9,)),
            dma((9,)),
            dma((3,)),
            dma((3,)),
            dma((1,)),
            dma((1,)),
            dma((3,)),
            dma((3,)),
        ],
        compiler_params=pltpu.CompilerParams(
            collective_id=0, has_side_effects=True, vmem_limit_bytes=60 << 20
        ),
    )(
        segment_units.reshape(1, -1),
        left_segments.reshape(1, -1),
        queries.T,
        key_rows.T,
        value_rows.T,
        cotangent.T,
        out_weight,
    )
    query_t, key_t, value_t, weight_t = pl.pallas_call(
        finish_kernel,
        out_shape=(out_t, out_t, out_t, jax.ShapeDtypeStruct((40, WIDTH), F32)),
        in_specs=[anywhere] * 6,
        out_specs=(vmem, vmem, vmem, vmem),
        scratch_shapes=[
            pltpu.VMEM((3, BLK, both), BF16),
            pltpu.VMEM((HALF, both), BF16),
            dma((9,)),
        ],
        compiler_params=pltpu.CompilerParams(vmem_limit_bytes=60 << 20),
    )(*pieces)
    return (query_t.T, key_t.T, value_t.T, weight_t.T)


def solution(mesh):
    placed = (
        P("tm", "head"),
        P("tm", "head"),
        P("tm", "head"),
        P("tm", "head"),
        P("head", None),
        P(),
        P(),
    )
    return jax.shard_map(
        shards,
        mesh=mesh,
        in_specs=placed,
        out_specs=(P("tm", "head"), P("tm", "head"), P("tm", "head"), P("head", "tm")),
        check_vma=False,
    )
```

```python
import functools

import jax
import jax.numpy as jnp
from jax import lax
from jax.experimental import pallas as pl
from jax.experimental.pallas import tpu as pltpu
from jax.sharding import PartitionSpec as P

HS = 64
UNIT = 16
BLK = 512
HEADS = 5
WIDTH = HEADS * HS
BACK = 5
HALF = BLK // 2
WEIGHT_WIDTH = 384
STRIP = 128
WIDE = 512
HIDDEN = -2e30
LOWEST = -1e30
F32 = jnp.float32
BF16 = jnp.bfloat16
MESH = pl.DeviceIdType.MESH


def kernel(
    tm_count,
    head_count,
    units_ref,
    left_ref,
    q_hbm,
    k_hbm,
    v_hbm,
    cot_hbm,
    w_hbm,
    dq_ref,
    dw_ref,
    own_ref,
    home_near,
    home_far,
    edge,
    slots,
    relay,
    cross,
    kv_all,
    probs,
    cot_all,
    w_ref,
    q_ref,
    rhs,
    gt,
    rows,
    square,
    work,
    out_t,
    dq_t,
    m_all,
    m_run,
    l_run,
    delta,
    dkv,
    from_mate,
    sums,
    chain_in,
    relay_back,
    cross_back,
    wt,
    z_in,
    z_sum,
    pair_out,
    pair_in,
    y_out,
    y_in,
    local,
    sent,
    got_k,
    got_v,
    got_relay,
    side_sent,
    side_got,
    back_sent,
    back_got,
    z_sent,
    z_got,
    pair_sent,
    pair_got,
    y_sent,
    y_got,
):
    t = lax.axis_index("tm")
    x = lax.axis_index("head")
    core = t % 2
    z = t // 8
    y = (t // 2) % 4
    low = t % 8

    def at(place):
        return {"tm": (place + tm_count) % tm_count}

    def chip(z_place, y_place):
        return (((z_place + 4) % 4) * 4 + y_place % 4) * 2 + core

    mate = at(t + 1 - 2 * core)
    before, after = chip(z, y + 3), chip(z, y + 1)
    inner = jnp.where((y == 1) | (y == 2), 1, 0)
    relay_to = chip(z + jnp.where(y >= 2, 1, 0), y + 3)
    relay_from = chip(z - inner, y + 1)
    back_to = chip(z - jnp.where(y < 2, 1, 0), y + 1)
    back_from = chip(z + inner, y + 3)

    greeted = [at(t - 2), at(t + 2), at(relay_from), at(back_from)]
    greeted += [{"head": (x + head_count + by) % head_count} for by in (-1, 1)]
    greeted += [at(t - 8 * i) for i in range(1, 4)]
    greeted += [at(8 * z + (low + 8 - i) % 8) for i in range(1, 8)]
    barrier = pltpu.get_barrier_semaphore()
    for target in greeted:
        pl.semaphore_signal(barrier, inc=1, device_id=target, device_id_type=MESH)
    edge_source = at(t + 5 * (2 * core - 1))
    pl.semaphore_signal(barrier, inc=1, device_id=edge_source, device_id_type=MESH)

    loads = [
        pltpu.make_async_copy(k_hbm, slots.at[0, 0:WIDTH], local.at[0]),
        pltpu.make_async_copy(v_hbm, slots.at[0, WIDTH : 2 * WIDTH], local.at[1]),
        pltpu.make_async_copy(q_hbm, q_ref, local.at[2]),
        pltpu.make_async_copy(
            cot_hbm, cot_all.at[pl.ds(pl.multiple_of(WIDTH * x, 64), WIDTH)], local.at[3]
        ),
        pltpu.make_async_copy(w_hbm, w_ref, local.at[4]),
    ]
    for load in loads:
        load.start()
    pl.semaphore_wait(barrier, len(greeted) + 1)

    def push(src, dst, send_sem, recv_sem, target):
        return pltpu.make_async_remote_copy(
            src_ref=src,
            dst_ref=dst,
            send_sem=send_sem,
            recv_sem=recv_sem,
            device_id=target,
            device_id_type=MESH,
        )

    def keys(src, slot, number, target):
        return push(src, slots.at[slot, 0:WIDTH], sent.at[number], got_k.at[slot], target)

    def values(src, slot, number, target):
        return push(
            src, slots.at[slot, WIDTH : 2 * WIDTH], sent.at[number], got_v.at[slot], target
        )

    def key_part(slot):
        return slots.at[slot, 0:WIDTH]

    def value_part(slot):
        return slots.at[slot, WIDTH : 2 * WIDTH]

    near_k = keys(k_hbm, 2, 0, at(t + 2))
    near_v = values(v_hbm, 2, 1, at(t + 2))
    over_first = push(v_hbm, cross, sent.at[1], got_relay.at[1], at(t + 8))
    over_second = values(cross, 2, 11, at(t - 6))
    relay_first = push(v_hbm, relay, sent.at[2], got_relay.at[0], at(relay_to))
    near_k.start()
    relay_first.start()
    def cot_rows(place, first, count):
        start = WIDTH * (place % head_count) + first
        return cot_all.at[pl.ds(pl.multiple_of(start, 32), count)]

    def aside(src, rows_there, number, by):
        place = {"head": (x + head_count + by) % head_count}
        return push(src, rows_there, side_sent.at[number], side_got.at[number], place)

    own_cot = cot_rows(x, 0, WIDTH)
    upper = cot_rows(x + head_count - 1, 0, WIDTH // 2)
    lower = cot_rows(x + 1, WIDTH // 2, WIDTH // 2)
    beside = [aside(cot_hbm, own_cot, 0, 1), aside(cot_hbm, own_cot, 1, -1)]
    opposite = [aside(upper, upper, 2, 1), aside(lower, lower, 3, -1)]
    for copy in beside:
        copy.start()

    @pl.when(y < 3)
    def _():
        near_v.start()

    @pl.when(y == 3)
    def _():
        over_first.start()

    direct_slot = 1 + 4 * core
    direct_to = at(t + 1 + 4 * core)
    direct_k = keys(k_hbm, direct_slot, 3, direct_to)
    direct_v = values(v_hbm, direct_slot, 4, direct_to)

    @pl.when(core == 0)
    def _():
        direct_k.start()
        direct_v.start()

    chain_k = keys(key_part(2), 4, 5, at(t + 2))
    relay_second = values(relay, 4, 6, at(before))
    pass_near = 3 - 2 * core
    pass_far = 5 - 2 * core
    pass_near_k = keys(key_part(2), pass_near, 7, mate)
    pass_near_v = values(value_part(2), pass_near, 8, mate)
    pass_far_k = keys(key_part(4), pass_far, 9, mate)
    pass_far_v = values(value_part(4), pass_far, 10, mate)

    segments = units_ref.shape[1]
    units = jnp.broadcast_to(units_ref[...].astype(F32), (8, segments)).astype(BF16)
    lefts = jnp.broadcast_to(left_ref[...].astype(F32), (8, segments)).astype(BF16)
    down = lax.broadcasted_iota(jnp.int32, (segments, 128), 0)
    over = lax.broadcasted_iota(jnp.int32, (segments, 128), 1)
    until = jnp.where(down <= over, 1.0, 0.0).astype(BF16)
    ahead = jnp.where(down < over, 1.0, 0.0).astype(BF16)
    same = jnp.where(down == over, 1.0, 0.0).astype(BF16)
    end_row = jnp.dot(units, until, preferred_element_type=F32)[0:1, :] * UNIT
    start_row = jnp.dot(units, ahead, preferred_element_type=F32)[0:1, :] * UNIT
    columns = (((0,), (1,)), ((), ()))
    end_col = lax.dot_general(until, units, columns, preferred_element_type=F32)[:, 0:1] * UNIT
    left_col = lax.dot_general(same, lefts, columns, preferred_element_type=F32)[:, 0:1]
    frame_row = (t * BLK + lax.broadcasted_iota(jnp.int32, (1, BLK), 1)).astype(F32)
    own_seg = jnp.sum(jnp.where(end_col <= frame_row, 1.0, 0.0), axis=0, keepdims=True)
    seg_down = lax.broadcasted_iota(jnp.int32, (128, BLK), 0).astype(F32)
    reach = jnp.sum(jnp.where(seg_down == own_seg, left_col, 0.0), axis=0, keepdims=True)
    lowest = jnp.maximum(own_seg - reach, 0.0)
    bias = jnp.where((seg_down >= lowest) & (seg_down <= own_seg), 0.0, HIDDEN).astype(BF16)

    blank = jnp.zeros((HS, BLK), BF16)
    lane = lax.broadcasted_iota(jnp.int32, (BLK, 128), 1)

    def spread(j, upright, transposed):
        g, half = divmod(j, 2)
        both = [transposed, blank] if half == 0 else [blank, transposed]
        if j < HEADS:
            rhs[j] = jnp.concatenate(both + [bias], axis=0)
        else:
            gt[j - HEADS] = jnp.concatenate(both, axis=0)
        zeros = jnp.zeros((BLK, HS), BF16)
        pair = [upright, zeros] if half == 0 else [zeros, upright]
        rows[g, BLK * half : BLK * (half + 1), :] = jnp.concatenate(pair, axis=1)

    loads[2].wait()
    queries_t = (q_ref[...].astype(F32) * HS**-0.5).astype(BF16)
    for j in range(HEADS):
        mine = queries_t[HS * j : HS * (j + 1), :]
        spread(j, mine.T, mine)
    m_run[...] = jnp.full(m_run.shape, LOWEST, F32)
    l_run[...] = jnp.zeros(l_run.shape, F32)
    out_t[...] = jnp.zeros(out_t.shape, F32)
    dq_t[...] = jnp.zeros(dq_t.shape, F32)
    loads[0].wait()
    loads[1].wait()

    def wait_slot(slot):
        keys(k_hbm, slot, 0, mate).wait_recv()
        values(v_hbm, slot, 1, mate).wait_recv()

    def near_event():
        relay_first.wait_recv()
        relay_second.start()

        near_k.wait_recv()
        chain_k.start()
        pass_near_k.start()
        for arrived, onward in zip(beside, opposite):
            arrived.wait_recv()
            onward.start()
        near_v.wait_recv()
        pass_near_v.start()

    def forward(step, carry):
        @pl.when((step == 1) & (core == 1))
        def _():
            direct_k.start()
            direct_v.start()

        @pl.when((step == 1) & (y == 3))
        def _():
            over_first.wait_recv()
            over_second.start()

        swapped = jnp.where(step == 0, 0, jnp.where(step < 3, 3 - step, 8 - step))
        slot = jnp.where(core == 0, swapped, step)

        @pl.when(step == 1 + core)
        def _():
            near_event()

        @pl.when((step == 2 - core) | (step == 3) | (step == 5))
        def _():
            wait_slot(slot)

        @pl.when(step == 4)
        def _():
            loads[3].wait()
            loads[4].wait()
            for copy in opposite:
                copy.wait_recv()
            grad_t = jnp.dot(w_ref[...], cot_all[...], preferred_element_type=F32).astype(BF16)
            for j in range(HEADS):
                mine = grad_t[HS * j : HS * (j + 1), :]
                spread(j + HEADS, mine.T, mine)

        @pl.when(step == 4)
        def _():
            keys(k_hbm, 4, 0, mate).wait_recv()
            pass_far_k.start()
            values(v_hbm, 4, 1, mate).wait_recv()
            pass_far_v.start()

        def upright(g):
            group = slice(128 * g, 128 * (g + 1))
            kv_all[slot, :, group] = slots[slot, group, :].T

        first = ((t + tm_count - slot) % tm_count) * BLK
        frames = (first + lax.broadcasted_iota(jnp.int32, (BLK, 128), 0)).astype(F32)
        hot = jnp.where((frames >= start_row) & (frames < end_row), 1.0, 0.0).astype(BF16)
        upright(0)
        pieces = BLK // WIDE
        units_of = HEADS * pieces
        top = None
        late = []
        for turn in range(units_of + 1):
            last = top
            if turn < units_of:
                h, c = divmod(turn, pieces)
                cols = slice(WIDE * c, WIDE * (c + 1))
                g = h // 2
                lhs = jnp.concatenate([kv_all[slot, :, 128 * g : 128 * (g + 1)], hot], axis=1)
                scores = jnp.dot(lhs, rhs[h, :, cols], preferred_element_type=F32)
                square[turn % 2] = scores
                top = jnp.max(scores.reshape(BLK // 8, 8, WIDE), axis=0)
                if turn < HEADS - 1:
                    upright(turn + 1)
            if turn == 0:
                continue
            h, c = divmod(turn - 1, pieces)
            cols = slice(WIDE * c, WIDE * (c + 1))
            m_old = m_run[h, 0:1, cols]
            m_new = jnp.maximum(m_old, jnp.max(last, axis=0, keepdims=True))
            factor = jnp.exp(m_old - m_new)
            m_run[h, 0:1, cols] = m_new
            m_all[slot, h, 0:1, cols] = m_new
            total = l_run[h, :, cols] * factor
            for r in range(0, BLK, STRIP):
                p = jnp.exp(square[(turn - 1) % 2, r : r + STRIP, :] - m_new)
                total = total + jnp.sum(p.reshape(STRIP // 8, 8, WIDE), axis=0)
                probs[slot, h, r : r + STRIP, cols] = p.astype(BF16)
            l_run[h, :, cols] = total
            late.append((h, cols, factor))
            if turn < 2:
                continue
            for h, cols, factor in late[-2:] if turn == units_of else late[-2:-1]:
                here = slice(HS * h, HS * (h + 1))
                out_t[here, cols] = out_t[here, cols] * factor + jnp.dot(
                    slots[slot, WIDTH + HS * h : WIDTH + HS * (h + 1), :],
                    probs[slot, h, :, cols],
                    preferred_element_type=F32,
                )
        return carry

    lax.fori_loop(0, BACK + 1, forward, 0)

    for h in range(HEADS):
        here = slice(HS * h, HS * (h + 1))
        total = jnp.sum(l_run[h], axis=0, keepdims=True)
        out = out_t[here, :] / total
        out_t[here, :] = out
        side = HS * ((h + HEADS) % 2)
        own_grad = gt[h, side : side + HS, :].astype(F32)
        delta[h, 0:1, :] = jnp.sum(out * own_grad, axis=0, keepdims=True)
        l_run[h, 0:1, :] = m_run[h, 0:1, :] + jnp.log(total)

    z_copies = [
        push(
            wt.at[(z + i) % 4], z_in.at[i - 1], z_sent.at[i - 1], z_got.at[i - 1], at(t + 8 * i)
        )
        for i in range(1, 4)
    ]
    attn = jnp.concatenate(
        [out_t[...].T.astype(BF16), jnp.zeros((BLK, WEIGHT_WIDTH - WIDTH), BF16)], axis=1
    )
    for part in range(4):
        piece = slice(WIDTH * part, WIDTH * (part + 1))
        wt[part] = jnp.dot(cot_all[piece, :], attn, preferred_element_type=F32).astype(BF16)
    for copy in z_copies:
        copy.start()
    pair_copy = push(pair_out, pair_in, pair_sent.at[0], pair_got.at[0], mate)
    y_copies = [
        push(
            y_out.at[(y + i) % 4],
            y_in.at[i - 1],
            y_sent.at[i - 1],
            y_got.at[i - 1],
            at(chip(z, y + i)),
        )
        for i in range(1, 4)
    ]

    def weight_rows(ring_place, parity):
        first = pl.multiple_of(80 * ring_place + 40 * parity, 8)
        block = z_sum[pl.ds(first, 40), :]
        return jnp.concatenate([block, jnp.zeros((8, WEIGHT_WIDTH), F32)], axis=0)

    far_slot, near_slot, edge_slot = 3 + 2 * core, 1 + 2 * core, 5 - 4 * core
    to_far = push(dkv.at[far_slot], from_mate.at[0], back_sent.at[0], back_got.at[0], mate)
    to_near = push(dkv.at[near_slot], from_mate.at[1], back_sent.at[1], back_got.at[1], mate)
    chain = push(sums.at[0, 0:HALF], chain_in, back_sent.at[2], back_got.at[2], at(t - 2))
    back_first = push(
        sums.at[0, HALF:BLK], relay_back, back_sent.at[3], back_got.at[3], at(back_to)
    )
    back_second = push(relay_back, home_far, back_sent.at[4], back_got.at[4], at(after))
    home_a = push(
        sums.at[1, 0:HALF], home_near.at[0:HALF], back_sent.at[5], back_got.at[5], at(t - 2)
    )
    home_b = push(
        sums.at[1, HALF:BLK], home_near.at[HALF:BLK], back_sent.at[7], back_got.at[7], at(t - 2)
    )
    over_back = push(sums.at[1, HALF:BLK], cross_back, back_sent.at[7], back_got.at[8], at(t - 8))
    over_home = push(
        cross_back, home_near.at[HALF:BLK], back_sent.at[8], back_got.at[7], at(t + 6)
    )
    edge_to = at(t - 5 + 4 * core)
    edge_copy = push(dkv.at[edge_slot], edge, back_sent.at[6], back_got.at[6], edge_to)

    def backward(step, carry):
        crossed = jnp.where(
            step < 2, 3 + step, jnp.where(step < 4, step - 1, jnp.where(step == 4, 5, 0))
        )
        slot = jnp.where(core == 0, crossed, 5 - step)
        pieces = BLK // WIDE
        units_of = HEADS * pieces
        done = []
        for turn in range(units_of + 1):
            if turn < units_of:
                h, c = divmod(turn, pieces)
                g = (h + HEADS) // 2
                square[turn % 2] = jnp.dot(
                    kv_all[slot, :, 128 * g : 128 * (g + 1)],
                    gt[h, :, WIDE * c : WIDE * (c + 1)],
                    preferred_element_type=F32,
                )
            if turn == 0:
                continue
            h, c = divmod(turn - 1, pieces)
            cols = slice(WIDE * c, WIDE * (c + 1))
            scale = jnp.exp(m_all[slot, h, 0:1, cols] - l_run[h, 0:1, cols])
            shift = delta[h, 0:1, cols]
            ds_at = BLK * (h % 2) + WIDE * c
            p_at = BLK * ((h + HEADS) % 2) + WIDE * c
            for r in range(0, BLK, STRIP):
                down = slice(r, r + STRIP)
                p = probs[slot, h, down, cols].astype(F32) * scale
                ds = p * (square[(turn - 1) % 2, down, :] - shift)
                work[h // 2, down, ds_at : ds_at + WIDE] = ds.astype(BF16)
                work[(h + HEADS) // 2, down, p_at : p_at + WIDE] = p.astype(BF16)
            done.append(h)
            if turn < 2:
                continue
            for h in done[-2:] if turn == units_of else done[-2:-1]:
                here = slice(HS * h, HS * (h + 1))
                dq_t[here, :] += jnp.dot(
                    slots[slot, here, :],
                    work[h // 2, :, BLK * (h % 2) : BLK * (h % 2 + 1)],
                    preferred_element_type=F32,
                )
                for g in ((), (0,), (3,), (1,), (2, 4))[h]:
                    dkv[slot, :, 128 * g : 128 * (g + 1)] = (
                        jnp.dot(work[g, :, 0:BLK], rows[g, 0:BLK], preferred_element_type=F32)
                        + jnp.dot(work[g, :, BLK:], rows[g, BLK:], preferred_element_type=F32)
                    ).astype(BF16)

        @pl.when(step == 0)
        def _():
            to_far.start()

        @pl.when(step == 1)
        def _():
            to_far.wait_recv()
            for part, copy in ((slice(0, HALF), chain), (slice(HALF, BLK), back_first)):
                both = dkv[4, part].astype(F32) + from_mate[0, part].astype(F32)
                sums[0, part] = both.astype(BF16)
                copy.start()

        @pl.when(step == 2)
        def _():
            to_near.start()
            for copy in z_copies:
                copy.wait_recv()
            z_sum[...] = wt[z].astype(F32)
            for i in range(3):
                z_sum[...] += z_in[i].astype(F32)
            for i in range(4):
                pair_out[i] = weight_rows(i, 1 - core).astype(BF16)
            pair_copy.start()

        @pl.when(step == 3)
        def _():
            to_near.wait_recv()
            both = dkv[2, HALF:BLK].astype(F32) + from_mate[1, HALF:BLK].astype(F32)
            sums[1, HALF:BLK] = both.astype(BF16)

            @pl.when(y > 0)
            def _():
                home_b.start()

            @pl.when(y == 0)
            def _():
                over_back.start()

            back_first.wait_recv()
            back_second.start()
            pair_copy.wait_recv()
            for i in range(4):
                y_out[i] = (weight_rows(i, core) + pair_in[i].astype(F32)).astype(BF16)
            for copy in y_copies:
                copy.start()

        @pl.when(step == 4)
        def _():
            edge_copy.start()
            chain.wait_recv()
            near = dkv[2, 0:HALF].astype(F32) + from_mate[1, 0:HALF].astype(F32)
            sums[1, 0:HALF] = (near + chain_in[...].astype(F32)).astype(BF16)
            home_a.start()

            @pl.when(y == 0)
            def _():
                over_back.wait_recv()
                over_home.start()

        return carry

    lax.fori_loop(0, BACK + 1, backward, 0)

    keep = pltpu.make_async_copy(dkv.at[0], own_ref, local.at[0])
    keep.start()
    dq_ref[...] = (dq_t[...] * HS**-0.5).astype(BF16)
    total = weight_rows(y, core) + pair_in[y].astype(F32)
    for i, copy in enumerate(y_copies):
        copy.wait_recv()
        total = total + y_in[i].astype(F32)
    dw_ref[...] = total[0:40, :WIDTH]
    for copy in [edge_copy, home_a, home_b, back_second, keep]:
        if copy is keep:
            copy.wait()
        else:
            copy.wait_recv()

    copies = [near_k, near_v, relay_first, direct_k, direct_v, chain_k, relay_second]
    copies += [pass_near_k, pass_near_v, pass_far_k, pass_far_v]
    copies += [to_far, to_near, chain, back_first, back_second, home_a, home_b, edge_copy]
    for copy in beside + opposite + copies + z_copies + y_copies + [pair_copy]:
        copy.wait_send()

    @pl.when(y == 3)
    def _():
        over_second.wait_send()

    @pl.when(y == 0)
    def _():
        over_home.wait_send()


def finish_kernel(
    dq, dw, own, near, far, edge, dq_ref, dk_ref, dv_ref, dw_ref, held, far_v, sems
):
    halves = [slice(HALF * half, HALF * (half + 1)) for half in range(2)]
    loads = [
        [
            pltpu.make_async_copy(src.at[part], held.at[i, part], sems.at[3 * half + i])
            for i, src in enumerate((own, edge, near))
        ]
        for half, part in enumerate(halves)
    ]
    loads[1].append(pltpu.make_async_copy(far, far_v, sems.at[6]))
    through = [
        pltpu.make_async_copy(dq, dq_ref, sems.at[7]),
        pltpu.make_async_copy(dw, dw_ref, sems.at[8]),
    ]
    for copy in loads[0] + loads[1] + through:
        copy.start()
    for half, part in enumerate(halves):
        for copy in loads[half]:
            copy.wait()
        total = held[0, part].astype(F32) + held[1, part].astype(F32) + held[2, part].astype(F32)
        if half == 1:
            total = total + far_v[...].astype(F32)
        total_t = total.T.astype(BF16)
        dk_ref[:, part] = total_t[:WIDTH]
        dv_ref[:, part] = total_t[WIDTH:]
    for copy in through:
        copy.wait()


def shards(queries, key_rows, value_rows, cotangent, out_weight, segment_units, left_segments):
    tm_count = lax.axis_size("tm")
    head_count = lax.axis_size("head")
    anywhere = pl.BlockSpec(memory_space=pl.ANY)
    vmem = pl.BlockSpec(memory_space=pltpu.VMEM)
    dma = pltpu.SemaphoreType.DMA
    out_t = jax.ShapeDtypeStruct((WIDTH, BLK), BF16)
    both = 2 * WIDTH
    blocks = BACK + 1
    block = jax.ShapeDtypeStruct((BLK, both), BF16)
    pieces = pl.pallas_call(
        functools.partial(kernel, tm_count, head_count),
        out_shape=(
            out_t,
            jax.ShapeDtypeStruct((40, WIDTH), F32),
            block,
            block,
            jax.ShapeDtypeStruct((HALF, both), BF16),
            block,
        ),
        in_specs=[vmem] * 2 + [anywhere] * 5,
        out_specs=(vmem, vmem, anywhere, anywhere, anywhere, anywhere),
        scratch_shapes=[
            pltpu.VMEM((blocks, both, BLK), BF16),
            pltpu.VMEM((WIDTH, BLK), BF16),
            pltpu.VMEM((WIDTH, BLK), BF16),
            pltpu.VMEM((blocks, BLK, both), BF16),
            pltpu.VMEM((blocks, HEADS, BLK, BLK), BF16),
            pltpu.VMEM((head_count * WIDTH, BLK), BF16),
            pltpu.VMEM((WIDTH, head_count * WIDTH), BF16),
            pltpu.VMEM((WIDTH, BLK), BF16),
            pltpu.VMEM((HEADS, 256, BLK), BF16),
            pltpu.VMEM((HEADS, 128, BLK), BF16),
            pltpu.VMEM((HEADS, 2 * BLK, 128), BF16),
            pltpu.VMEM((2, BLK, WIDE), F32),
            pltpu.VMEM((HEADS, BLK, 2 * BLK), BF16),
            pltpu.VMEM((WIDTH, BLK), F32),
            pltpu.VMEM((WIDTH, BLK), F32),
            pltpu.VMEM((blocks, HEADS, 8, BLK), F32),
            pltpu.VMEM((HEADS, 8, BLK), F32),
            pltpu.VMEM((HEADS, 8, BLK), F32),
            pltpu.VMEM((HEADS, 8, BLK), F32),
            pltpu.VMEM((blocks, BLK, both), BF16),
            pltpu.VMEM((2, BLK, both), BF16),
            pltpu.VMEM((2, BLK, both), BF16),
            pltpu.VMEM((HALF, both), BF16),
            pltpu.VMEM((HALF, both), BF16),
            pltpu.VMEM((HALF, both), BF16),
            pltpu.VMEM((4, WIDTH, WEIGHT_WIDTH), BF16),
            pltpu.VMEM((3, WIDTH, WEIGHT_WIDTH), BF16),
            pltpu.VMEM((WIDTH, WEIGHT_WIDTH), F32),
            pltpu.VMEM((4, 48, WEIGHT_WIDTH), BF16),
            pltpu.VMEM((4, 48, WEIGHT_WIDTH), BF16),
            pltpu.VMEM((4, 48, WEIGHT_WIDTH), BF16),
            pltpu.VMEM((3, 48, WEIGHT_WIDTH), BF16),
            dma((5,)),
            dma((12,)),
            dma((blocks,)),
            dma((blocks,)),
            dma((2,)),
            dma((4,)),
            dma((4,)),
            dma((9,)),
            dma((9,)),
            dma((3,)),
            dma((3,)),
            dma((1,)),
            dma((1,)),
            dma((3,)),
            dma((3,)),
        ],
        compiler_params=pltpu.CompilerParams(
            collective_id=0, has_side_effects=True, vmem_limit_bytes=60 << 20
        ),
    )(
        segment_units.reshape(1, -1),
        left_segments.reshape(1, -1),
        queries.T,
        key_rows.T,
        value_rows.T,
        cotangent.T,
        out_weight,
    )
    query_t, key_t, value_t, weight_t = pl.pallas_call(
        finish_kernel,
        out_shape=(out_t, out_t, out_t, jax.ShapeDtypeStruct((40, WIDTH), F32)),
        in_specs=[anywhere] * 6,
        out_specs=(vmem, vmem, vmem, vmem),
        scratch_shapes=[
            pltpu.VMEM((3, BLK, both), BF16),
            pltpu.VMEM((HALF, both), BF16),
            dma((9,)),
        ],
        compiler_params=pltpu.CompilerParams(vmem_limit_bytes=60 << 20),
    )(*pieces)
    return (query_t.T, key_t.T, value_t.T, weight_t.T)


def solution(mesh):
    placed = (
        P("tm", "head"),
        P("tm", "head"),
        P("tm", "head"),
        P("tm", "head"),
        P("head", None),
        P(),
        P(),
    )
    return jax.shard_map(
        shards,
        mesh=mesh,
        in_specs=placed,
        out_specs=(P("tm", "head"), P("tm", "head"), P("tm", "head"), P("head", "tm")),
        check_vma=False,
    )
```
